32 devices in a mesh: groups: 2 (over x), port: 16 (over z, y, core).
Axes of the slice: x: 2, y: 2, z: 4, core: 2. Of those that a mesh axis runs over, the one named last changes fastest.
Arguments:
- measured: bfloat16 [4, 2, 4096, 4096], P('groups', None, 'port'), parts along dimension 0, may hold values from -6 to 6
- out_factor: bfloat16 [4096, 1024], P('port', 'groups'), parts along dimension 1, may hold values from -0.25 to 0.25
- in_factor: bfloat16 [1024, 4096], P('groups', 'port'), parts along dimension 0, may hold values from -6 to 6
- pole_rates: float32 [1024], P('groups'), parts along dimension 0, may hold values from 0.1 to 10
- freq_index: int32 [4], P('groups'), parts along dimension 0, may hold values from 0 to 1023
- quad_codes: int32 [4], P('groups'), parts along dimension 0, may hold values from 1 to 4
Outputs:
- grad_out: float32 [4096, 1024], P('port', 'groups'), parts along dimension 1
- grad_in_t: float32 [4096, 1024], P('port', 'groups'), parts along dimension 1
The draws below stay inside these ranges and needn't reach their ends.
There are 2 independent parts, one for each index of `groups`. The reference program is written for one: setup_inputs(seed, part) draws one part's arguments, and reference() takes and returns one part's arrays. A program takes and returns all parts, laid end to end along the dimension named above; each array names one. Nothing has to cross between parts.
All inputs are finite; a program needn't handle non-finite values.
Results may differ from the reference program's by a relative error of at most 0.002.
Values may be sent and summed in bfloat16 or wider, within the bound.
No kernel may reach another device: no remote copies, remote signals or barrier semaphores. Data moves between devices by JAX's collectives and lax.ppermute only.
A program may use at most 64 MiB of HBM per device.

```python
import math
import jax
import jax.numpy as jnp

P_OUT = 4096
P_IN = 4096
NP = 512
F = 2
GRID = 1024


def block_scale(stream_key, dims, shards, least, top_value):
    loudness, own = 1.0, jax.random.fold_in(stream_key, 6)
    for axis_at, blocks in shards:
        steps = jnp.exp(jax.random.uniform(jax.random.fold_in(own, axis_at), (blocks,), jnp.float32, least / len(shards), top_value / len(shards)))
        loudness = loudness * jnp.repeat(steps, dims[axis_at] // blocks).reshape([-1 if axis == axis_at else 1 for axis in range(len(dims))])
    return loudness


def bell_draw(own_key, shape, spread, limit, cuts=(), dtype=jnp.bfloat16):
    entries = spread * jax.random.normal(own_key, shape, jnp.float32)
    if cuts:
        entries = entries * block_scale(own_key, shape, cuts, -0.22, 0.18)
    return jnp.clip(entries, -limit, limit).astype(dtype)


def setup_inputs(seed: int = 0, part: int = 0) -> dict:
    arg_keys = jax.random.split(jax.random.key(seed), 7)
    own_keys = jax.random.split(jax.random.fold_in(arg_keys[6], part), 7)
    return {
        "measured": bell_draw(own_keys[0], (F, 2, P_OUT, P_IN), 1.0, 6.0, ((2, 16),)),
        "out_factor": bell_draw(own_keys[1], (P_OUT, NP), NP ** -0.5, 0.25, ((0, 16),)),
        "in_factor": bell_draw(own_keys[2], (NP, P_IN), 1.0, 6.0, ((1, 16),)),
        "pole_rates": jnp.clip(jnp.exp(jax.random.uniform(own_keys[3], (NP,), jnp.float32, math.log(0.1), math.log(10.0))), 0.1, 10.0),
        "freq_index": jax.random.randint(own_keys[4], (F,), 0, GRID).astype(jnp.int32),
        "quad_codes": jax.random.randint(own_keys[5], (F,), 1, 5).astype(jnp.int32),
    }


low_freq = 0.1
log_span = math.log(100.0)


def pole_terms(freq_index, pole_rates):
    omega = low_freq * jnp.exp(log_span * freq_index.astype(jnp.float32) / (GRID - 1))
    denominator = pole_rates[None, :] * pole_rates[None, :] + omega[:, None] * omega[:, None]
    real_side = pole_rates[None, :] / denominator
    imag_side = -omega[:, None] / denominator
    return jnp.stack([real_side, imag_side], axis=1)


def reference(measured, out_factor, in_factor, pole_rates, freq_index, quad_codes):
    coefficients = pole_terms(freq_index, pole_rates)
    weights = quad_codes.astype(jnp.float32) * 0.25
    grad_out = jnp.zeros((P_OUT, NP), jnp.float32)
    grad_in_t = jnp.zeros((P_IN, NP), jnp.float32)
    for freq_slot in range(F):
        for comp_slot in range(2):
            column_scale = coefficients[freq_slot, comp_slot]
            scaled = (out_factor.astype(jnp.float32) * column_scale[None, :]).astype(jnp.bfloat16)
            model = jnp.dot(scaled, in_factor, preferred_element_type=jnp.float32)
            residual = (model - measured[freq_slot, comp_slot].astype(jnp.float32)).astype(jnp.bfloat16)
            factor = weights[freq_slot] * column_scale
            grad_out = grad_out + factor[None, :] * jnp.dot(residual, in_factor.T, preferred_element_type=jnp.float32)
            grad_in_t = grad_in_t + factor[None, :] * jnp.dot(residual.T, out_factor, preferred_element_type=jnp.float32)
    return grad_out * (P_IN ** -0.5), grad_in_t * (P_OUT ** -0.5)
```

```python
import math

import jax
import jax.numpy as jnp
from jax import lax
from jax.experimental import pallas as pl
from jax.experimental.pallas import tpu as pltpu
from jax.sharding import PartitionSpec as P

GRID = 1024


low_freq = 0.1
log_span = math.log(100.0)
least_code = 1e-36


def pole_terms(freq_index, pole_rates):
    omega = low_freq * jnp.exp(log_span * freq_index.astype(jnp.float32) / (GRID - 1))
    denominator = pole_rates[None, :] * pole_rates[None, :] + omega[:, None] * omega[:, None]
    real_side = pole_rates[None, :] / denominator
    imag_side = -omega[:, None] / denominator
    return jnp.stack([real_side, imag_side], axis=1)


def encode(value):
    return ((value * jnp.abs(value)) * (value * value)).astype(jnp.bfloat16)


def decode(code):
    code = code.astype(jnp.float32)
    inverse_root = lax.rsqrt(jnp.maximum(jnp.abs(code), least_code))
    return (code * inverse_root) * (inverse_root * lax.rsqrt(inverse_root))


def block_at(rank, step, slabs, flip):
    slab = lax.rem(lax.div(rank, 4) + (slabs - step), slabs)
    return 4 * slab + (lax.rem(rank, 4) ^ flip)


def slab_kernel(
    rank_ref,
    measured_0,
    measured_1,
    measured_2,
    measured_3,
    factor_0,
    factor_1,
    factor_2,
    factor_3,
    scaled_ref,
    turned_ref,
    pole_weight_ref,
    row_weight_ref,
    update_in_ref,
    keep_ref,
    send_ref,
    update_ref,
    factor_scr,
    partial_scr,
):
    del rank_ref
    step = pl.program_id(0)
    width = factor_0.shape[1]

    @pl.when(step == 0)
    def _():
        for at, factor in enumerate((factor_0, factor_1, factor_2, factor_3)):
            factor_scr[:, at * width : (at + 1) * width] = factor[...]

    factor = factor_scr[...]
    model = jnp.dot(scaled_ref[0], factor, preferred_element_type=jnp.float32)
    measured = jnp.concatenate(
        [ref[0, 0].astype(jnp.float32) for ref in (measured_0, measured_1, measured_2, measured_3)],
        axis=1,
    )
    residual = (model - measured).astype(jnp.bfloat16)
    update = lax.dot_general(
        residual, factor, (((1,), (1,)), ((), ())), preferred_element_type=jnp.float32
    )
    update = row_weight_ref[0] * update

    @pl.when(step == 0)
    def _():
        update_ref[...] = update_in_ref[...] + update

    @pl.when(step > 0)
    def _():
        update_ref[...] += update

    partial = jnp.dot(turned_ref[...], residual, preferred_element_type=jnp.float32)
    weight = pole_weight_ref[0]
    weight = jnp.concatenate([weight] * (partial.shape[1] // weight.shape[1]), axis=1)
    partial = weight * partial

    @pl.when(step == 0)
    def _():
        partial_scr[...] = partial

    @pl.when(step > 0)
    def _():
        partial_scr[...] += partial

    @pl.when(step == pl.num_programs(0) - 1)
    def _():
        keep_ref[0] = partial_scr[:, :width]
        keep_ref[1] = partial_scr[:, 2 * width : 3 * width]
        send_ref[0] = encode(partial_scr[:, width : 2 * width])
        send_ref[1] = encode(partial_scr[:, 3 * width :])


def slab_by_kernel(rank, step, slabs, measured, factors, scaled, turned, pole_weight, row_weight, update):
    freq_count, comps, rows, _ = measured.shape
    poles, width = factors[0].shape
    terms = freq_count * comps
    slab = len(factors) * width
    whole = lambda *shape: pl.BlockSpec(shape, lambda t, rank_ref: (0,) * len(shape))

    def measured_spec(flip):
        return pl.BlockSpec(
            (1, 1, rows, width),
            lambda t, rank_ref: (
                lax.div(t, comps),
                lax.rem(t, comps),
                0,
                block_at(rank_ref[0], step, slabs, flip),
            ),
        )

    flops = 2 * 3 * terms * rows * poles * slab
    moved = 2 * terms * rows * (slab + poles) + 12 * poles * slab
    return pl.pallas_call(
        slab_kernel,
        grid_spec=pltpu.PrefetchScalarGridSpec(
            num_scalar_prefetch=1,
            grid=(terms,),
            in_specs=[measured_spec(at) for at in range(4)]
            + [whole(poles, width)] * 4
            + [
                pl.BlockSpec((1, rows, poles), lambda t, rank_ref: (t, 0, 0)),
                whole(poles, rows),
                pl.BlockSpec((1, poles, pole_weight.shape[2]), lambda t, rank_ref: (t, 0, 0)),
                pl.BlockSpec((1, 1, poles), lambda t, rank_ref: (t, 0, 0)),
                whole(rows, poles),
            ],
            out_specs=[
                whole(2, poles, width),
                whole(2, poles, width),
                whole(rows, poles),
            ],
            scratch_shapes=[
                pltpu.VMEM((poles, slab), jnp.bfloat16),
                pltpu.VMEM((poles, slab), jnp.float32),
            ],
        ),
        out_shape=[
            jax.ShapeDtypeStruct((2, poles, width), jnp.float32),
            jax.ShapeDtypeStruct((2, poles, width), jnp.bfloat16),
            jax.ShapeDtypeStruct((rows, poles), jnp.float32),
        ],
        compiler_params=pltpu.CompilerParams(
            dimension_semantics=("arbitrary",), vmem_limit_bytes=32 * 1024 * 1024
        ),
        cost_estimate=pl.CostEstimate(flops=flops, bytes_accessed=moved, transcendentals=0),
        name="slab",
    )(rank, *([measured] * 4), *factors, scaled, turned, pole_weight, row_weight, update)


def slab_by_ops(rank, step, slabs, measured, factors, scaled, turned, pole_weight, row_weight, update):
    freq_count, comps, rows, _ = measured.shape
    width = factors[0].shape[1]
    terms = freq_count * comps
    factor = jnp.concatenate(factors, axis=1)
    seen = jnp.concatenate(
        [
            lax.dynamic_slice_in_dim(
                measured, block_at(rank[0], step, slabs, flip) * width, width, 3
            )
            for flip in range(4)
        ],
        axis=3,
    ).reshape(terms, rows, 4 * width)
    model = jnp.einsum("tik,kj->tij", scaled, factor, preferred_element_type=jnp.float32)
    residual = (model - seen.astype(jnp.float32)).astype(jnp.bfloat16)
    term_update = jnp.einsum("tij,kj->tik", residual, factor, preferred_element_type=jnp.float32)
    update = update + jnp.sum(row_weight * term_update, axis=0)
    partial = jnp.einsum("ki,tij->tkj", turned, residual, preferred_element_type=jnp.float32)
    partial = jnp.sum(pole_weight[:, :, :1] * partial, axis=0)
    parts = [partial[:, at * width : (at + 1) * width] for at in range(4)]
    return jnp.stack([parts[0], parts[2]]), encode(jnp.stack([parts[1], parts[3]])), update


def on_device(measured, out_factor, in_factor, pole_rates, freq_index, quad_codes):
    freq_count, comps, rows, total_in = measured.shape
    poles, width = in_factor.shape
    terms = freq_count * comps
    ranks = lax.axis_size("port")
    rank = lax.axis_index("port").astype(jnp.int32).reshape(1)
    slabs = ranks // 4
    total_out = rows * ranks

    def to_core(block):
        return lax.ppermute(block, "port", [(i, i ^ 1) for i in range(ranks)])

    def to_side(block):
        return lax.ppermute(block, "port", [(i, i ^ 2) for i in range(ranks)])

    def to_next(block):
        return lax.ppermute(block, "port", [(i, (i + 4) % ranks) for i in range(ranks)])

    coefficients = pole_terms(freq_index, pole_rates)
    weights = quad_codes.astype(jnp.float32) * 0.25
    weighted = (weights[:, None, None] * coefficients).reshape(terms, poles)
    scaled = (
        out_factor.astype(jnp.float32)[None, None, :, :] * coefficients[:, :, None, :]
    ).astype(jnp.bfloat16)
    scaled = scaled.reshape(terms, rows, poles)
    turned = out_factor.T
    lanes = min(width, 128)
    pole_weight = jnp.broadcast_to(weighted[:, :, None], (terms, poles, lanes))
    row_weight = weighted[:, None, :]

    one_slab = slab_by_kernel if width % 128 == 0 else slab_by_ops
    own = [in_factor]
    for _ in range(1, slabs):
        own.append(to_next(own[-1]))

    def compute(step, update):
        near = own[step]
        far = to_side(near)
        factors = [near, to_core(near), far, to_core(far)]
        return one_slab(
            rank, step, slabs, measured, factors, scaled, turned, pole_weight, row_weight, update
        )

    update = jnp.zeros((rows, poles), jnp.float32)
    own_keep, own_send, update = compute(0, update)
    own_sum = own_keep + decode(to_core(own_send))
    own_far = to_side(encode(own_sum[1]))

    arriving = None
    for step in range(1, slabs):
        keep, send, update = compute(step, update)
        total = keep + decode(to_core(send))
        if step == 1:
            arriving = to_next(encode(total))
            continue
        if step == 2:
            total = total + decode(arriving)
            total = total[0] + decode(to_side(encode(total[1])))
        else:
            total = total[0] + decode(to_side(encode(total[1]))) + decode(arriving)
        arriving = to_next(encode(total))

    grad_in = own_sum[0] + decode(own_far) + decode(arriving)
    grad_out = update * (1.0 / math.sqrt(total_in))
    grad_in_t = (grad_in * (1.0 / math.sqrt(total_out))).T
    return (grad_out, grad_in_t)


def solution(mesh):
    in_specs = (
        P("groups", None, "port", None),
        P("port", "groups"),
        P("groups", "port"),
        P("groups"),
        P("groups"),
        P("groups"),
    )
    out_specs = (P("port", "groups"), P("port", "groups"))
    return jax.shard_map(
        on_device, mesh=mesh, in_specs=in_specs, out_specs=out_specs, check_vma=False
    )
```

```python
import functools
import math

import jax
import jax.numpy as jnp
from jax import lax
from jax.experimental import pallas as pl
from jax.experimental.pallas import tpu as pltpu
from jax.sharding import PartitionSpec as P

GRID = 1024


low_freq = 0.1
log_span = math.log(100.0)
least_code = 1e-36


def pole_terms(freq_index, pole_rates):
    omega = low_freq * jnp.exp(log_span * freq_index.astype(jnp.float32) / (GRID - 1))
    denominator = pole_rates[None, :] * pole_rates[None, :] + omega[:, None] * omega[:, None]
    real_side = pole_rates[None, :] / denominator
    imag_side = -omega[:, None] / denominator
    return jnp.stack([real_side, imag_side], axis=1)


def encode(value):
    return ((value * jnp.abs(value)) * (value * value)).astype(jnp.bfloat16)


def decode(code):
    code = code.astype(jnp.float32)
    inverse_root = lax.rsqrt(jnp.maximum(jnp.abs(code), least_code))
    return (code * inverse_root) * (inverse_root * lax.rsqrt(inverse_root))


def block_at(rank, step, slabs, flip):
    slab = lax.rem(lax.div(rank, 4) + (slabs - step), slabs)
    return 4 * slab + (lax.rem(rank, 4) ^ flip)


def prepare_kernel(
    freq_ref, quad_ref, rates_ref, factor_ref, scaled_ref, turned_ref, pole_weight_ref, row_weight_ref
):
    rates = rates_ref[...]
    factor = factor_ref[...].astype(jnp.float32)
    turned_ref[...] = factor.T.astype(jnp.bfloat16)
    rows = factor.shape[0]
    lanes = pole_weight_ref.shape[2]
    for freq_slot in range(freq_ref.shape[0]):
        index = jnp.full(rates.shape, freq_ref[freq_slot], jnp.int32).astype(jnp.float32)
        weight = jnp.full(rates.shape, quad_ref[freq_slot], jnp.int32).astype(jnp.float32) * 0.25
        omega = low_freq * jnp.exp(log_span * index / (GRID - 1))
        denominator = rates * rates + omega * omega
        for comp_slot, coefficient in enumerate((rates / denominator, -omega / denominator)):
            term = 2 * freq_slot + comp_slot
            scaled_ref[pl.ds(term * rows, rows), :] = (factor * coefficient).astype(jnp.bfloat16)
            weighted = weight * coefficient
            row_weight_ref[term] = weighted
            pole_weight_ref[term] = jnp.broadcast_to(weighted, (lanes, weighted.shape[1])).T


def prepare_by_kernel(freq_index, quad_codes, pole_rates, out_factor, lanes):
    rows, poles = out_factor.shape
    terms = 2 * freq_index.shape[0]
    vmem = pl.BlockSpec(memory_space=pltpu.VMEM)
    smem = pl.BlockSpec(memory_space=pltpu.SMEM)
    return pl.pallas_call(
        prepare_kernel,
        in_specs=[smem, smem, vmem, vmem],
        out_specs=[vmem] * 4,
        out_shape=[
            jax.ShapeDtypeStruct((terms * rows, poles), jnp.bfloat16),
            jax.ShapeDtypeStruct((poles, rows), jnp.bfloat16),
            jax.ShapeDtypeStruct((terms, poles, lanes), jnp.float32),
            jax.ShapeDtypeStruct((terms, 1, poles), jnp.float32),
        ],
        cost_estimate=pl.CostEstimate(
            flops=4 * terms * rows * poles, bytes_accessed=4 * terms * rows * poles, transcendentals=0
        ),
        name="prepare",
    )(freq_index, quad_codes, pole_rates[None, :], out_factor)


def slab_kernel(
    step,
    slabs,
    rank_ref,
    measured_ref,
    factor_0,
    factor_1,
    factor_2,
    factor_3,
    scaled_ref,
    turned_ref,
    pole_weight_ref,
    row_weight_ref,
    update_in_ref,
    keep_ref,
    send_ref,
    update_ref,
    seen_scr,
    factor_scr,
    residual_scr,
    arrived,
):
    factors = (factor_0, factor_1, factor_2, factor_3)
    width = factor_0.shape[1]
    rows = turned_ref.shape[1]
    terms = row_weight_ref.shape[0]
    copies = []
    for flip in range(4):
        first = pl.multiple_of(block_at(rank_ref[0], step, slabs, flip) * width, width)
        copy = pltpu.make_async_copy(
            measured_ref.at[:, :, :, pl.ds(first, width)], seen_scr.at[flip], arrived.at[flip]
        )
        copy.start()
        copies.append(copy)

    for flip, factor in enumerate(factors):
        block = factor[...]
        factor_scr[:, flip * width : (flip + 1) * width] = block
        model = jnp.dot(scaled_ref[...], block, preferred_element_type=jnp.float32)
        copies[flip].wait()
        seen = seen_scr[flip].reshape(terms * rows, width).astype(jnp.float32)
        residual_scr[:, flip * width : (flip + 1) * width] = (model - seen).astype(jnp.bfloat16)
        partial = None
        for term in range(terms):
            part = jnp.dot(
                turned_ref[...],
                residual_scr[term * rows : (term + 1) * rows, flip * width : (flip + 1) * width],
                preferred_element_type=jnp.float32,
            )
            weight = pole_weight_ref[term]
            weight = jnp.concatenate([weight] * (width // weight.shape[1]), axis=1)
            partial = weight * part if partial is None else partial + weight * part
        if flip % 2 == 0:
            keep_ref[flip // 2] = partial
        else:
            send_ref[flip // 2] = encode(partial)

    update = lax.dot_general(
        residual_scr[...],
        factor_scr[...],
        (((1,), (1,)), ((), ())),
        preferred_element_type=jnp.float32,
    )
    total = update_in_ref[...]
    for term in range(terms):
        total = total + row_weight_ref[term] * update[term * rows : (term + 1) * rows]
    update_ref[...] = total


def slab_by_kernel(
    rank, step, slabs, measured, factors, scaled, turned, pole_weight, row_weight, update
):
    freq_count, comps, rows, _ = measured.shape
    poles, width = factors[0].shape
    terms = freq_count * comps
    slab = len(factors) * width
    flops = 2 * 3 * terms * rows * poles * slab
    moved = 2 * terms * rows * (slab + poles) + 12 * poles * slab
    vmem = pl.BlockSpec(memory_space=pltpu.VMEM)
    return pl.pallas_call(
        functools.partial(slab_kernel, step, slabs),
        in_specs=[pl.BlockSpec(memory_space=pltpu.SMEM), pl.BlockSpec(memory_space=pltpu.HBM)]
        + [vmem] * 9,
        out_specs=[vmem] * 3,
        out_shape=[
            jax.ShapeDtypeStruct((2, poles, width), jnp.float32),
            jax.ShapeDtypeStruct((2, poles, width), jnp.bfloat16),
            jax.ShapeDtypeStruct((rows, poles), jnp.float32),
        ],
        scratch_shapes=[
            pltpu.VMEM((4, freq_count, comps, rows, width), jnp.bfloat16),
            pltpu.VMEM((poles, slab), jnp.bfloat16),
            pltpu.VMEM((terms * rows, slab), jnp.bfloat16),
            pltpu.SemaphoreType.DMA((4,)),
        ],
        compiler_params=pltpu.CompilerParams(vmem_limit_bytes=46 * 1024 * 1024),
        cost_estimate=pl.CostEstimate(flops=flops, bytes_accessed=moved, transcendentals=0),
        name="slab",
    )(
        rank,
        measured,
        *factors,
        scaled,
        turned,
        pole_weight,
        row_weight,
        update,
    )


def slab_by_ops(rank, step, slabs, measured, factors, scaled, turned, pole_weight, row_weight, update):
    freq_count, comps, rows, _ = measured.shape
    width = factors[0].shape[1]
    terms = freq_count * comps
    factor = jnp.concatenate(factors, axis=1)
    seen = jnp.concatenate(
        [
            lax.dynamic_slice_in_dim(
                measured, block_at(rank[0], step, slabs, flip) * width, width, 3
            )
            for flip in range(4)
        ],
        axis=3,
    ).reshape(terms, rows, 4 * width)
    model = jnp.einsum(
        "tik,kj->tij", scaled.reshape(terms, rows, -1), factor, preferred_element_type=jnp.float32)
    residual = (model - seen.astype(jnp.float32)).astype(jnp.bfloat16)
    term_update = jnp.einsum("tij,kj->tik", residual, factor, preferred_element_type=jnp.float32)
    update = update + jnp.sum(row_weight * term_update, axis=0)
    partial = jnp.einsum("ki,tij->tkj", turned, residual, preferred_element_type=jnp.float32)
    partial = jnp.sum(pole_weight[:, :, :1] * partial, axis=0)
    parts = [partial[:, at * width : (at + 1) * width] for at in range(4)]
    return jnp.stack([parts[0], parts[2]]), encode(jnp.stack([parts[1], parts[3]])), update


def prepare_by_ops(freq_index, quad_codes, pole_rates, out_factor, lanes):
    rows, poles = out_factor.shape
    coefficients = pole_terms(freq_index, pole_rates)
    weights = quad_codes.astype(jnp.float32) * 0.25
    weighted = (weights[:, None, None] * coefficients).reshape(-1, poles)
    scaled = (
        out_factor.astype(jnp.float32)[None, None, :, :] * coefficients[:, :, None, :]
    ).astype(jnp.bfloat16)
    pole_weight = jnp.broadcast_to(weighted[:, :, None], (weighted.shape[0], poles, lanes))
    return scaled.reshape(-1, poles), out_factor.T, pole_weight, weighted[:, None, :]


def after(value, *earlier):
    return lax.optimization_barrier((value, *earlier))[0]


def on_device(measured, out_factor, in_factor, pole_rates, freq_index, quad_codes):
    rows, total_in = measured.shape[2:]
    poles, width = in_factor.shape
    ranks = lax.axis_size("port")
    rank = lax.axis_index("port").astype(jnp.int32).reshape(1)
    slabs = ranks // 4
    total_out = rows * ranks
    tiled = width % 128 == 0 and rows % 128 == 0
    one_slab = slab_by_kernel if tiled else slab_by_ops
    prepare = prepare_by_kernel if tiled else prepare_by_ops

    def to_core(block):
        return lax.ppermute(block, "port", [(i, i ^ 1) for i in range(ranks)])

    def to_side(block):
        return lax.ppermute(block, "port", [(i, i ^ 2) for i in range(ranks)])

    def to_next(block):
        return lax.ppermute(block, "port", [(i, (i + 4) % ranks) for i in range(ranks)])

    constants = prepare(freq_index, quad_codes, pole_rates, out_factor, min(width, 128))

    nears, fars = [in_factor], [to_side(in_factor)]
    update = jnp.zeros((rows, poles), jnp.float32)
    keeps, sends = [], []
    for step in range(slabs):
        mates = [to_core(nears[step]), to_core(fars[step])]
        factors = [nears[step], mates[0], fars[step], mates[1]]
        if step + 1 < slabs:
            nears.append(to_next(nears[step]))
            last = step + 2 == slabs and slabs > 2
            fars.append(to_next(fars[step]) if last else to_side(nears[step + 1]))
            update = after(update, nears[step + 1])
        keep, send, update = one_slab(
            rank, step, slabs, measured, factors, *constants, update
        )
        keeps.append(keep)
        sends.append(send)

    arriving = None
    for step in list(range(1, slabs)) + [0]:
        total = keeps[step] + decode(to_core(sends[step]))
        total = total[0] + decode(to_side(encode(total[1])))
        if arriving is not None:
            total = total + decode(arriving)
        if step > 0:
            arriving = to_next(encode(total))

    grad_out = update * (1.0 / math.sqrt(total_in))
    grad_in_t = (total * (1.0 / math.sqrt(total_out))).T
    return (grad_out, grad_in_t)


def solution(mesh):
    in_specs = (
        P("groups", None, "port", None),
        P("port", "groups"),
        P("groups", "port"),
        P("groups"),
        P("groups"),
        P("groups"),
    )
    out_specs = (P("port", "groups"), P("port", "groups"))
    return jax.shard_map(
        on_device, mesh=mesh, in_specs=in_specs, out_specs=out_specs, check_vma=False
    )
```

```python
import functools
import math

import jax
import jax.numpy as jnp
from jax import lax
from jax.experimental import pallas as pl
from jax.experimental.pallas import tpu as pltpu
from jax.sharding import PartitionSpec as P

GRID = 1024


low_freq = 0.1
log_span = math.log(100.0)
least_code = 1e-36


def pole_terms(freq_index, pole_rates):
    omega = low_freq * jnp.exp(log_span * freq_index.astype(jnp.float32) / (GRID - 1))
    denominator = pole_rates[None, :] * pole_rates[None, :] + omega[:, None] * omega[:, None]
    real_side = pole_rates[None, :] / denominator
    imag_side = -omega[:, None] / denominator
    return jnp.stack([real_side, imag_side], axis=1)


def encode(value):
    return ((value * jnp.abs(value)) * (value * value)).astype(jnp.bfloat16)


def decode(code):
    code = code.astype(jnp.float32)
    inverse_root = lax.rsqrt(jnp.maximum(jnp.abs(code), least_code))
    return (code * inverse_root) * (inverse_root * lax.rsqrt(inverse_root))


def block_at(rank, step, slabs, flip):
    slab = lax.rem(lax.div(rank, 4) + (slabs - step), slabs)
    return 4 * slab + (lax.rem(rank, 4) ^ flip)


def prepare_kernel(
    freq_ref, quad_ref, rates_ref, factor_ref, scaled_ref, turned_ref, pole_weight_ref, row_weight_ref
):
    rates = rates_ref[...]
    factor = factor_ref[...].astype(jnp.float32)
    turned_ref[...] = factor.T.astype(jnp.bfloat16)
    rows = factor.shape[0]
    lanes = pole_weight_ref.shape[2]
    for freq_slot in range(freq_ref.shape[0]):
        index = jnp.full(rates.shape, freq_ref[freq_slot], jnp.int32).astype(jnp.float32)
        weight = jnp.full(rates.shape, quad_ref[freq_slot], jnp.int32).astype(jnp.float32) * 0.25
        omega = low_freq * jnp.exp(log_span * index / (GRID - 1))
        denominator = rates * rates + omega * omega
        for comp_slot, coefficient in enumerate((rates / denominator, -omega / denominator)):
            term = 2 * freq_slot + comp_slot
            scaled_ref[pl.ds(term * rows, rows), :] = (factor * coefficient).astype(jnp.bfloat16)
            weighted = weight * coefficient
            row_weight_ref[term] = weighted
            pole_weight_ref[term] = jnp.broadcast_to(weighted, (lanes, weighted.shape[1])).T


def prepare_by_kernel(freq_index, quad_codes, pole_rates, out_factor, lanes):
    rows, poles = out_factor.shape
    terms = 2 * freq_index.shape[0]
    vmem = pl.BlockSpec(memory_space=pltpu.VMEM)
    smem = pl.BlockSpec(memory_space=pltpu.SMEM)
    return pl.pallas_call(
        prepare_kernel,
        in_specs=[smem, smem, vmem, vmem],
        out_specs=[vmem] * 4,
        out_shape=[
            jax.ShapeDtypeStruct((terms * rows, poles), jnp.bfloat16),
            jax.ShapeDtypeStruct((poles, rows), jnp.bfloat16),
            jax.ShapeDtypeStruct((terms, poles, lanes), jnp.float32),
            jax.ShapeDtypeStruct((terms, 1, poles), jnp.float32),
        ],
        cost_estimate=pl.CostEstimate(
            flops=4 * terms * rows * poles, bytes_accessed=4 * terms * rows * poles, transcendentals=0
        ),
        compiler_params=pltpu.CompilerParams(vmem_limit_bytes=16 * 1024 * 1024),
        name="prepare",
    )(freq_index, quad_codes, pole_rates[None, :], out_factor)


def half_kernel(
    step,
    slabs,
    side,
    rank_ref,
    measured_ref,
    factor_0,
    factor_1,
    scaled_ref,
    turned_ref,
    pole_weight_ref,
    row_weight_ref,
    update_in_ref,
    *refs,
):
    keep_ref, send_ref, update_ref, seen_scr, factor_scr, residual_scr, arrived = refs[-7:]
    width = factor_0.shape[1]
    rows = turned_ref.shape[1]
    terms = row_weight_ref.shape[0]
    copies = []
    for core in range(2):
        block = block_at(rank_ref[0], step, slabs, 2 * side + core)
        first = pl.multiple_of(block * width, width)
        copy = pltpu.make_async_copy(
            measured_ref.at[:, :, :, pl.ds(first, width)], seen_scr.at[core], arrived.at[core]
        )
        copy.start()
        copies.append(copy)

    for core, factor_ref in enumerate((factor_0, factor_1)):
        columns = slice(core * width, (core + 1) * width)
        factor = factor_ref[...]
        factor_scr[:, columns] = factor
        model = jnp.dot(scaled_ref[...], factor, preferred_element_type=jnp.float32)
        copies[core].wait()
        seen = seen_scr[core].reshape(terms * rows, width).astype(jnp.float32)
        residual_scr[:, columns] = (model - seen).astype(jnp.bfloat16)
        partial = None
        for term in range(terms):
            part = jnp.dot(
                turned_ref[...],
                residual_scr[term * rows : (term + 1) * rows, columns],
                preferred_element_type=jnp.float32,
            )
            weight = pole_weight_ref[term]
            weight = jnp.concatenate([weight] * (width // weight.shape[1]), axis=1)
            partial = weight * part if partial is None else partial + weight * part
        if core == 0:
            keep_ref[side] = partial
        else:
            send_ref[side] = encode(partial)

    update = lax.dot_general(
        residual_scr[...],
        factor_scr[...],
        (((1,), (1,)), ((), ())),
        preferred_element_type=jnp.float32,
    )
    total = update_in_ref[...]
    for term in range(terms):
        total = total + row_weight_ref[term] * update[term * rows : (term + 1) * rows]
    update_ref[...] = total


def half_by_kernel(rank, step, slabs, side, measured, factors, constants, update, sums):
    scaled, turned, pole_weight, row_weight = constants
    freq_count, comps, rows, _ = measured.shape
    poles, width = factors[0].shape
    terms = freq_count * comps
    half = len(factors) * width
    flops = 2 * 3 * terms * rows * poles * half
    moved = 2 * terms * rows * (half + poles) + 12 * poles * half
    vmem = pl.BlockSpec(memory_space=pltpu.VMEM)
    aliases = {8: 2} if side == 0 else {8: 2, 9: 0, 10: 1}
    keep, send, update = pl.pallas_call(
        functools.partial(half_kernel, step, slabs, side),
        in_specs=[pl.BlockSpec(memory_space=pltpu.SMEM), pl.BlockSpec(memory_space=pl.ANY)]
        + [vmem] * (7 if side == 0 else 9),
        out_specs=[vmem] * 3,
        out_shape=[
            jax.ShapeDtypeStruct((2, poles, width), jnp.float32),
            jax.ShapeDtypeStruct((2, poles, width), jnp.bfloat16),
            jax.ShapeDtypeStruct((rows, poles), jnp.float32),
        ],
        scratch_shapes=[
            pltpu.VMEM((2, freq_count, comps, rows, width), jnp.bfloat16),
            pltpu.VMEM((poles, half), jnp.bfloat16),
            pltpu.VMEM((terms * rows, half), jnp.bfloat16),
            pltpu.SemaphoreType.DMA((2,)),
        ],
        input_output_aliases=aliases,
        compiler_params=pltpu.CompilerParams(vmem_limit_bytes=46 * 1024 * 1024),
        cost_estimate=pl.CostEstimate(flops=50 * flops, bytes_accessed=50 * moved, transcendentals=0),
        name="near" if side == 0 else "far",
    )(rank, measured, *factors, scaled, turned, pole_weight, row_weight, update, *sums)
    return (keep, send), update


def half_by_ops(rank, step, slabs, side, measured, factors, constants, update, sums):
    scaled, turned, pole_weight, row_weight = constants
    freq_count, comps, rows, _ = measured.shape
    width = factors[0].shape[1]
    terms = freq_count * comps
    factor = jnp.concatenate(factors, axis=1)
    seen = jnp.concatenate(
        [
            lax.dynamic_slice_in_dim(
                measured, block_at(rank[0], step, slabs, 2 * side + core) * width, width, 3
            )
            for core in range(2)
        ],
        axis=3,
    ).reshape(terms, rows, 2 * width)
    model = jnp.einsum(
        "tik,kj->tij",
        scaled.reshape(terms, rows, -1),
        factor,
        preferred_element_type=jnp.float32,
    )
    residual = (model - seen.astype(jnp.float32)).astype(jnp.bfloat16)
    term_update = jnp.einsum("tij,kj->tik", residual, factor, preferred_element_type=jnp.float32)
    update = update + jnp.sum(row_weight * term_update, axis=0)
    partial = jnp.einsum("ki,tij->tkj", turned, residual, preferred_element_type=jnp.float32)
    partial = jnp.sum(pole_weight[:, :, :1] * partial, axis=0)
    keep, send = partial[None, :, :width], encode(partial[None, :, width:])
    if side == 1:
        keep, send = jnp.concatenate([sums[0], keep]), jnp.concatenate([sums[1], send])
    return (keep, send), update


def prepare_by_ops(freq_index, quad_codes, pole_rates, out_factor, lanes):
    rows, poles = out_factor.shape
    coefficients = pole_terms(freq_index, pole_rates)
    weights = quad_codes.astype(jnp.float32) * 0.25
    weighted = (weights[:, None, None] * coefficients).reshape(-1, poles)
    scaled = (
        out_factor.astype(jnp.float32)[None, None, :, :] * coefficients[:, :, None, :]
    ).astype(jnp.bfloat16)
    pole_weight = jnp.broadcast_to(weighted[:, :, None], (weighted.shape[0], poles, lanes))
    return scaled.reshape(-1, poles), out_factor.T, pole_weight, weighted[:, None, :]


def after(value, *earlier):
    return lax.optimization_barrier((value, *earlier))[0]


def on_device(measured, out_factor, in_factor, pole_rates, freq_index, quad_codes):
    rows, total_in = measured.shape[2:]
    poles, width = in_factor.shape
    ranks = lax.axis_size("port")
    rank = lax.axis_index("port").astype(jnp.int32).reshape(1)
    slabs = ranks // 4
    total_out = rows * ranks
    tiled = width % 128 == 0 and rows % 128 == 0
    one_half = half_by_kernel if tiled else half_by_ops
    prepare = prepare_by_kernel if tiled else prepare_by_ops

    def to_core(block):
        return lax.ppermute(block, "port", [(i, i ^ 1) for i in range(ranks)])

    def to_side(block):
        return lax.ppermute(block, "port", [(i, i ^ 2) for i in range(ranks)])

    def to_next(block):
        return lax.ppermute(block, "port", [(i, (i + 4) % ranks) for i in range(ranks)])

    near = in_factor
    coming_near = to_next(near)
    coming_far = to_side(near)
    near_pair = [near, to_core(near)]
    constants = prepare(freq_index, quad_codes, pole_rates, out_factor, min(width, 128))
    update = jnp.zeros((rows, poles), jnp.float32)
    sums = [()] * slabs
    totals = [None] * slabs
    codes = [None] * slabs
    arriving = None

    def half(step, side, factors, update):
        return one_half(
            rank, step, slabs, side, measured, factors, constants, update, sums[step]
        )

    def collect(step, update):
        keep, send = sums[step]
        totals[step] = keep + decode(after(to_core(send), update))
        codes[step] = encode(totals[step][1])
        return after(update, codes[step])

    def pass_on(step, update, arriving):
        total = totals[step][0] + decode(after(to_side(codes[step]), update))
        if arriving is not None:
            total = total + decode(arriving)
        code = encode(total)
        return after(update, code), to_next(code)

    sums[0], update = half(0, 0, near_pair, update)
    for step in range(slabs):
        far = after(coming_far, update)
        if step + 1 < slabs:
            near = after(coming_near, update)
            if step + 2 < slabs:
                coming_near = to_next(near)
            if step + 2 == slabs and slabs > 2:
                coming_far = to_next(far)
            else:
                coming_far = to_side(near)
            near_pair = [near, to_core(near)]
            update = after(update, near)
        sums[step], update = half(step, 1, [far, to_core(far)], update)
        if step + 1 < slabs:
            sums[step + 1], update = half(step + 1, 0, near_pair, update)
        if step > 0:
            update = collect(step, update)
        if step > 1:
            update, arriving = pass_on(step - 1, update, arriving)
    if slabs > 1:
        update, arriving = pass_on(slabs - 1, update, arriving)
    update = collect(0, update)
    total = totals[0][0] + decode(to_side(codes[0]))
    if arriving is not None:
        total = total + decode(arriving)

    grad_out = update * (1.0 / math.sqrt(total_in))
    grad_in_t = (total * (1.0 / math.sqrt(total_out))).T
    return (grad_out, grad_in_t)


def solution(mesh):
    in_specs = (
        P("groups", None, "port", None),
        P("port", "groups"),
        P("groups", "port"),
        P("groups"),
        P("groups"),
        P("groups"),
    )
    out_specs = (P("port", "groups"), P("port", "groups"))
    return jax.shard_map(
        on_device, mesh=mesh, in_specs=in_specs, out_specs=out_specs, check_vma=False
    )
```

```python
import functools
import math

import jax
import jax.numpy as jnp
from jax import lax
from jax.experimental import pallas as pl
from jax.experimental.pallas import tpu as pltpu
from jax.sharding import PartitionSpec as P

GRID = 1024


low_freq = 0.1
log_span = math.log(100.0)
least_code = 1e-36


def pole_terms(freq_index, pole_rates):
    omega = low_freq * jnp.exp(log_span * freq_index.astype(jnp.float32) / (GRID - 1))
    denominator = pole_rates[None, :] * pole_rates[None, :] + omega[:, None] * omega[:, None]
    real_side = pole_rates[None, :] / denominator
    imag_side = -omega[:, None] / denominator
    return jnp.stack([real_side, imag_side], axis=1)


def encode(value):
    return ((value * jnp.abs(value)) * (value * value)).astype(jnp.bfloat16)


def decode(code):
    code = code.astype(jnp.float32)
    inverse_root = lax.rsqrt(jnp.maximum(jnp.abs(code), least_code))
    return (code * inverse_root) * (inverse_root * lax.rsqrt(inverse_root))


def block_at(rank, step, slabs, flip):
    slab = lax.rem(lax.div(rank, 4) + (slabs - step), slabs)
    return 4 * slab + (lax.rem(rank, 4) ^ flip)


def prepare_kernel(
    slabs,
    rank_ref,
    freq_ref,
    quad_ref,
    rates_ref,
    factor_ref,
    measured_ref,
    scaled_ref,
    turned_ref,
    pole_weight_ref,
    row_weight_ref,
    *refs,
):
    arrived = refs[-1]
    width = refs[0].shape[-1]
    copies = []
    for at in range(4 * slabs):
        block = block_at(rank_ref[0], at // 4, slabs, at % 4)
        first = pl.multiple_of(block * width, width)
        copy = pltpu.make_async_copy(
            measured_ref.at[:, :, :, pl.ds(first, width)], refs[at // 2].at[at % 2], arrived.at[at]
        )
        copy.start()
        copies.append(copy)
    rates = rates_ref[...]
    factor = factor_ref[...].astype(jnp.float32)
    turned_ref[...] = factor.T.astype(jnp.bfloat16)
    rows = factor.shape[0]
    lanes = pole_weight_ref.shape[2]
    for freq_slot in range(freq_ref.shape[0]):
        index = jnp.full(rates.shape, freq_ref[freq_slot], jnp.int32).astype(jnp.float32)
        weight = jnp.full(rates.shape, quad_ref[freq_slot], jnp.int32).astype(jnp.float32) * 0.25
        omega = low_freq * jnp.exp(log_span * index / (GRID - 1))
        denominator = rates * rates + omega * omega
        for comp_slot, coefficient in enumerate((rates / denominator, -omega / denominator)):
            term = 2 * freq_slot + comp_slot
            scaled_ref[pl.ds(term * rows, rows), :] = (factor * coefficient).astype(jnp.bfloat16)
            weighted = weight * coefficient
            row_weight_ref[term] = weighted
            pole_weight_ref[term] = jnp.broadcast_to(weighted, (lanes, weighted.shape[1])).T
    for copy in copies:
        copy.wait()


def prepare_by_kernel(
    rank, slabs, freq_index, quad_codes, pole_rates, out_factor, measured, width, lanes
):
    rows, poles = out_factor.shape
    terms = 2 * freq_index.shape[0]
    vmem = pl.BlockSpec(memory_space=pltpu.VMEM)
    smem = pl.BlockSpec(memory_space=pltpu.SMEM)
    made = pl.pallas_call(
        functools.partial(prepare_kernel, slabs),
        in_specs=[smem, smem, smem, vmem, vmem, pl.BlockSpec(memory_space=pltpu.HBM)],
        out_specs=[vmem] * (4 + 2 * slabs),
        out_shape=[
            jax.ShapeDtypeStruct((terms * rows, poles), jnp.bfloat16),
            jax.ShapeDtypeStruct((poles, rows), jnp.bfloat16),
            jax.ShapeDtypeStruct((terms, poles, lanes), jnp.float32),
            jax.ShapeDtypeStruct((terms, 1, poles), jnp.float32),
        ]
        + [jax.ShapeDtypeStruct((2, *measured.shape[:3], width), jnp.bfloat16)] * (2 * slabs),
        scratch_shapes=[pltpu.SemaphoreType.DMA((4 * slabs,))],
        compiler_params=pltpu.CompilerParams(vmem_limit_bytes=40 * 1024 * 1024),
        cost_estimate=pl.CostEstimate(
            flops=4 * terms * rows * poles, bytes_accessed=4 * terms * rows * poles, transcendentals=0
        ),
        name="prepare",
    )(rank, freq_index, quad_codes, pole_rates[None, :], out_factor, measured)
    return made[:4], list(made[4:])


def half_kernel(
    factor_0, factor_1, scaled_ref, turned_ref, pole_weight_ref, seen_ref, *refs
):
    keep_ref, send_ref, residual_ref, held_ref = refs[-4:]
    width = factor_0.shape[1]
    rows = turned_ref.shape[1]
    terms = pole_weight_ref.shape[0]
    for core, factor_ref in enumerate((factor_0, factor_1)):
        factor = factor_ref[...]
        held_ref[core] = factor
        model = jnp.dot(scaled_ref[...], factor, preferred_element_type=jnp.float32)
        seen = seen_ref[core].reshape(terms * rows, width).astype(jnp.float32)
        residual = (model - seen).astype(jnp.bfloat16)
        residual_ref[core] = residual.reshape(residual_ref.shape[1:])
        partial = None
        for term in range(terms):
            part = jnp.dot(
                turned_ref[...],
                residual[term * rows : (term + 1) * rows],
                preferred_element_type=jnp.float32,
            )
            weight = pole_weight_ref[term]
            weight = jnp.concatenate([weight] * (width // weight.shape[1]), axis=1)
            partial = weight * part if partial is None else partial + weight * part
        if core == 0:
            keep_ref[...] = partial
        elif len(refs) > 4:
            send_ref[0] = refs[0][...]
            send_ref[1] = encode(partial)
        else:
            send_ref[...] = encode(partial)


def half_by_kernel(factors, constants, seen, near_send):
    scaled, turned, pole_weight, _ = constants
    poles, width = factors[0].shape
    rows = turned.shape[1]
    terms = pole_weight.shape[0]
    half = len(factors) * width
    flops = 2 * 2 * terms * rows * poles * half
    vmem = pl.BlockSpec(memory_space=pltpu.VMEM)
    beside = [] if near_send is None else [near_send]
    return pl.pallas_call(
        half_kernel,
        in_specs=[vmem] * (6 + len(beside)),
        out_specs=[vmem] * 4,
        out_shape=[
            jax.ShapeDtypeStruct((poles, width), jnp.float32),
            jax.ShapeDtypeStruct((2, poles, width) if beside else (poles, width), jnp.bfloat16),
            jax.ShapeDtypeStruct(seen.shape, seen.dtype),
            jax.ShapeDtypeStruct((2, poles, width), jnp.bfloat16),
        ],
        input_output_aliases={5: 2},
        compiler_params=pltpu.CompilerParams(vmem_limit_bytes=24 * 1024 * 1024),
        cost_estimate=pl.CostEstimate(
            flops=50 * flops, bytes_accessed=100 * terms * rows * half, transcendentals=0
        ),
        name="far" if beside else "near",
    )(*factors, scaled, turned, pole_weight, seen, *beside)


def update_kernel(halves, *refs):
    row_weight_ref, total_ref = refs[2 * halves], refs[-1]
    terms = row_weight_ref.shape[0]
    rows, width = refs[0].shape[-2:]
    total = None
    for at in range(halves):
        residual_ref, held_ref = refs[2 * at : 2 * at + 2]
        for core in range(2):
            part = lax.dot_general(
                residual_ref[core].reshape(terms * rows, width),
                held_ref[core],
                (((1,), (1,)), ((), ())),
                preferred_element_type=jnp.float32,
            )
            total = part if total is None else total + part
    update = refs[2 * halves + 1][...] if len(refs) > 2 * halves + 2 else 0.0
    for term in range(terms):
        update = update + row_weight_ref[term] * total[term * rows : (term + 1) * rows]
    total_ref[...] = update


def update_by_kernel(halves, row_weight, update):
    poles, width = halves[0][1].shape[1:]
    rows = halves[0][0].shape[-2]
    terms = row_weight.shape[0]
    flops = 4 * len(halves) * terms * rows * poles * width
    vmem = pl.BlockSpec(memory_space=pltpu.VMEM)
    operands = [array for half in halves for array in half]
    operands += [row_weight] if update is None else [row_weight, update]
    return pl.pallas_call(
        functools.partial(update_kernel, len(halves)),
        in_specs=[vmem] * len(operands),
        out_specs=vmem,
        out_shape=jax.ShapeDtypeStruct((rows, poles), jnp.float32),
        compiler_params=pltpu.CompilerParams(vmem_limit_bytes=24 * 1024 * 1024),
        cost_estimate=pl.CostEstimate(
            flops=50 * flops, bytes_accessed=100 * terms * rows * width, transcendentals=0
        ),
        name="update",
    )(*operands)


def prepare_by_ops(
    rank, slabs, freq_index, quad_codes, pole_rates, out_factor, measured, width, lanes
):
    rows, poles = out_factor.shape
    coefficients = pole_terms(freq_index, pole_rates)
    weights = quad_codes.astype(jnp.float32) * 0.25
    weighted = (weights[:, None, None] * coefficients).reshape(-1, poles)
    scaled = (
        out_factor.astype(jnp.float32)[None, None, :, :] * coefficients[:, :, None, :]
    ).astype(jnp.bfloat16)
    pole_weight = jnp.broadcast_to(weighted[:, :, None], (weighted.shape[0], poles, lanes))
    blocks = [
        lax.dynamic_slice_in_dim(
            measured, block_at(rank[0], at // 4, slabs, at % 4) * width, width, 3
        )
        for at in range(4 * slabs)
    ]
    seen = [jnp.stack(blocks[at : at + 2]) for at in range(0, 4 * slabs, 2)]
    constants = [scaled.reshape(-1, poles), out_factor.T, pole_weight, weighted[:, None, :]]
    return constants, seen


def half_by_ops(factors, constants, seen, near_send):
    scaled, turned, pole_weight, _ = constants
    width = factors[0].shape[1]
    rows = turned.shape[1]
    terms = pole_weight.shape[0]
    partials, residuals = [], []
    for core, factor in enumerate(factors):
        model = jnp.dot(scaled, factor, preferred_element_type=jnp.float32)
        residual = model - seen[core].reshape(terms * rows, width).astype(jnp.float32)
        residual = residual.astype(jnp.bfloat16)
        residuals.append(residual.reshape(seen.shape[1:]))
        partial = jnp.einsum(
            "ki,tij->tkj",
            turned,
            residual.reshape(terms, rows, width),
            preferred_element_type=jnp.float32,
        )
        partials.append(jnp.sum(pole_weight[:, :, :1] * partial, axis=0))
    send = encode(partials[1])
    if near_send is not None:
        send = jnp.stack([near_send, send])
    return partials[0], send, jnp.stack(residuals), jnp.stack(factors)


def update_by_ops(halves, row_weight, update):
    rows, width = halves[0][0].shape[-2:]
    terms = row_weight.shape[0]
    total = sum(
        jnp.einsum(
            "tij,kj->tik",
            residual[core].reshape(terms, rows, width),
            held[core],
            preferred_element_type=jnp.float32,
        )
        for residual, held in halves
        for core in range(2)
    )
    part = jnp.sum(row_weight * total, axis=0)
    return part if update is None else update + part


def after(value, *earlier):
    return lax.optimization_barrier((value, *earlier))[0]


def on_device(measured, out_factor, in_factor, pole_rates, freq_index, quad_codes):
    rows, total_in = measured.shape[2:]
    poles, width = in_factor.shape
    ranks = lax.axis_size("port")
    rank = lax.axis_index("port").astype(jnp.int32).reshape(1)
    slabs = ranks // 4
    total_out = rows * ranks
    tiled = width % 128 == 0 and rows % 128 == 0
    prepare = prepare_by_kernel if tiled else prepare_by_ops
    one_half = half_by_kernel if tiled else half_by_ops
    add_update = update_by_kernel if tiled else update_by_ops

    def to_core(block):
        return lax.ppermute(block, "port", [(i, i ^ 1) for i in range(ranks)])

    def to_side(block):
        return lax.ppermute(block, "port", [(i, i ^ 2) for i in range(ranks)])

    def to_next(block):
        return lax.ppermute(block, "port", [(i, (i + 4) % ranks) for i in range(ranks)])

    near = in_factor
    coming_near = to_next(near)
    coming_far = to_side(near)
    near_pair = [near, to_core(near)]
    constants, seen = prepare(
        rank,
        slabs,
        freq_index,
        quad_codes,
        pole_rates,
        out_factor,
        measured,
        width,
        min(width, 128),
    )
    nears = [None] * slabs
    keeps = [None] * slabs
    sends = [None] * slabs
    codes = [None] * slabs
    from_sides = [None] * slabs
    halves = []

    def near_half(step, pair, token):
        keep, sends[step], *parts = one_half(pair, constants, after(seen[2 * step], token), None)
        halves.append(parts)
        keeps[step] = [keep]
        return parts[0]

    def far_half(step, pair, token):
        keep, sends[step], *parts = one_half(
            pair, constants, after(seen[2 * step + 1], token), sends[step]
        )
        halves.append(parts)
        keeps[step].append(keep)
        return parts[0]

    def collect(step, token):
        received = decode(after(to_core(sends[step]), token))
        nears[step] = keeps[step][0] + received[0]
        codes[step] = encode(keeps[step][1] + received[1])
        return to_side(codes[step])

    def pass_on(step, arriving, token):
        total = nears[step] + decode(after(from_sides[step], token))
        if arriving is not None:
            total = total + decode(after(arriving, token))
        return encode(total)

    arriving = None
    row_weight = constants[3]
    token = near_half(0, near_pair, row_weight)
    for step in range(slabs):
        far = after(coming_far, token)
        if step + 1 < slabs:
            near = after(coming_near, token)
            if step + 2 < slabs:
                coming_near = to_next(near)
            if step + 2 == slabs and slabs > 2:
                coming_far = to_next(far)
            else:
                coming_far = to_side(near)
            near_pair = [near, to_core(near)]
            token = after(token, near)
        token = far_half(step, [far, to_core(far)], token)
        if step + 1 < slabs:
            token = near_half(step + 1, near_pair, token)
        else:
            token = add_update(halves[:2], after(row_weight, token), None)
        if step > 0:
            from_sides[step] = collect(step, token)
            token = after(token, codes[step])
        if step > 1:
            code = pass_on(step - 1, arriving, token)
            arriving = to_next(code)
            token = after(token, code)

    update = token
    if slabs > 1:
        middle = 1 + slabs
        update = add_update(halves[2:middle], row_weight, update)
        code = pass_on(slabs - 1, arriving, update)
        arriving = to_next(code)
        update = after(update, code)
    from_sides[0] = collect(0, update)
    if slabs > 1:
        update = after(update, codes[0])
        update = add_update(halves[middle:], row_weight, update)
    total = nears[0] + decode(after(from_sides[0], update))
    if arriving is not None:
        total = total + decode(after(arriving, update))

    grad_out = update * (1.0 / math.sqrt(total_in))
    grad_in_t = (total * (1.0 / math.sqrt(total_out))).T
    return (grad_out, grad_in_t)


def solution(mesh):
    in_specs = (
        P("groups", None, "port", None),
        P("port", "groups"),
        P("groups", "port"),
        P("groups"),
        P("groups"),
        P("groups"),
    )
    out_specs = (P("port", "groups"), P("port", "groups"))
    return jax.shard_map(
        on_device, mesh=mesh, in_specs=in_specs, out_specs=out_specs, check_vma=False
    )
```

```python
import functools
import math

import jax
import jax.numpy as jnp
from jax import lax
from jax.experimental import pallas as pl
from jax.experimental.pallas import tpu as pltpu
from jax.sharding import PartitionSpec as P

GRID = 1024


low_freq = 0.1
log_span = math.log(100.0)
least_code = 1e-36


def pole_terms(freq_index, pole_rates):
    omega = low_freq * jnp.exp(log_span * freq_index.astype(jnp.float32) / (GRID - 1))
    denominator = pole_rates[None, :] * pole_rates[None, :] + omega[:, None] * omega[:, None]
    real_side = pole_rates[None, :] / denominator
    imag_side = -omega[:, None] / denominator
    return jnp.stack([real_side, imag_side], axis=1)


def encode(value):
    return ((value * jnp.abs(value)) * (value * value)).astype(jnp.bfloat16)


def decode(code):
    code = code.astype(jnp.float32)
    inverse_root = lax.rsqrt(jnp.maximum(jnp.abs(code), least_code))
    return (code * inverse_root) * (inverse_root * lax.rsqrt(inverse_root))


def ring_order(slabs):
    return [0, *range(1, slabs, 2), *reversed(range(2, slabs, 2))]


def block_at(rank, step, slabs, flip):
    slab = lax.div(rank, 4)
    place = jnp.where(lax.rem(slab, 2) == 1, lax.div(slab + 1, 2), slabs - lax.div(slab, 2))
    place = lax.rem(place + (slabs - step), slabs)
    slab = jnp.where(place <= slabs // 2, 2 * place - 1, 2 * (slabs - place))
    slab = jnp.where(place == 0, 0, slab)
    return 4 * slab + (lax.rem(rank, 4) ^ flip)


def start_copies(rank_ref, measured_ref, first_half, slabs, halves, arrived):
    width = halves[0].shape[-1]
    copies = []
    for at, half in enumerate(halves):
        for core in range(2):
            place = 2 * (first_half + at) + core
            block = block_at(rank_ref[0], place // 4, slabs, place % 4)
            columns = pl.ds(pl.multiple_of(block * width, width), width)
            copy = pltpu.make_async_copy(
                measured_ref.at[:, :, :, columns], half.at[core], arrived.at[2 * at + core]
            )
            copy.start()
            copies.append(copy)
    return copies


def copy_kernel(first_half, slabs, rank_ref, measured_ref, after_ref, *refs):
    del after_ref
    for copy in start_copies(rank_ref, measured_ref, first_half, slabs, refs[:-1], refs[-1]):
        copy.wait()


def copy_by_kernel(rank, slabs, measured, width, first_half, token):
    halves = 2 * slabs - first_half
    vmem = pl.BlockSpec(memory_space=pltpu.VMEM)
    anywhere = pl.BlockSpec(memory_space=pl.ANY)
    shape = jax.ShapeDtypeStruct((2, *measured.shape[:3], width), jnp.bfloat16)
    return pl.pallas_call(
        functools.partial(copy_kernel, first_half, slabs),
        in_specs=[pl.BlockSpec(memory_space=pltpu.SMEM), anywhere, anywhere],
        out_specs=[vmem] * halves,
        out_shape=[shape] * halves,
        scratch_shapes=[pltpu.SemaphoreType.DMA((2 * halves,))],
        compiler_params=pltpu.CompilerParams(vmem_limit_bytes=40 * 1024 * 1024),
        cost_estimate=pl.CostEstimate(
            flops=0, bytes_accessed=100 * halves * measured.size // slabs, transcendentals=0
        ),
        name="copy_measured",
    )(rank, measured, token)


def prepare_kernel(
    slabs,
    rank_ref,
    freq_ref,
    quad_ref,
    rates_ref,
    factor_ref,
    measured_ref,
    scaled_ref,
    turned_ref,
    pole_weight_ref,
    row_weight_ref,
    *refs,
):
    copies = start_copies(rank_ref, measured_ref, 0, slabs, refs[:-1], refs[-1])
    rates = rates_ref[...]
    factor = factor_ref[...].astype(jnp.float32)
    turned_ref[...] = factor.T.astype(jnp.bfloat16)
    rows = factor.shape[0]
    lanes = pole_weight_ref.shape[2]
    for freq_slot in range(freq_ref.shape[0]):
        index = jnp.full(rates.shape, freq_ref[freq_slot], jnp.int32).astype(jnp.float32)
        weight = jnp.full(rates.shape, quad_ref[freq_slot], jnp.int32).astype(jnp.float32) * 0.25
        omega = low_freq * jnp.exp(log_span * index / (GRID - 1))
        denominator = rates * rates + omega * omega
        for comp_slot, coefficient in enumerate((rates / denominator, -omega / denominator)):
            term = 2 * freq_slot + comp_slot
            scaled_ref[pl.ds(term * rows, rows), :] = (factor * coefficient).astype(jnp.bfloat16)
            weighted = weight * coefficient
            row_weight_ref[term] = weighted
            pole_weight_ref[term] = jnp.broadcast_to(weighted, (lanes, weighted.shape[1])).T
    for copy in copies:
        copy.wait()


def prepare_by_kernel(
    rank, slabs, freq_index, quad_codes, pole_rates, out_factor, measured, width, lanes, halves
):
    rows, poles = out_factor.shape
    terms = 2 * freq_index.shape[0]
    vmem = pl.BlockSpec(memory_space=pltpu.VMEM)
    smem = pl.BlockSpec(memory_space=pltpu.SMEM)
    made = pl.pallas_call(
        functools.partial(prepare_kernel, slabs),
        in_specs=[smem, smem, smem, vmem, vmem, pl.BlockSpec(memory_space=pltpu.HBM)],
        out_specs=[vmem] * (4 + halves),
        out_shape=[
            jax.ShapeDtypeStruct((terms * rows, poles), jnp.bfloat16),
            jax.ShapeDtypeStruct((poles, rows), jnp.bfloat16),
            jax.ShapeDtypeStruct((terms, poles, lanes), jnp.float32),
            jax.ShapeDtypeStruct((terms, 1, poles), jnp.float32),
        ]
        + [jax.ShapeDtypeStruct((2, *measured.shape[:3], width), jnp.bfloat16)] * halves,
        scratch_shapes=[pltpu.SemaphoreType.DMA((2 * halves,))],
        compiler_params=pltpu.CompilerParams(vmem_limit_bytes=46 * 1024 * 1024),
        cost_estimate=pl.CostEstimate(
            flops=4 * terms * rows * poles, bytes_accessed=4 * terms * rows * poles, transcendentals=0
        ),
        name="prepare",
    )(rank, freq_index, quad_codes, pole_rates[None, :], out_factor, measured)
    return made[:4], list(made[4:])


def half_kernel(
    factor_0, factor_1, scaled_ref, turned_ref, pole_weight_ref, seen_ref, *refs
):
    keep_ref, send_ref, residual_ref, held_ref = refs[-4:]
    width = factor_0.shape[1]
    rows = turned_ref.shape[1]
    terms = pole_weight_ref.shape[0]
    for core, factor_ref in enumerate((factor_0, factor_1)):
        factor = factor_ref[...]
        held_ref[core] = factor
        model = jnp.dot(scaled_ref[...], factor, preferred_element_type=jnp.float32)
        seen = seen_ref[core].reshape(terms * rows, width).astype(jnp.float32)
        residual = (model - seen).astype(jnp.bfloat16)
        residual_ref[core] = residual.reshape(residual_ref.shape[1:])
        partial = None
        for term in range(terms):
            part = jnp.dot(
                turned_ref[...],
                residual[term * rows : (term + 1) * rows],
                preferred_element_type=jnp.float32,
            )
            weight = pole_weight_ref[term]
            weight = jnp.concatenate([weight] * (width // weight.shape[1]), axis=1)
            partial = weight * part if partial is None else partial + weight * part
        if core == 0:
            keep_ref[...] = partial
        elif len(refs) > 4:
            send_ref[0] = refs[0][...]
            send_ref[1] = encode(partial)
        else:
            send_ref[...] = encode(partial)


def half_by_kernel(factors, constants, seen, near_send):
    scaled, turned, pole_weight, _ = constants
    poles, width = factors[0].shape
    rows = turned.shape[1]
    terms = pole_weight.shape[0]
    half = len(factors) * width
    flops = 2 * 2 * terms * rows * poles * half
    vmem = pl.BlockSpec(memory_space=pltpu.VMEM)
    beside = [] if near_send is None else [near_send]
    return pl.pallas_call(
        half_kernel,
        in_specs=[vmem] * (6 + len(beside)),
        out_specs=[vmem] * 4,
        out_shape=[
            jax.ShapeDtypeStruct((poles, width), jnp.float32),
            jax.ShapeDtypeStruct((2, poles, width) if beside else (poles, width), jnp.bfloat16),
            jax.ShapeDtypeStruct(seen.shape, seen.dtype),
            jax.ShapeDtypeStruct((2, poles, width), jnp.bfloat16),
        ],
        input_output_aliases={5: 2},
        compiler_params=pltpu.CompilerParams(vmem_limit_bytes=24 * 1024 * 1024),
        cost_estimate=pl.CostEstimate(
            flops=50 * flops, bytes_accessed=100 * terms * rows * half, transcendentals=0
        ),
        name="far" if beside else "near",
    )(*factors, scaled, turned, pole_weight, seen, *beside)


def update_kernel(halves, *refs):
    row_weight_ref, total_ref = refs[2 * halves], refs[-1]
    terms = row_weight_ref.shape[0]
    rows, width = refs[0].shape[-2:]
    total = None
    for at in range(halves):
        residual_ref, held_ref = refs[2 * at : 2 * at + 2]
        for core in range(2):
            part = lax.dot_general(
                residual_ref[core].reshape(terms * rows, width),
                held_ref[core],
                (((1,), (1,)), ((), ())),
                preferred_element_type=jnp.float32,
            )
            total = part if total is None else total + part
    update = refs[2 * halves + 1][...] if len(refs) > 2 * halves + 2 else 0.0
    for term in range(terms):
        update = update + row_weight_ref[term] * total[term * rows : (term + 1) * rows]
    total_ref[...] = update


def update_by_kernel(halves, row_weight, update):
    poles, width = halves[0][1].shape[1:]
    rows = halves[0][0].shape[-2]
    terms = row_weight.shape[0]
    flops = 4 * len(halves) * terms * rows * poles * width
    vmem = pl.BlockSpec(memory_space=pltpu.VMEM)
    operands = [array for half in halves for array in half]
    operands += [row_weight] if update is None else [row_weight, update]
    return pl.pallas_call(
        functools.partial(update_kernel, len(halves)),
        in_specs=[vmem] * len(operands),
        out_specs=vmem,
        out_shape=jax.ShapeDtypeStruct((rows, poles), jnp.float32),
        compiler_params=pltpu.CompilerParams(vmem_limit_bytes=24 * 1024 * 1024),
        cost_estimate=pl.CostEstimate(
            flops=50 * flops, bytes_accessed=100 * terms * rows * width, transcendentals=0
        ),
        name="update",
    )(*operands)


def slice_by_ops(rank, slabs, measured, width, first_half, last_half):
    blocks = [
        lax.dynamic_slice_in_dim(
            measured, block_at(rank[0], at // 4, slabs, at % 4) * width, width, 3
        )
        for at in range(2 * first_half, 2 * last_half)
    ]
    return [jnp.stack(blocks[at : at + 2]) for at in range(0, len(blocks), 2)]


def copy_by_ops(rank, slabs, measured, width, first_half, token):
    return slice_by_ops(rank, slabs, measured, width, first_half, 2 * slabs)


def prepare_by_ops(
    rank, slabs, freq_index, quad_codes, pole_rates, out_factor, measured, width, lanes, halves
):
    rows, poles = out_factor.shape
    coefficients = pole_terms(freq_index, pole_rates)
    weights = quad_codes.astype(jnp.float32) * 0.25
    weighted = (weights[:, None, None] * coefficients).reshape(-1, poles)
    scaled = (
        out_factor.astype(jnp.float32)[None, None, :, :] * coefficients[:, :, None, :]
    ).astype(jnp.bfloat16)
    pole_weight = jnp.broadcast_to(weighted[:, :, None], (weighted.shape[0], poles, lanes))
    seen = slice_by_ops(rank, slabs, measured, width, 0, halves)
    constants = [scaled.reshape(-1, poles), out_factor.T, pole_weight, weighted[:, None, :]]
    return constants, seen


def half_by_ops(factors, constants, seen, near_send):
    scaled, turned, pole_weight, _ = constants
    width = factors[0].shape[1]
    rows = turned.shape[1]
    terms = pole_weight.shape[0]
    partials, residuals = [], []
    for core, factor in enumerate(factors):
        model = jnp.dot(scaled, factor, preferred_element_type=jnp.float32)
        residual = model - seen[core].reshape(terms * rows, width).astype(jnp.float32)
        residual = residual.astype(jnp.bfloat16)
        residuals.append(residual.reshape(seen.shape[1:]))
        partial = jnp.einsum(
            "ki,tij->tkj",
            turned,
            residual.reshape(terms, rows, width),
            preferred_element_type=jnp.float32,
        )
        partials.append(jnp.sum(pole_weight[:, :, :1] * partial, axis=0))
    send = encode(partials[1])
    if near_send is not None:
        send = jnp.stack([near_send, send])
    return partials[0], send, jnp.stack(residuals), jnp.stack(factors)


def update_by_ops(halves, row_weight, update):
    rows, width = halves[0][0].shape[-2:]
    terms = row_weight.shape[0]
    total = sum(
        jnp.einsum(
            "tij,kj->tik",
            residual[core].reshape(terms, rows, width),
            held[core],
            preferred_element_type=jnp.float32,
        )
        for residual, held in halves
        for core in range(2)
    )
    part = jnp.sum(row_weight * total, axis=0)
    return part if update is None else update + part


def after(value, earlier):
    return lax.optimization_barrier((value, *earlier))[0]


def on_device(measured, out_factor, in_factor, pole_rates, freq_index, quad_codes):
    rows, total_in = measured.shape[2:]
    poles, width = in_factor.shape
    ranks = lax.axis_size("port")
    rank = lax.axis_index("port").astype(jnp.int32).reshape(1)
    slabs = ranks // 4
    total_out = rows * ranks
    tiled = width % 128 == 0 and rows % 128 == 0
    prepare = prepare_by_kernel if tiled else prepare_by_ops
    one_half = half_by_kernel if tiled else half_by_ops
    add_update = update_by_kernel if tiled else update_by_ops
    copy_rest = copy_by_kernel if tiled else copy_by_ops
    at_once = min(3, 2 * slabs)

    def to_core(block):
        return lax.ppermute(block, "port", [(i, i ^ 1) for i in range(ranks)])

    def to_side(block):
        return lax.ppermute(block, "port", [(i, i ^ 2) for i in range(ranks)])

    ring = ring_order(slabs)
    after_slab = {slab: ring[(at + 1) % slabs] for at, slab in enumerate(ring)}

    def to_next(block):
        pairs = [(i, 4 * after_slab[i // 4] + i % 4) for i in range(ranks)]
        return lax.ppermute(block, "port", pairs)

    near = in_factor
    coming_near = to_next(near)
    coming_far = to_side(near)
    near_pair = [near, to_core(near)]
    constants, seen = prepare(
        rank,
        slabs,
        freq_index,
        quad_codes,
        pole_rates,
        out_factor,
        measured,
        width,
        min(width, 128),
        at_once,
    )
    nears = [None] * slabs
    keeps = [None] * slabs
    sends = [None] * slabs
    codes = [None] * slabs
    from_sides = [None] * slabs
    halves = []

    def near_half(step, pair, token):
        keep, sends[step], *parts = one_half(pair, constants, after(seen[2 * step], token), None)
        halves.append(parts)
        keeps[step] = [keep]
        return [parts[0]]

    def far_half(step, pair, token):
        keep, sends[step], *parts = one_half(
            pair, constants, after(seen[2 * step + 1], token), sends[step]
        )
        halves.append(parts)
        keeps[step].append(keep)
        return [parts[0]]

    def collect(step, token):
        received = decode(after(to_core(sends[step]), token))
        nears[step] = keeps[step][0] + received[0]
        codes[step] = encode(keeps[step][1] + received[1])
        return to_side(codes[step])

    def pass_on(step, arriving, token):
        total = nears[step] + decode(after(from_sides[step], token))
        if arriving is not None:
            total = total + decode(after(arriving, token))
        return encode(total)

    arriving = None
    update = None
    row_weight = constants[3]
    token = [row_weight]
    for step in range(slabs):
        far = after(coming_far, token)
        first_pair = near_pair
        if step + 1 < slabs:
            near = after(coming_near, token)
            if step + 2 < slabs:
                coming_near = to_next(near)
            if step + 2 == slabs and slabs > 2:
                coming_far = to_next(far)
            else:
                coming_far = to_side(near)
            near_pair = [near, to_core(near)]
            token = [*token, near]
        if step == 0:
            token = near_half(0, first_pair, token)
        else:
            update = add_update([halves[step - 1]], after(row_weight, [*token, far]), update)
            token = [*token, update]
        token = far_half(step, [far, to_core(far)], token)
        if step + 1 < slabs:
            token = near_half(step + 1, near_pair, token)
            if step == 0 and at_once < 2 * slabs:
                rest = copy_rest(rank, slabs, measured, width, at_once, token[0])
                seen.extend(rest)
                token = [*token, rest[0]]
        else:
            update = add_update([halves[step]], after(row_weight, token), update)
            token = [update]
        if step > 0:
            from_sides[step] = collect(step, token)
            token = [*token, codes[step]]
        if step > 1:
            code = pass_on(step - 1, arriving, token)
            arriving = to_next(code)
            token = [*token, code]

    if slabs > 1:
        middle = slabs + slabs // 2
        update = add_update(halves[slabs:middle], after(row_weight, token), update)
        code = pass_on(slabs - 1, arriving, [update])
        arriving = to_next(code)
        token = [update, code]
    from_sides[0] = collect(0, token)
    if slabs > 1:
        token = [*token, codes[0]]
        update = add_update(halves[middle:], after(row_weight, token), update)
    total = nears[0] + decode(after(from_sides[0], [update]))
    if arriving is not None:
        total = total + decode(after(arriving, [update]))

    grad_out = update * (1.0 / math.sqrt(total_in))
    grad_in_t = (total * (1.0 / math.sqrt(total_out))).T
    return (grad_out, grad_in_t)


def solution(mesh):
    in_specs = (
        P("groups", None, "port", None),
        P("port", "groups"),
        P("groups", "port"),
        P("groups"),
        P("groups"),
        P("groups"),
    )
    out_specs = (P("port", "groups"), P("port", "groups"))
    return jax.shard_map(
        on_device, mesh=mesh, in_specs=in_specs, out_specs=out_specs, check_vma=False
    )
```

```python
import functools
import math

import jax
import jax.numpy as jnp
from jax import lax
from jax.experimental import pallas as pl
from jax.experimental.pallas import tpu as pltpu
from jax.sharding import PartitionSpec as P

GRID = 1024


low_freq = 0.1
log_span = math.log(100.0)
least_code = 1e-36


def pole_terms(freq_index, pole_rates):
    omega = low_freq * jnp.exp(log_span * freq_index.astype(jnp.float32) / (GRID - 1))
    denominator = pole_rates[None, :] * pole_rates[None, :] + omega[:, None] * omega[:, None]
    real_side = pole_rates[None, :] / denominator
    imag_side = -omega[:, None] / denominator
    return jnp.stack([real_side, imag_side], axis=1)


def encode(value):
    return ((value * jnp.abs(value)) * (value * value)).astype(jnp.bfloat16)


def decode(code):
    code = code.astype(jnp.float32)
    inverse_root = lax.rsqrt(jnp.maximum(jnp.abs(code), least_code))
    return (code * inverse_root) * (inverse_root * lax.rsqrt(inverse_root))


def ring_order(slabs):
    return [0, *range(1, slabs, 2), *reversed(range(2, slabs, 2))]


def block_at(rank, step, slabs, flip):
    slab = lax.div(rank, 4)
    place = jnp.where(lax.rem(slab, 2) == 1, lax.div(slab + 1, 2), slabs - lax.div(slab, 2))
    place = lax.rem(place + (slabs - step), slabs)
    slab = jnp.where(place <= slabs // 2, 2 * place - 1, 2 * (slabs - place))
    slab = jnp.where(place == 0, 0, slab)
    return 4 * slab + (lax.rem(rank, 4) ^ flip)


def start_copies(rank_ref, measured_ref, first_half, slabs, halves, arrived):
    width = halves[0].shape[-1]
    copies = []
    for at, half in enumerate(halves):
        for core in range(2):
            place = 2 * (first_half + at) + core
            block = block_at(rank_ref[0], place // 4, slabs, place % 4)
            columns = pl.ds(pl.multiple_of(block * width, width), width)
            copy = pltpu.make_async_copy(
                measured_ref.at[:, :, :, columns], half.at[core], arrived.at[2 * at + core]
            )
            copy.start()
            copies.append(copy)
    return copies


def copy_kernel(first_half, slabs, rank_ref, measured_ref, after_ref, *refs):
    del after_ref
    for copy in start_copies(rank_ref, measured_ref, first_half, slabs, refs[:-1], refs[-1]):
        copy.wait()


def copy_by_kernel(rank, slabs, measured, width, first_half, token):
    halves = 2 * slabs - first_half
    vmem = pl.BlockSpec(memory_space=pltpu.VMEM)
    anywhere = pl.BlockSpec(memory_space=pl.ANY)
    shape = jax.ShapeDtypeStruct((2, *measured.shape[:3], width), jnp.bfloat16)
    return pl.pallas_call(
        functools.partial(copy_kernel, first_half, slabs),
        in_specs=[pl.BlockSpec(memory_space=pltpu.SMEM), anywhere, anywhere],
        out_specs=[vmem] * halves,
        out_shape=[shape] * halves,
        scratch_shapes=[pltpu.SemaphoreType.DMA((2 * halves,))],
        compiler_params=pltpu.CompilerParams(vmem_limit_bytes=16 * 1024 * 1024),
        cost_estimate=pl.CostEstimate(
            flops=0, bytes_accessed=halves * measured.size // slabs, transcendentals=0
        ),
        name="copy_measured",
    )(rank, pltpu.with_memory_space_constraint(measured, pltpu.HBM), token)


def prepare_kernel(
    slabs,
    rank_ref,
    freq_hbm,
    quad_hbm,
    rates_hbm,
    factor_hbm,
    measured_ref,
    scaled_ref,
    turned_ref,
    pole_weight_ref,
    row_weight_ref,
    *refs,
):
    freq_ref, quad_ref, rates_ref, factor_ref, came, arrived = refs[-6:]
    pairs = ((freq_hbm, freq_ref), (quad_hbm, quad_ref), (rates_hbm, rates_ref), (factor_hbm, factor_ref))
    small = [pltpu.make_async_copy(*pair, came.at[at]) for at, pair in enumerate(pairs)]
    for copy in small:
        copy.start()
    copies = start_copies(rank_ref, measured_ref, 0, slabs, refs[:-6], arrived)
    for copy in small:
        copy.wait()
    rates = rates_ref[...]
    factor = factor_ref[...].astype(jnp.float32)
    turned_ref[...] = factor.T.astype(jnp.bfloat16)
    rows = factor.shape[0]
    lanes = pole_weight_ref.shape[2]
    for freq_slot in range(freq_ref.shape[0]):
        index = jnp.full(rates.shape, freq_ref[freq_slot], jnp.int32).astype(jnp.float32)
        weight = jnp.full(rates.shape, quad_ref[freq_slot], jnp.int32).astype(jnp.float32) * 0.25
        omega = low_freq * jnp.exp(log_span * index / (GRID - 1))
        denominator = rates * rates + omega * omega
        for comp_slot, coefficient in enumerate((rates / denominator, -omega / denominator)):
            term = 2 * freq_slot + comp_slot
            scaled_ref[pl.ds(term * rows, rows), :] = (factor * coefficient).astype(jnp.bfloat16)
            weighted = weight * coefficient
            row_weight_ref[term] = weighted
            pole_weight_ref[term] = jnp.broadcast_to(weighted, (lanes, weighted.shape[1])).T
    for copy in copies:
        copy.wait()


def prepare_by_kernel(
    rank, slabs, freq_index, quad_codes, pole_rates, out_factor, measured, width, lanes, halves
):
    rows, poles = out_factor.shape
    terms = 2 * freq_index.shape[0]
    vmem = pl.BlockSpec(memory_space=pltpu.VMEM)
    smem = pl.BlockSpec(memory_space=pltpu.SMEM)
    anywhere = pl.BlockSpec(memory_space=pl.ANY)
    operands = (freq_index, quad_codes, pole_rates[None, :], out_factor, measured)
    made = pl.pallas_call(
        functools.partial(prepare_kernel, slabs),
        in_specs=[smem] + [anywhere] * 5,
        out_specs=[vmem] * (4 + halves),
        out_shape=[
            jax.ShapeDtypeStruct((terms * rows, poles), jnp.bfloat16),
            jax.ShapeDtypeStruct((poles, rows), jnp.bfloat16),
            jax.ShapeDtypeStruct((terms, poles, lanes), jnp.float32),
            jax.ShapeDtypeStruct((terms, 1, poles), jnp.float32),
        ]
        + [jax.ShapeDtypeStruct((2, *measured.shape[:3], width), jnp.bfloat16)] * halves,
        scratch_shapes=[
            pltpu.SMEM(freq_index.shape, jnp.int32),
            pltpu.SMEM(quad_codes.shape, jnp.int32),
            pltpu.VMEM((1, poles), jnp.float32),
            pltpu.VMEM((rows, poles), jnp.bfloat16),
            pltpu.SemaphoreType.DMA((4,)),
            pltpu.SemaphoreType.DMA((2 * halves,)),
        ],
        compiler_params=pltpu.CompilerParams(vmem_limit_bytes=16 * 1024 * 1024),
        cost_estimate=pl.CostEstimate(
            flops=0, bytes_accessed=halves * measured.size // slabs, transcendentals=0
        ),
        name="prepare",
    )(rank, *[pltpu.with_memory_space_constraint(array, pltpu.HBM) for array in operands])
    return made[:4], list(made[4:])


def half_kernel(
    factor_0, factor_1, scaled_ref, turned_ref, pole_weight_ref, seen_ref, *refs
):
    keep_ref, send_ref, residual_ref, held_ref = refs[-4:]
    width = factor_0.shape[1]
    rows = turned_ref.shape[1]
    terms = pole_weight_ref.shape[0]
    for core, factor_ref in enumerate((factor_0, factor_1)):
        factor = factor_ref[...]
        held_ref[core] = factor
        model = jnp.dot(scaled_ref[...], factor, preferred_element_type=jnp.float32)
        seen = seen_ref[core].reshape(terms * rows, width).astype(jnp.float32)
        residual = (model - seen).astype(jnp.bfloat16)
        residual_ref[core] = residual.reshape(residual_ref.shape[1:])
        partial = None
        for term in range(terms):
            part = jnp.dot(
                turned_ref[...],
                residual[term * rows : (term + 1) * rows],
                preferred_element_type=jnp.float32,
            )
            weight = pole_weight_ref[term]
            weight = jnp.concatenate([weight] * (width // weight.shape[1]), axis=1)
            partial = weight * part if partial is None else partial + weight * part
        if core == 0:
            keep_ref[...] = partial
        elif len(refs) > 4:
            send_ref[0] = refs[0][...]
            send_ref[1] = encode(partial)
        else:
            send_ref[...] = encode(partial)


def half_by_kernel(factors, constants, seen, near_send):
    scaled, turned, pole_weight, _ = constants
    poles, width = factors[0].shape
    rows = turned.shape[1]
    terms = pole_weight.shape[0]
    half = len(factors) * width
    flops = 2 * 2 * terms * rows * poles * half
    vmem = pl.BlockSpec(memory_space=pltpu.VMEM)
    beside = [] if near_send is None else [near_send]
    return pl.pallas_call(
        half_kernel,
        in_specs=[vmem] * (6 + len(beside)),
        out_specs=[vmem] * 4,
        out_shape=[
            jax.ShapeDtypeStruct((poles, width), jnp.float32),
            jax.ShapeDtypeStruct((2, poles, width) if beside else (poles, width), jnp.bfloat16),
            jax.ShapeDtypeStruct(seen.shape, seen.dtype),
            jax.ShapeDtypeStruct((2, poles, width), jnp.bfloat16),
        ],
        input_output_aliases={5: 2},
        compiler_params=pltpu.CompilerParams(vmem_limit_bytes=16 * 1024 * 1024),
        cost_estimate=pl.CostEstimate(
            flops=10 * flops, bytes_accessed=2 * terms * rows * half, transcendentals=0
        ),
        name="far" if beside else "near",
    )(*factors, scaled, turned, pole_weight, seen, *beside)


def update_kernel(halves, *refs):
    row_weight_ref, total_ref = refs[2 * halves], refs[-1]
    terms = row_weight_ref.shape[0]
    rows, width = refs[0].shape[-2:]
    total = None
    for at in range(halves):
        residual_ref, held_ref = refs[2 * at : 2 * at + 2]
        for core in range(2):
            part = lax.dot_general(
                residual_ref[core].reshape(terms * rows, width),
                held_ref[core],
                (((1,), (1,)), ((), ())),
                preferred_element_type=jnp.float32,
            )
            total = part if total is None else total + part
    update = refs[2 * halves + 1][...] if len(refs) > 2 * halves + 2 else 0.0
    for term in range(terms):
        update = update + row_weight_ref[term] * total[term * rows : (term + 1) * rows]
    total_ref[...] = update


def update_by_kernel(halves, row_weight, update):
    poles, width = halves[0][1].shape[1:]
    rows = halves[0][0].shape[-2]
    terms = row_weight.shape[0]
    flops = 4 * len(halves) * terms * rows * poles * width
    vmem = pl.BlockSpec(memory_space=pltpu.VMEM)
    operands = [array for half in halves for array in half]
    operands += [row_weight] if update is None else [row_weight, update]
    return pl.pallas_call(
        functools.partial(update_kernel, len(halves)),
        in_specs=[vmem] * len(operands),
        out_specs=vmem,
        out_shape=jax.ShapeDtypeStruct((rows, poles), jnp.float32),
        compiler_params=pltpu.CompilerParams(vmem_limit_bytes=16 * 1024 * 1024),
        cost_estimate=pl.CostEstimate(
            flops=30 * flops, bytes_accessed=2 * terms * rows * width, transcendentals=0
        ),
        name="update",
    )(*operands)


def slice_by_ops(rank, slabs, measured, width, first_half, last_half):
    blocks = [
        lax.dynamic_slice_in_dim(
            measured, block_at(rank[0], at // 4, slabs, at % 4) * width, width, 3
        )
        for at in range(2 * first_half, 2 * last_half)
    ]
    return [jnp.stack(blocks[at : at + 2]) for at in range(0, len(blocks), 2)]


def copy_by_ops(rank, slabs, measured, width, first_half, token):
    return slice_by_ops(rank, slabs, measured, width, first_half, 2 * slabs)


def prepare_by_ops(
    rank, slabs, freq_index, quad_codes, pole_rates, out_factor, measured, width, lanes, halves
):
    rows, poles = out_factor.shape
    coefficients = pole_terms(freq_index, pole_rates)
    weights = quad_codes.astype(jnp.float32) * 0.25
    weighted = (weights[:, None, None] * coefficients).reshape(-1, poles)
    scaled = (
        out_factor.astype(jnp.float32)[None, None, :, :] * coefficients[:, :, None, :]
    ).astype(jnp.bfloat16)
    pole_weight = jnp.broadcast_to(weighted[:, :, None], (weighted.shape[0], poles, lanes))
    seen = slice_by_ops(rank, slabs, measured, width, 0, halves)
    constants = [scaled.reshape(-1, poles), out_factor.T, pole_weight, weighted[:, None, :]]
    return constants, seen


def half_by_ops(factors, constants, seen, near_send):
    scaled, turned, pole_weight, _ = constants
    width = factors[0].shape[1]
    rows = turned.shape[1]
    terms = pole_weight.shape[0]
    partials, residuals = [], []
    for core, factor in enumerate(factors):
        model = jnp.dot(scaled, factor, preferred_element_type=jnp.float32)
        residual = model - seen[core].reshape(terms * rows, width).astype(jnp.float32)
        residual = residual.astype(jnp.bfloat16)
        residuals.append(residual.reshape(seen.shape[1:]))
        partial = jnp.einsum(
            "ki,tij->tkj",
            turned,
            residual.reshape(terms, rows, width),
            preferred_element_type=jnp.float32,
        )
        partials.append(jnp.sum(pole_weight[:, :, :1] * partial, axis=0))
    send = encode(partials[1])
    if near_send is not None:
        send = jnp.stack([near_send, send])
    return partials[0], send, jnp.stack(residuals), jnp.stack(factors)


def update_by_ops(halves, row_weight, update):
    rows, width = halves[0][0].shape[-2:]
    terms = row_weight.shape[0]
    total = sum(
        jnp.einsum(
            "tij,kj->tik",
            residual[core].reshape(terms, rows, width),
            held[core],
            preferred_element_type=jnp.float32,
        )
        for residual, held in halves
        for core in range(2)
    )
    part = jnp.sum(row_weight * total, axis=0)
    return part if update is None else update + part


def after(value, earlier):
    return lax.optimization_barrier((value, *earlier))[0]


def on_device(measured, out_factor, in_factor, pole_rates, freq_index, quad_codes):
    rows, total_in = measured.shape[2:]
    poles, width = in_factor.shape
    ranks = lax.axis_size("port")
    rank = lax.axis_index("port").astype(jnp.int32).reshape(1)
    slabs = ranks // 4
    total_out = rows * ranks
    tiled = width % 128 == 0 and rows % 128 == 0
    prepare = prepare_by_kernel if tiled else prepare_by_ops
    one_half = half_by_kernel if tiled else half_by_ops
    add_update = update_by_kernel if tiled else update_by_ops
    copy_rest = copy_by_kernel if tiled else copy_by_ops
    at_once = min(3, 2 * slabs)

    def to_core(block):
        return lax.ppermute(block, "port", [(i, i ^ 1) for i in range(ranks)])

    def to_side(block):
        return lax.ppermute(block, "port", [(i, i ^ 2) for i in range(ranks)])

    ring = ring_order(slabs)
    place = {slab: at for at, slab in enumerate(ring)}

    def along(block, hops):
        pairs = [
            (i, 4 * ring[(place[i // 4] + hops) % slabs] + i % 4) for i in range(ranks)
        ]
        return lax.ppermute(block, "port", pairs)

    near = in_factor
    coming_nears = [None] + [along(near, step) for step in range(1, slabs)]
    coming_far = to_side(near)
    near_pair = [near, to_core(near)]
    constants, seen = prepare(
        rank,
        slabs,
        freq_index,
        quad_codes,
        pole_rates,
        out_factor,
        measured,
        width,
        min(width, 128),
        at_once,
    )
    nears = [None] * slabs
    keeps = [None] * slabs
    sends = [None] * slabs
    codes = [None] * slabs
    from_sides = [None] * slabs
    halves = []

    def near_half(step, pair, token):
        keep, sends[step], *parts = one_half(pair, constants, after(seen[2 * step], token), None)
        halves.append(parts)
        keeps[step] = [keep]
        return [parts[0]]

    def far_half(step, pair, token):
        keep, sends[step], *parts = one_half(
            pair, constants, after(seen[2 * step + 1], token), sends[step]
        )
        halves.append(parts)
        keeps[step].append(keep)
        return [parts[0]]

    def collect(step, token):
        received = decode(after(to_core(sends[step]), token))
        nears[step] = keeps[step][0] + received[0]
        codes[step] = encode(keeps[step][1] + received[1])
        return to_side(codes[step])

    def pass_on(step, arriving, token):
        total = nears[step] + decode(after(from_sides[step], token))
        if arriving is not None:
            total = total + decode(after(arriving, token))
        return encode(total)

    arriving = None
    from_next = None
    update = None
    row_weight = constants[3]
    token = [row_weight]
    for step in range(slabs):
        far = after(coming_far, token)
        first_pair = near_pair
        if step + 1 < slabs:
            near = after(coming_nears[step + 1], token)
            if step + 2 == slabs and slabs > 2:
                coming_far = along(far, 1)
            else:
                coming_far = to_side(near)
            near_pair = [near, to_core(near)]
            token = [*token, near]
        if step == 0:
            token = near_half(0, first_pair, token)
        else:
            update = add_update([halves[step - 1]], after(row_weight, [*token, far]), update)
            token = [*token, update]
        token = far_half(step, [far, to_core(far)], token)
        if step + 1 < slabs:
            token = near_half(step + 1, near_pair, token)
            if step == 0 and at_once < 2 * slabs:
                rest = copy_rest(rank, slabs, measured, width, at_once, token[0])
                seen.extend(rest)
                token = [*token, rest[0]]
        else:
            update = add_update([halves[step]], after(row_weight, token), update)
            token = [update]
        if step > 0:
            from_sides[step] = collect(step, token)
            token = [*token, codes[step]]
        if step > 2:
            code = pass_on(step - 1, arriving, token)
            arriving = along(code, 1)
            token = [*token, code]

    if slabs > 2:
        code = pass_on(1, None, token)
        from_next = along(code, -1)
        token = [*token, code]

    if slabs > 1:
        middle = slabs + slabs // 2
        update = add_update(halves[slabs:middle], after(row_weight, token), update)
        code = pass_on(slabs - 1, arriving, [update])
        arriving = along(code, 1)
        token = [update, code]
    from_sides[0] = collect(0, token)
    if slabs > 1:
        token = [*token, codes[0]]
        update = add_update(halves[middle:], after(row_weight, token), update)
    total = nears[0] + decode(after(from_sides[0], [update]))
    for sums in (from_next, arriving):
        if sums is not None:
            total = total + decode(after(sums, [update]))

    grad_out = update * (1.0 / math.sqrt(total_in))
    grad_in_t = (total * (1.0 / math.sqrt(total_out))).T
    return (grad_out, grad_in_t)


def solution(mesh):
    in_specs = (
        P("groups", None, "port", None),
        P("port", "groups"),
        P("groups", "port"),
        P("groups"),
        P("groups"),
        P("groups"),
    )
    out_specs = (P("port", "groups"), P("port", "groups"))
    return jax.shard_map(
        on_device, mesh=mesh, in_specs=in_specs, out_specs=out_specs, check_vma=False
    )
```

```python
import functools
import math

import jax
import jax.numpy as jnp
from jax import lax
from jax.experimental import pallas as pl
from jax.experimental.pallas import tpu as pltpu
from jax.sharding import PartitionSpec as P

GRID = 1024


low_freq = 0.1
log_span = math.log(100.0)
least_code = 1e-36


def pole_terms(freq_index, pole_rates):
    omega = low_freq * jnp.exp(log_span * freq_index.astype(jnp.float32) / (GRID - 1))
    denominator = pole_rates[None, :] * pole_rates[None, :] + omega[:, None] * omega[:, None]
    real_side = pole_rates[None, :] / denominator
    imag_side = -omega[:, None] / denominator
    return jnp.stack([real_side, imag_side], axis=1)


def encode(value):
    return ((value * jnp.abs(value)) * (value * value)).astype(jnp.bfloat16)


def decode(code):
    code = code.astype(jnp.float32)
    inverse_root = lax.rsqrt(jnp.maximum(jnp.abs(code), least_code))
    return (code * inverse_root) * (inverse_root * lax.rsqrt(inverse_root))


def ring_order(slabs):
    return [0, *range(1, slabs, 2), *reversed(range(2, slabs, 2))]


def block_at(rank, step, slabs, flip):
    slab = lax.div(rank, 4)
    place = jnp.where(lax.rem(slab, 2) == 1, lax.div(slab + 1, 2), slabs - lax.div(slab, 2))
    place = lax.rem(place + (slabs - step), slabs)
    slab = jnp.where(place <= slabs // 2, 2 * place - 1, 2 * (slabs - place))
    slab = jnp.where(place == 0, 0, slab)
    return 4 * slab + (lax.rem(rank, 4) ^ flip)


def start_copies(rank_ref, measured_ref, first_half, slabs, halves, arrived):
    width = halves[0].shape[-1]
    copies = []
    for at, half in enumerate(halves):
        for core in range(2):
            place = 2 * (first_half + at) + core
            block = block_at(rank_ref[0], place // 4, slabs, place % 4)
            columns = pl.ds(pl.multiple_of(block * width, width), width)
            copy = pltpu.make_async_copy(
                measured_ref.at[:, :, :, columns], half.at[core], arrived.at[2 * at + core]
            )
            copy.start()
            copies.append(copy)
    return copies


def prepare_kernel(
    slabs,
    rank_ref,
    freq_hbm,
    quad_hbm,
    rates_hbm,
    factor_hbm,
    measured_ref,
    scaled_ref,
    turned_ref,
    pole_weight_ref,
    row_weight_ref,
    *refs,
):
    freq_ref, quad_ref, rates_ref, factor_ref, came, arrived = refs[-6:]
    pairs = ((freq_hbm, freq_ref), (quad_hbm, quad_ref), (rates_hbm, rates_ref), (factor_hbm, factor_ref))
    small = [pltpu.make_async_copy(*pair, came.at[at]) for at, pair in enumerate(pairs)]
    for copy in small:
        copy.start()
    copies = start_copies(rank_ref, measured_ref, 0, slabs, refs[:-6], arrived)
    for copy in small:
        copy.wait()
    rates = rates_ref[...]
    factor = factor_ref[...].astype(jnp.float32)
    turned_ref[...] = factor.T.astype(jnp.bfloat16)
    rows = factor.shape[0]
    lanes = pole_weight_ref.shape[2]
    for freq_slot in range(freq_ref.shape[0]):
        index = jnp.full(rates.shape, freq_ref[freq_slot], jnp.int32).astype(jnp.float32)
        weight = jnp.full(rates.shape, quad_ref[freq_slot], jnp.int32).astype(jnp.float32) * 0.25
        omega = low_freq * jnp.exp(log_span * index / (GRID - 1))
        denominator = rates * rates + omega * omega
        for comp_slot, coefficient in enumerate((rates / denominator, -omega / denominator)):
            term = 2 * freq_slot + comp_slot
            scaled_ref[pl.ds(term * rows, rows), :] = (factor * coefficient).astype(jnp.bfloat16)
            weighted = weight * coefficient
            row_weight_ref[term] = weighted
            pole_weight_ref[term] = jnp.broadcast_to(weighted, (lanes, weighted.shape[1])).T
    for copy in copies:
        copy.wait()


def prepare_by_kernel(
    rank, slabs, freq_index, quad_codes, pole_rates, out_factor, measured, width, lanes, halves
):
    rows, poles = out_factor.shape
    terms = 2 * freq_index.shape[0]
    vmem = pl.BlockSpec(memory_space=pltpu.VMEM)
    smem = pl.BlockSpec(memory_space=pltpu.SMEM)
    anywhere = pl.BlockSpec(memory_space=pl.ANY)
    operands = (freq_index, quad_codes, pole_rates[None, :], out_factor, measured)
    made = pl.pallas_call(
        functools.partial(prepare_kernel, slabs),
        in_specs=[smem] + [anywhere] * 5,
        out_specs=[vmem] * (4 + halves),
        out_shape=[
            jax.ShapeDtypeStruct((terms * rows, poles), jnp.bfloat16),
            jax.ShapeDtypeStruct((poles, rows), jnp.bfloat16),
            jax.ShapeDtypeStruct((terms, poles, lanes), jnp.float32),
            jax.ShapeDtypeStruct((terms, 1, poles), jnp.float32),
        ]
        + [jax.ShapeDtypeStruct((2, *measured.shape[:3], width), jnp.bfloat16)] * halves,
        scratch_shapes=[
            pltpu.SMEM(freq_index.shape, jnp.int32),
            pltpu.SMEM(quad_codes.shape, jnp.int32),
            pltpu.VMEM((1, poles), jnp.float32),
            pltpu.VMEM((rows, poles), jnp.bfloat16),
            pltpu.SemaphoreType.DMA((4,)),
            pltpu.SemaphoreType.DMA((2 * halves,)),
        ],
        compiler_params=pltpu.CompilerParams(vmem_limit_bytes=16 * 1024 * 1024),
        cost_estimate=pl.CostEstimate(
            flops=0, bytes_accessed=halves * measured.size // slabs, transcendentals=0
        ),
        name="prepare",
    )(rank, *[pltpu.with_memory_space_constraint(array, pltpu.HBM) for array in operands])
    return made[:4], list(made[4:])


def half_kernel(
    factor_0, factor_1, scaled_ref, turned_ref, pole_weight_ref, seen_ref, *refs
):
    keep_ref, send_ref, residual_ref, held_ref = refs[-4:]
    width = factor_0.shape[1]
    rows = turned_ref.shape[1]
    terms = pole_weight_ref.shape[0]
    for core, factor_ref in enumerate((factor_0, factor_1)):
        factor = factor_ref[...]
        held_ref[core] = factor
        model = jnp.dot(scaled_ref[...], factor, preferred_element_type=jnp.float32)
        seen = seen_ref[core].reshape(terms * rows, width).astype(jnp.float32)
        residual = (model - seen).astype(jnp.bfloat16)
        residual_ref[core] = residual.reshape(residual_ref.shape[1:])
        partial = None
        for term in range(terms):
            part = jnp.dot(
                turned_ref[...],
                residual[term * rows : (term + 1) * rows],
                preferred_element_type=jnp.float32,
            )
            weight = pole_weight_ref[term]
            weight = jnp.concatenate([weight] * (width // weight.shape[1]), axis=1)
            partial = weight * part if partial is None else partial + weight * part
        if core == 0:
            keep_ref[...] = partial
        elif len(refs) > 4:
            send_ref[0] = refs[0][...]
            send_ref[1] = encode(partial)
        else:
            send_ref[...] = encode(partial)


def half_by_kernel(factors, constants, seen, near_send):
    scaled, turned, pole_weight, _ = constants
    poles, width = factors[0].shape
    rows = turned.shape[1]
    terms = pole_weight.shape[0]
    half = len(factors) * width
    flops = 2 * 2 * terms * rows * poles * half
    vmem = pl.BlockSpec(memory_space=pltpu.VMEM)
    beside = [] if near_send is None else [near_send]
    return pl.pallas_call(
        half_kernel,
        in_specs=[vmem] * (6 + len(beside)),
        out_specs=[vmem] * 4,
        out_shape=[
            jax.ShapeDtypeStruct((poles, width), jnp.float32),
            jax.ShapeDtypeStruct((2, poles, width) if beside else (poles, width), jnp.bfloat16),
            jax.ShapeDtypeStruct(seen.shape, seen.dtype),
            jax.ShapeDtypeStruct((2, poles, width), jnp.bfloat16),
        ],
        input_output_aliases={5: 2},
        compiler_params=pltpu.CompilerParams(vmem_limit_bytes=16 * 1024 * 1024),
        cost_estimate=pl.CostEstimate(
            flops=10 * flops, bytes_accessed=2 * terms * rows * half, transcendentals=0
        ),
        name="far" if beside else "near",
    )(*factors, scaled, turned, pole_weight, seen, *beside)


def update_kernel(halves, scale, *refs):
    row_weight_ref, total_ref = refs[2 * halves], refs[-1]
    terms = row_weight_ref.shape[0]
    rows, width = refs[0].shape[-2:]
    total = None
    for at in range(halves):
        residual_ref, held_ref = refs[2 * at : 2 * at + 2]
        for core in range(2):
            part = lax.dot_general(
                residual_ref[core].reshape(terms * rows, width),
                held_ref[core],
                (((1,), (1,)), ((), ())),
                preferred_element_type=jnp.float32,
            )
            total = part if total is None else total + part
    update = refs[2 * halves + 1][...] if len(refs) > 2 * halves + 2 else 0.0
    for term in range(terms):
        update = update + row_weight_ref[term] * total[term * rows : (term + 1) * rows]
    total_ref[...] = update if scale is None else update * scale


def update_by_kernel(halves, row_weight, update, scale=None):
    poles, width = halves[0][1].shape[1:]
    rows = halves[0][0].shape[-2]
    terms = row_weight.shape[0]
    flops = 4 * len(halves) * terms * rows * poles * width
    vmem = pl.BlockSpec(memory_space=pltpu.VMEM)
    operands = [array for half in halves for array in half]
    operands += [row_weight] if update is None else [row_weight, update]
    return pl.pallas_call(
        functools.partial(update_kernel, len(halves), scale),
        in_specs=[vmem] * len(operands),
        out_specs=vmem,
        out_shape=jax.ShapeDtypeStruct((rows, poles), jnp.float32),
        compiler_params=pltpu.CompilerParams(vmem_limit_bytes=16 * 1024 * 1024),
        cost_estimate=pl.CostEstimate(
            flops=30 * flops, bytes_accessed=2 * terms * rows * width, transcendentals=0
        ),
        name="update",
    )(*operands)


def slice_by_ops(rank, slabs, measured, width, first_half, last_half):
    blocks = [
        lax.dynamic_slice_in_dim(
            measured, block_at(rank[0], at // 4, slabs, at % 4) * width, width, 3
        )
        for at in range(2 * first_half, 2 * last_half)
    ]
    return [jnp.stack(blocks[at : at + 2]) for at in range(0, len(blocks), 2)]


def prepare_by_ops(
    rank, slabs, freq_index, quad_codes, pole_rates, out_factor, measured, width, lanes, halves
):
    rows, poles = out_factor.shape
    coefficients = pole_terms(freq_index, pole_rates)
    weights = quad_codes.astype(jnp.float32) * 0.25
    weighted = (weights[:, None, None] * coefficients).reshape(-1, poles)
    scaled = (
        out_factor.astype(jnp.float32)[None, None, :, :] * coefficients[:, :, None, :]
    ).astype(jnp.bfloat16)
    pole_weight = jnp.broadcast_to(weighted[:, :, None], (weighted.shape[0], poles, lanes))
    seen = slice_by_ops(rank, slabs, measured, width, 0, halves)
    constants = [scaled.reshape(-1, poles), out_factor.T, pole_weight, weighted[:, None, :]]
    return constants, seen


def half_by_ops(factors, constants, seen, near_send):
    scaled, turned, pole_weight, _ = constants
    width = factors[0].shape[1]
    rows = turned.shape[1]
    terms = pole_weight.shape[0]
    partials, residuals = [], []
    for core, factor in enumerate(factors):
        model = jnp.dot(scaled, factor, preferred_element_type=jnp.float32)
        residual = model - seen[core].reshape(terms * rows, width).astype(jnp.float32)
        residual = residual.astype(jnp.bfloat16)
        residuals.append(residual.reshape(seen.shape[1:]))
        partial = jnp.einsum(
            "ki,tij->tkj",
            turned,
            residual.reshape(terms, rows, width),
            preferred_element_type=jnp.float32,
        )
        partials.append(jnp.sum(pole_weight[:, :, :1] * partial, axis=0))
    send = encode(partials[1])
    if near_send is not None:
        send = jnp.stack([near_send, send])
    return partials[0], send, jnp.stack(residuals), jnp.stack(factors)


def update_by_ops(halves, row_weight, update, scale=None):
    rows, width = halves[0][0].shape[-2:]
    terms = row_weight.shape[0]
    total = sum(
        jnp.einsum(
            "tij,kj->tik",
            residual[core].reshape(terms, rows, width),
            held[core],
            preferred_element_type=jnp.float32,
        )
        for residual, held in halves
        for core in range(2)
    )
    part = jnp.sum(row_weight * total, axis=0)
    total = part if update is None else update + part
    return total if scale is None else total * scale


def after(value, earlier):
    return lax.optimization_barrier((value, *earlier))[0]


def on_device(measured, out_factor, in_factor, pole_rates, freq_index, quad_codes):
    rows, total_in = measured.shape[2:]
    poles, width = in_factor.shape
    ranks = lax.axis_size("port")
    rank = lax.axis_index("port").astype(jnp.int32).reshape(1)
    slabs = ranks // 4
    total_out = rows * ranks
    tiled = width % 128 == 0 and rows % 128 == 0
    prepare = prepare_by_kernel if tiled else prepare_by_ops
    one_half = half_by_kernel if tiled else half_by_ops
    add_update = update_by_kernel if tiled else update_by_ops

    def to_core(block):
        return lax.ppermute(block, "port", [(i, i ^ 1) for i in range(ranks)])

    def to_side(block):
        return lax.ppermute(block, "port", [(i, i ^ 2) for i in range(ranks)])

    ring = ring_order(slabs)
    place = {slab: at for at, slab in enumerate(ring)}

    def along(block, hops):
        pairs = [
            (i, 4 * ring[(place[i // 4] + hops) % slabs] + i % 4) for i in range(ranks)
        ]
        return lax.ppermute(block, "port", pairs)

    near = in_factor
    coming_near = along(near, 1)
    coming_far = to_side(near)
    near_pair = [near, to_core(near)]
    constants, seen = prepare(
        rank,
        slabs,
        freq_index,
        quad_codes,
        pole_rates,
        out_factor,
        measured,
        width,
        min(width, 128),
        2 * slabs,
    )
    nears = [None] * slabs
    keeps = [None] * slabs
    sends = [None] * slabs
    codes = [None] * slabs
    from_sides = [None] * slabs
    halves = []

    def near_half(step, pair, token):
        keep, sends[step], *parts = one_half(pair, constants, after(seen[2 * step], token), None)
        halves.append(parts)
        keeps[step] = [keep]
        return [parts[0]]

    def far_half(step, pair, token):
        keep, sends[step], *parts = one_half(
            pair, constants, after(seen[2 * step + 1], token), sends[step]
        )
        halves.append(parts)
        keeps[step].append(keep)
        return [parts[0]]

    def collect(step, token):
        received = decode(after(to_core(sends[step]), token))
        nears[step] = keeps[step][0] + received[0]
        codes[step] = encode(keeps[step][1] + received[1])
        return [*token, codes[step]]

    def pass_on(step, arriving, token):
        total = nears[step] + decode(after(from_sides[step], token))
        if arriving is not None:
            total = total + decode(after(arriving, token))
        return encode(total)

    arriving = None
    from_next = None
    update = None
    row_weight = constants[3]
    token = near_half(0, near_pair, [row_weight])
    for step in range(slabs):
        far = after(coming_far, token)
        if step + 1 < slabs:
            near = after(coming_near, token)
            if step + 2 < slabs:
                coming_near = along(near, 1)
            if step + 2 == slabs and slabs > 2:
                coming_far = along(far, 1)
            else:
                coming_far = to_side(near)
            near_pair = [near, to_core(near)]
            token = [*token, near]
        if step > 0:
            update = add_update([halves[step - 1]], after(row_weight, [*token, far]), update)
            token = [*token, update]
        token = far_half(step, [far, to_core(far)], token)
        if step + 1 < slabs:
            token = near_half(step + 1, near_pair, token)
        else:
            update = add_update([halves[step]], after(row_weight, token), update)
            token = [update]
            if slabs > 2:
                code = pass_on(1, None, token)
                from_next = along(code, -1)
                token = [*token, code]
        token = collect(step, token)
        if step > 0:
            from_sides[step] = to_side(codes[step])
        if step > 2:
            code = pass_on(step - 1, arriving, token)
            arriving = along(code, 1)
            token = [*token, code]

    if slabs > 1:
        middle = slabs + slabs // 2
        update = add_update(halves[slabs:middle], after(row_weight, token), update)
        code = pass_on(slabs - 1, arriving, [update])
        arriving = along(code, 1)
        token = [update, code]
    from_sides[0] = to_side(after(codes[0], token))
    if slabs > 1:
        grad_out = add_update(
            halves[middle:], after(row_weight, token), update, 1.0 / math.sqrt(total_in)
        )
    else:
        grad_out = update * (1.0 / math.sqrt(total_in))
    total = nears[0] + decode(after(from_sides[0], [grad_out]))
    for sums in (from_next, arriving):
        if sums is not None:
            total = total + decode(after(sums, [grad_out]))

    grad_in_t = (total * (1.0 / math.sqrt(total_out))).T
    return (grad_out, grad_in_t)


def solution(mesh):
    in_specs = (
        P("groups", None, "port", None),
        P("port", "groups"),
        P("groups", "port"),
        P("groups"),
        P("groups"),
        P("groups"),
    )
    out_specs = (P("port", "groups"), P("port", "groups"))
    return jax.shard_map(
        on_device, mesh=mesh, in_specs=in_specs, out_specs=out_specs, check_vma=False
    )
```

```python
import functools
import math

import jax
import jax.numpy as jnp
from jax import lax
from jax.experimental import pallas as pl
from jax.experimental.pallas import tpu as pltpu
from jax.sharding import PartitionSpec as P

GRID = 1024


low_freq = 0.1
log_span = math.log(100.0)
least_code = 1e-36


def pole_terms(freq_index, pole_rates):
    omega = low_freq * jnp.exp(log_span * freq_index.astype(jnp.float32) / (GRID - 1))
    denominator = pole_rates[None, :] * pole_rates[None, :] + omega[:, None] * omega[:, None]
    real_side = pole_rates[None, :] / denominator
    imag_side = -omega[:, None] / denominator
    return jnp.stack([real_side, imag_side], axis=1)


def encode(value):
    return ((value * jnp.abs(value)) * (value * value)).astype(jnp.bfloat16)


def decode(code):
    code = code.astype(jnp.float32)
    inverse_root = lax.rsqrt(jnp.maximum(jnp.abs(code), least_code))
    return (code * inverse_root) * (inverse_root * lax.rsqrt(inverse_root))


def ring_order(slabs):
    return [0, *range(1, slabs, 2), *reversed(range(2, slabs, 2))]


def block_at(rank, step, slabs, flip):
    slab = lax.div(rank, 4)
    place = jnp.where(lax.rem(slab, 2) == 1, lax.div(slab + 1, 2), slabs - lax.div(slab, 2))
    place = lax.rem(place + (slabs - step), slabs)
    slab = jnp.where(place <= slabs // 2, 2 * place - 1, 2 * (slabs - place))
    slab = jnp.where(place == 0, 0, slab)
    return 4 * slab + (lax.rem(rank, 4) ^ flip)


def start_copies(rank_ref, measured_ref, first_half, slabs, halves, arrived):
    width = halves[0].shape[-1]
    copies = []
    for at, half in enumerate(halves):
        for core in range(2):
            place = 2 * (first_half + at) + core
            block = block_at(rank_ref[0], place // 4, slabs, place % 4)
            columns = pl.ds(pl.multiple_of(block * width, width), width)
            copy = pltpu.make_async_copy(
                measured_ref.at[:, :, :, columns], half.at[core], arrived.at[2 * at + core]
            )
            copy.start()
            copies.append(copy)
    return copies


def prepare_kernel(
    slabs,
    rank_ref,
    freq_hbm,
    quad_hbm,
    rates_hbm,
    factor_hbm,
    measured_ref,
    scaled_ref,
    turned_ref,
    pole_weight_ref,
    row_weight_ref,
    *refs,
):
    freq_ref, quad_ref, rates_ref, factor_ref, came, arrived = refs[-6:]
    pairs = ((freq_hbm, freq_ref), (quad_hbm, quad_ref), (rates_hbm, rates_ref), (factor_hbm, factor_ref))
    small = [pltpu.make_async_copy(*pair, came.at[at]) for at, pair in enumerate(pairs)]
    for copy in small:
        copy.start()
    copies = start_copies(rank_ref, measured_ref, 0, slabs, refs[:-6], arrived)
    for copy in small:
        copy.wait()
    rates = rates_ref[...]
    factor = factor_ref[...].astype(jnp.float32)
    turned_ref[...] = factor.T.astype(jnp.bfloat16)
    rows = factor.shape[0]
    lanes = pole_weight_ref.shape[2]
    for freq_slot in range(freq_ref.shape[0]):
        index = jnp.full(rates.shape, freq_ref[freq_slot], jnp.int32).astype(jnp.float32)
        weight = jnp.full(rates.shape, quad_ref[freq_slot], jnp.int32).astype(jnp.float32) * 0.25
        omega = low_freq * jnp.exp(log_span * index / (GRID - 1))
        denominator = rates * rates + omega * omega
        for comp_slot, coefficient in enumerate((rates / denominator, -omega / denominator)):
            term = 2 * freq_slot + comp_slot
            scaled_ref[pl.ds(term * rows, rows), :] = (factor * coefficient).astype(jnp.bfloat16)
            weighted = weight * coefficient
            row_weight_ref[term] = weighted
            pole_weight_ref[term] = jnp.broadcast_to(weighted, (lanes, weighted.shape[1])).T
    for copy in copies:
        copy.wait()


def prepare_by_kernel(
    rank, slabs, freq_index, quad_codes, pole_rates, out_factor, measured, width, lanes, halves
):
    rows, poles = out_factor.shape
    terms = 2 * freq_index.shape[0]
    vmem = pl.BlockSpec(memory_space=pltpu.VMEM)
    smem = pl.BlockSpec(memory_space=pltpu.SMEM)
    anywhere = pl.BlockSpec(memory_space=pl.ANY)
    operands = (freq_index, quad_codes, pole_rates[None, :], out_factor, measured)
    made = pl.pallas_call(
        functools.partial(prepare_kernel, slabs),
        in_specs=[smem] + [anywhere] * 5,
        out_specs=[vmem] * (4 + halves),
        out_shape=[
            jax.ShapeDtypeStruct((terms * rows, poles), jnp.bfloat16),
            jax.ShapeDtypeStruct((poles, rows), jnp.bfloat16),
            jax.ShapeDtypeStruct((terms, poles, lanes), jnp.float32),
            jax.ShapeDtypeStruct((terms, 1, poles), jnp.float32),
        ]
        + [jax.ShapeDtypeStruct((2, *measured.shape[:3], width), jnp.bfloat16)] * halves,
        scratch_shapes=[
            pltpu.SMEM(freq_index.shape, jnp.int32),
            pltpu.SMEM(quad_codes.shape, jnp.int32),
            pltpu.VMEM((1, poles), jnp.float32),
            pltpu.VMEM((rows, poles), jnp.bfloat16),
            pltpu.SemaphoreType.DMA((4,)),
            pltpu.SemaphoreType.DMA((2 * halves,)),
        ],
        compiler_params=pltpu.CompilerParams(vmem_limit_bytes=16 * 1024 * 1024),
        cost_estimate=pl.CostEstimate(
            flops=0, bytes_accessed=halves * measured.size // slabs, transcendentals=0
        ),
        name="prepare",
    )(rank, *[pltpu.with_memory_space_constraint(array, pltpu.HBM) for array in operands])
    return made[:4], list(made[4:])


def half_kernel(
    factor_0, factor_1, scaled_ref, turned_ref, pole_weight_ref, seen_ref, *refs
):
    keep_ref, send_ref, residual_ref, held_ref = refs[-4:]
    width = factor_0.shape[1]
    rows = turned_ref.shape[1]
    terms = pole_weight_ref.shape[0]
    for core, factor_ref in enumerate((factor_0, factor_1)):
        factor = factor_ref[...]
        held_ref[core] = factor
        model = jnp.dot(scaled_ref[...], factor, preferred_element_type=jnp.float32)
        seen = seen_ref[core].reshape(terms * rows, width).astype(jnp.float32)
        residual = (model - seen).astype(jnp.bfloat16)
        residual_ref[core] = residual.reshape(residual_ref.shape[1:])
        partial = None
        for term in range(terms):
            part = jnp.dot(
                turned_ref[...],
                residual[term * rows : (term + 1) * rows],
                preferred_element_type=jnp.float32,
            )
            weight = pole_weight_ref[term]
            weight = jnp.concatenate([weight] * (width // weight.shape[1]), axis=1)
            partial = weight * part if partial is None else partial + weight * part
        if core == 0:
            keep_ref[...] = partial
        elif len(refs) > 4:
            send_ref[0] = refs[0][...]
            send_ref[1] = encode(partial)
        else:
            send_ref[...] = encode(partial)


def half_by_kernel(factors, constants, seen, near_send):
    scaled, turned, pole_weight, _ = constants
    poles, width = factors[0].shape
    rows = turned.shape[1]
    terms = pole_weight.shape[0]
    half = len(factors) * width
    flops = 2 * 2 * terms * rows * poles * half
    vmem = pl.BlockSpec(memory_space=pltpu.VMEM)
    beside = [] if near_send is None else [near_send]
    return pl.pallas_call(
        half_kernel,
        in_specs=[vmem] * (6 + len(beside)),
        out_specs=[vmem] * 4,
        out_shape=[
            jax.ShapeDtypeStruct((poles, width), jnp.float32),
            jax.ShapeDtypeStruct((2, poles, width) if beside else (poles, width), jnp.bfloat16),
            jax.ShapeDtypeStruct(seen.shape, seen.dtype),
            jax.ShapeDtypeStruct((2, poles, width), jnp.bfloat16),
        ],
        input_output_aliases={5: 2},
        compiler_params=pltpu.CompilerParams(vmem_limit_bytes=16 * 1024 * 1024),
        cost_estimate=pl.CostEstimate(
            flops=10 * flops, bytes_accessed=2 * terms * rows * half, transcendentals=0
        ),
        name="far" if beside else "near",
    )(*factors, scaled, turned, pole_weight, seen, *beside)


def update_kernel(halves, scale, *refs):
    row_weight_ref, *refs, total_ref = refs
    terms = row_weight_ref.shape[0]
    rows, width = refs[0].shape[-2:]
    total = None
    for at in range(halves):
        residual_ref, held_ref = refs[2 * at : 2 * at + 2]
        for core in range(2):
            part = lax.dot_general(
                residual_ref[core].reshape(terms * rows, width),
                held_ref[core],
                (((1,), (1,)), ((), ())),
                preferred_element_type=jnp.float32,
            )
            total = part if total is None else total + part
    update = refs[2 * halves][...] if len(refs) > 2 * halves else 0.0
    for term in range(terms):
        update = update + row_weight_ref[term] * total[term * rows : (term + 1) * rows]
    total_ref[...] = update if scale is None else update * scale


def update_by_kernel(halves, row_weight, update, scale=None):
    poles, width = halves[0][1].shape[1:]
    rows = halves[0][0].shape[-2]
    terms = row_weight.shape[0]
    flops = 4 * len(halves) * terms * rows * poles * width
    vmem = pl.BlockSpec(memory_space=pltpu.VMEM)
    operands = [row_weight, *[array for half in halves for array in half]]
    operands += [] if update is None else [update]
    return pl.pallas_call(
        functools.partial(update_kernel, len(halves), scale),
        in_specs=[vmem] * len(operands),
        out_specs=vmem,
        out_shape=jax.ShapeDtypeStruct((rows, poles), jnp.float32),
        compiler_params=pltpu.CompilerParams(vmem_limit_bytes=16 * 1024 * 1024),
        cost_estimate=pl.CostEstimate(
            flops=20 * flops, bytes_accessed=2 * terms * rows * width, transcendentals=0
        ),
        name="update",
    )(*operands)


def slice_by_ops(rank, slabs, measured, width, first_half, last_half):
    blocks = [
        lax.dynamic_slice_in_dim(
            measured, block_at(rank[0], at // 4, slabs, at % 4) * width, width, 3
        )
        for at in range(2 * first_half, 2 * last_half)
    ]
    return [jnp.stack(blocks[at : at + 2]) for at in range(0, len(blocks), 2)]


def prepare_by_ops(
    rank, slabs, freq_index, quad_codes, pole_rates, out_factor, measured, width, lanes, halves
):
    rows, poles = out_factor.shape
    coefficients = pole_terms(freq_index, pole_rates)
    weights = quad_codes.astype(jnp.float32) * 0.25
    weighted = (weights[:, None, None] * coefficients).reshape(-1, poles)
    scaled = (
        out_factor.astype(jnp.float32)[None, None, :, :] * coefficients[:, :, None, :]
    ).astype(jnp.bfloat16)
    pole_weight = jnp.broadcast_to(weighted[:, :, None], (weighted.shape[0], poles, lanes))
    seen = slice_by_ops(rank, slabs, measured, width, 0, halves)
    constants = [scaled.reshape(-1, poles), out_factor.T, pole_weight, weighted[:, None, :]]
    return constants, seen


def half_by_ops(factors, constants, seen, near_send):
    scaled, turned, pole_weight, _ = constants
    width = factors[0].shape[1]
    rows = turned.shape[1]
    terms = pole_weight.shape[0]
    partials, residuals = [], []
    for core, factor in enumerate(factors):
        model = jnp.dot(scaled, factor, preferred_element_type=jnp.float32)
        residual = model - seen[core].reshape(terms * rows, width).astype(jnp.float32)
        residual = residual.astype(jnp.bfloat16)
        residuals.append(residual.reshape(seen.shape[1:]))
        partial = jnp.einsum(
            "ki,tij->tkj",
            turned,
            residual.reshape(terms, rows, width),
            preferred_element_type=jnp.float32,
        )
        partials.append(jnp.sum(pole_weight[:, :, :1] * partial, axis=0))
    send = encode(partials[1])
    if near_send is not None:
        send = jnp.stack([near_send, send])
    return partials[0], send, jnp.stack(residuals), jnp.stack(factors)


def update_by_ops(halves, row_weight, update, scale=None):
    rows, width = halves[0][0].shape[-2:]
    terms = row_weight.shape[0]
    total = sum(
        jnp.einsum(
            "tij,kj->tik",
            residual[core].reshape(terms, rows, width),
            held[core],
            preferred_element_type=jnp.float32,
        )
        for residual, held in halves
        for core in range(2)
    )
    part = jnp.sum(row_weight * total, axis=0)
    total = part if update is None else update + part
    return total if scale is None else total * scale


def after(value, earlier):
    return lax.optimization_barrier((value, *earlier))[0]


def on_device(measured, out_factor, in_factor, pole_rates, freq_index, quad_codes):
    rows, total_in = measured.shape[2:]
    poles, width = in_factor.shape
    ranks = lax.axis_size("port")
    rank = lax.axis_index("port").astype(jnp.int32).reshape(1)
    slabs = ranks // 4
    total_out = rows * ranks
    tiled = width % 128 == 0 and rows % 128 == 0
    prepare = prepare_by_kernel if tiled else prepare_by_ops
    one_half = half_by_kernel if tiled else half_by_ops
    add_update = update_by_kernel if tiled else update_by_ops

    def to_core(block):
        return lax.ppermute(block, "port", [(i, i ^ 1) for i in range(ranks)])

    def to_side(block):
        return lax.ppermute(block, "port", [(i, i ^ 2) for i in range(ranks)])

    ring = ring_order(slabs)
    place = {slab: at for at, slab in enumerate(ring)}

    def along(block, hops):
        pairs = [
            (i, 4 * ring[(place[i // 4] + hops) % slabs] + i % 4) for i in range(ranks)
        ]
        return lax.ppermute(block, "port", pairs)

    near = in_factor
    coming_near = along(near, 1)
    coming_far = to_side(near)
    near_pair = [near, to_core(near)]
    constants, seen = prepare(
        rank,
        slabs,
        freq_index,
        quad_codes,
        pole_rates,
        out_factor,
        measured,
        width,
        min(width, 128),
        2 * slabs,
    )
    nears = [None] * slabs
    keeps = [None] * slabs
    sends = [None] * slabs
    codes = [None] * slabs
    from_sides = [None] * slabs
    halves = []

    def near_half(step, pair, token):
        keep, sends[step], *parts = one_half(pair, constants, after(seen[2 * step], token), None)
        halves.append(parts)
        keeps[step] = [keep]
        return [parts[0]]

    def far_half(step, pair, token):
        keep, sends[step], *parts = one_half(
            pair, constants, after(seen[2 * step + 1], token), sends[step]
        )
        halves.append(parts)
        keeps[step].append(keep)
        return [parts[0]]

    def collect(step, token):
        received = decode(after(to_core(sends[step]), token))
        nears[step] = keeps[step][0] + received[0]
        codes[step] = encode(keeps[step][1] + received[1])
        return [*token, codes[step]]

    def pass_on(step, arriving, token):
        total = nears[step] + decode(after(from_sides[step], token))
        if arriving is not None:
            total = total + decode(after(arriving, token))
        return encode(total)

    arriving = None
    from_next = None
    update = None
    row_weight = constants[3]
    token = near_half(0, near_pair, [row_weight])
    for step in range(slabs):
        if step + 1 < slabs:
            near = after(coming_near, token)
            token = [*token, near]
            if step + 2 < slabs:
                coming_near = along(near, 1)
        far = after(coming_far, token)
        if step + 1 < slabs:
            if step + 2 == slabs:
                coming_far = along(far, 1)
            elif step > 0:
                coming_far = to_side(near)
            near_pair = [near, to_core(near)]
        if step > 0:
            update = add_update([halves[step - 1]], after(row_weight, [*token, far]), update)
            token = [*token, update]
        if step + 1 == slabs and slabs > 2:
            code = pass_on(1, None, token)
            from_next = along(code, -1)
            token = [*token, code]
        token = far_half(step, [far, to_core(far)], token)
        if step == 0 and slabs > 2:
            coming_far = to_side(after(near, token))
        if step + 1 < slabs:
            token = near_half(step + 1, near_pair, token)
        else:
            update = add_update([halves[step]], after(row_weight, token), update)
            token = [update]
        token = collect(step, token)
        if step > 0:
            from_sides[step] = to_side(codes[step])
        if step > 2:
            code = pass_on(step - 1, arriving, token)
            arriving = along(code, 1)
            token = [*token, code]

    if slabs > 1:
        middle = slabs + slabs // 2
        update = add_update(halves[slabs:middle], after(row_weight, token), update)
        code = pass_on(slabs - 1, arriving, [update])
        arriving = along(code, 1)
        token = [update, code]
    from_sides[0] = to_side(after(codes[0], token))
    if slabs > 1:
        grad_out = add_update(
            halves[middle:], after(row_weight, token), update, 1.0 / math.sqrt(total_in)
        )
    else:
        grad_out = update * (1.0 / math.sqrt(total_in))
    total = nears[0] + decode(after(from_sides[0], [grad_out]))
    for sums in (from_next, arriving):
        if sums is not None:
            total = total + decode(after(sums, [grad_out]))

    grad_in_t = (total * (1.0 / math.sqrt(total_out))).T
    return (grad_out, grad_in_t)


def solution(mesh):
    in_specs = (
        P("groups", None, "port", None),
        P("port", "groups"),
        P("groups", "port"),
        P("groups"),
        P("groups"),
        P("groups"),
    )
    out_specs = (P("port", "groups"), P("port", "groups"))
    return jax.shard_map(
        on_device, mesh=mesh, in_specs=in_specs, out_specs=out_specs, check_vma=False
    )
```

```python
import functools
import math

import jax
import jax.numpy as jnp
from jax import lax
from jax.experimental import pallas as pl
from jax.experimental.pallas import tpu as pltpu
from jax.sharding import PartitionSpec as P

GRID = 1024


low_freq = 0.1
log_span = math.log(100.0)
least_code = 1e-36


def pole_terms(freq_index, pole_rates):
    omega = low_freq * jnp.exp(log_span * freq_index.astype(jnp.float32) / (GRID - 1))
    denominator = pole_rates[None, :] * pole_rates[None, :] + omega[:, None] * omega[:, None]
    real_side = pole_rates[None, :] / denominator
    imag_side = -omega[:, None] / denominator
    return jnp.stack([real_side, imag_side], axis=1)


def encode(value):
    return ((value * jnp.abs(value)) * (value * value)).astype(jnp.bfloat16)


def decode(code):
    code = code.astype(jnp.float32)
    inverse_root = lax.rsqrt(jnp.maximum(jnp.abs(code), least_code))
    return (code * inverse_root) * (inverse_root * lax.rsqrt(inverse_root))


def ring_order(slabs):
    return [0, *range(1, slabs, 2), *reversed(range(2, slabs, 2))]


def block_at(rank, step, slabs, flip):
    slab = lax.div(rank, 4)
    place = jnp.where(lax.rem(slab, 2) == 1, lax.div(slab + 1, 2), slabs - lax.div(slab, 2))
    place = lax.rem(place + (slabs - step), slabs)
    slab = jnp.where(place <= slabs // 2, 2 * place - 1, 2 * (slabs - place))
    slab = jnp.where(place == 0, 0, slab)
    return 4 * slab + (lax.rem(rank, 4) ^ flip)


def start_copies(rank_ref, measured_ref, first_half, slabs, halves, arrived):
    width = halves[0].shape[-1]
    copies = []
    for at, half in enumerate(halves):
        for core in range(2):
            place = 2 * (first_half + at) + core
            block = block_at(rank_ref[0], place // 4, slabs, place % 4)
            columns = pl.ds(pl.multiple_of(block * width, width), width)
            copy = pltpu.make_async_copy(
                measured_ref.at[:, :, :, columns], half.at[core], arrived.at[2 * at + core]
            )
            copy.start()
            copies.append(copy)
    return copies


def prepare_kernel(
    slabs,
    rank_ref,
    freq_hbm,
    quad_hbm,
    rates_hbm,
    factor_hbm,
    measured_ref,
    scaled_ref,
    turned_ref,
    pole_weight_ref,
    row_weight_ref,
    *refs,
):
    freq_ref, quad_ref, rates_ref, factor_ref, came, arrived = refs[-6:]
    pairs = ((freq_hbm, freq_ref), (quad_hbm, quad_ref), (rates_hbm, rates_ref), (factor_hbm, factor_ref))
    small = [pltpu.make_async_copy(*pair, came.at[at]) for at, pair in enumerate(pairs)]
    for copy in small:
        copy.start()
    copies = start_copies(rank_ref, measured_ref, 0, slabs, refs[:-6], arrived)
    for copy in small:
        copy.wait()
    rates = rates_ref[...]
    factor = factor_ref[...].astype(jnp.float32)
    turned_ref[...] = factor.T.astype(jnp.bfloat16)
    rows = factor.shape[0]
    lanes = pole_weight_ref.shape[2]
    for freq_slot in range(freq_ref.shape[0]):
        index = jnp.full(rates.shape, freq_ref[freq_slot], jnp.int32).astype(jnp.float32)
        weight = jnp.full(rates.shape, quad_ref[freq_slot], jnp.int32).astype(jnp.float32) * 0.25
        omega = low_freq * jnp.exp(log_span * index / (GRID - 1))
        denominator = rates * rates + omega * omega
        for comp_slot, coefficient in enumerate((rates / denominator, -omega / denominator)):
            term = 2 * freq_slot + comp_slot
            scaled_ref[pl.ds(term * rows, rows), :] = (factor * coefficient).astype(jnp.bfloat16)
            weighted = weight * coefficient
            row_weight_ref[term] = weighted
            pole_weight_ref[term] = jnp.broadcast_to(weighted, (lanes, weighted.shape[1])).T
    for copy in copies:
        copy.wait()


def prepare_by_kernel(
    rank, slabs, freq_index, quad_codes, pole_rates, out_factor, measured, width, lanes, halves
):
    rows, poles = out_factor.shape
    terms = 2 * freq_index.shape[0]
    vmem = pl.BlockSpec(memory_space=pltpu.VMEM)
    smem = pl.BlockSpec(memory_space=pltpu.SMEM)
    anywhere = pl.BlockSpec(memory_space=pl.ANY)
    operands = (freq_index, quad_codes, pole_rates[None, :], out_factor, measured)
    made = pl.pallas_call(
        functools.partial(prepare_kernel, slabs),
        in_specs=[smem] + [anywhere] * 5,
        out_specs=[vmem] * (4 + halves),
        out_shape=[
            jax.ShapeDtypeStruct((terms * rows, poles), jnp.bfloat16),
            jax.ShapeDtypeStruct((poles, rows), jnp.bfloat16),
            jax.ShapeDtypeStruct((terms, poles, lanes), jnp.float32),
            jax.ShapeDtypeStruct((terms, 1, poles), jnp.float32),
        ]
        + [jax.ShapeDtypeStruct((2, *measured.shape[:3], width), jnp.bfloat16)] * halves,
        scratch_shapes=[
            pltpu.SMEM(freq_index.shape, jnp.int32),
            pltpu.SMEM(quad_codes.shape, jnp.int32),
            pltpu.VMEM((1, poles), jnp.float32),
            pltpu.VMEM((rows, poles), jnp.bfloat16),
            pltpu.SemaphoreType.DMA((4,)),
            pltpu.SemaphoreType.DMA((2 * halves,)),
        ],
        compiler_params=pltpu.CompilerParams(vmem_limit_bytes=16 * 1024 * 1024),
        cost_estimate=pl.CostEstimate(
            flops=0, bytes_accessed=halves * measured.size // slabs, transcendentals=0
        ),
        name="prepare",
    )(rank, *[pltpu.with_memory_space_constraint(array, pltpu.HBM) for array in operands])
    return made[:4], list(made[4:])


def half_kernel(
    factor_0, factor_1, scaled_ref, turned_ref, pole_weight_ref, seen_ref, *refs
):
    keep_ref, send_ref, residual_ref, held_ref = refs[-4:]
    width = factor_0.shape[1]
    rows = turned_ref.shape[1]
    terms = pole_weight_ref.shape[0]
    for core, factor_ref in enumerate((factor_0, factor_1)):
        factor = factor_ref[...]
        held_ref[core] = factor
        model = jnp.dot(scaled_ref[...], factor, preferred_element_type=jnp.float32)
        seen = seen_ref[core].reshape(terms * rows, width).astype(jnp.float32)
        residual = (model - seen).astype(jnp.bfloat16)
        residual_ref[core] = residual.reshape(residual_ref.shape[1:])
        partial = None
        for term in range(terms):
            part = jnp.dot(
                turned_ref[...],
                residual[term * rows : (term + 1) * rows],
                preferred_element_type=jnp.float32,
            )
            weight = pole_weight_ref[term]
            weight = jnp.concatenate([weight] * (width // weight.shape[1]), axis=1)
            partial = weight * part if partial is None else partial + weight * part
        if core == 0:
            keep_ref[...] = partial
        elif len(refs) > 4:
            send_ref[0] = refs[0][...]
            send_ref[1] = encode(partial)
        else:
            send_ref[...] = encode(partial)


def half_by_kernel(factors, constants, seen, near_send):
    scaled, turned, pole_weight, _ = constants
    poles, width = factors[0].shape
    rows = turned.shape[1]
    terms = pole_weight.shape[0]
    half = len(factors) * width
    flops = 2 * 2 * terms * rows * poles * half
    vmem = pl.BlockSpec(memory_space=pltpu.VMEM)
    beside = [] if near_send is None else [near_send]
    return pl.pallas_call(
        half_kernel,
        in_specs=[vmem] * (6 + len(beside)),
        out_specs=[vmem] * 4,
        out_shape=[
            jax.ShapeDtypeStruct((poles, width), jnp.float32),
            jax.ShapeDtypeStruct((2, poles, width) if beside else (poles, width), jnp.bfloat16),
            jax.ShapeDtypeStruct(seen.shape, seen.dtype),
            jax.ShapeDtypeStruct((2, poles, width), jnp.bfloat16),
        ],
        input_output_aliases={5: 2},
        compiler_params=pltpu.CompilerParams(vmem_limit_bytes=16 * 1024 * 1024),
        cost_estimate=pl.CostEstimate(
            flops=10 * flops, bytes_accessed=2 * terms * rows * half, transcendentals=0
        ),
        name="far" if beside else "near",
    )(*factors, scaled, turned, pole_weight, seen, *beside)


def update_kernel(halves, scale, *refs):
    row_weight_ref, *refs, total_ref = refs
    terms = row_weight_ref.shape[0]
    rows, width = refs[0].shape[-2:]
    total = None
    for at in range(halves):
        residual_ref, held_ref = refs[2 * at : 2 * at + 2]
        for core in range(2):
            part = lax.dot_general(
                residual_ref[core].reshape(terms * rows, width),
                held_ref[core],
                (((1,), (1,)), ((), ())),
                preferred_element_type=jnp.float32,
            )
            total = part if total is None else total + part
    update = refs[2 * halves][...] if len(refs) > 2 * halves else 0.0
    for term in range(terms):
        update = update + row_weight_ref[term] * total[term * rows : (term + 1) * rows]
    total_ref[...] = update if scale is None else update * scale


def update_by_kernel(halves, row_weight, update, scale=None):
    poles, width = halves[0][1].shape[1:]
    rows = halves[0][0].shape[-2]
    terms = row_weight.shape[0]
    flops = 4 * len(halves) * terms * rows * poles * width
    vmem = pl.BlockSpec(memory_space=pltpu.VMEM)
    operands = [row_weight, *[array for half in halves for array in half]]
    operands += [] if update is None else [update]
    return pl.pallas_call(
        functools.partial(update_kernel, len(halves), scale),
        in_specs=[vmem] * len(operands),
        out_specs=vmem,
        out_shape=jax.ShapeDtypeStruct((rows, poles), jnp.float32),
        compiler_params=pltpu.CompilerParams(vmem_limit_bytes=16 * 1024 * 1024),
        cost_estimate=pl.CostEstimate(
            flops=20 * flops, bytes_accessed=2 * terms * rows * width, transcendentals=0
        ),
        name="update",
    )(*operands)


def slice_by_ops(rank, slabs, measured, width, first_half, last_half):
    blocks = [
        lax.dynamic_slice_in_dim(
            measured, block_at(rank[0], at // 4, slabs, at % 4) * width, width, 3
        )
        for at in range(2 * first_half, 2 * last_half)
    ]
    return [jnp.stack(blocks[at : at + 2]) for at in range(0, len(blocks), 2)]


def prepare_by_ops(
    rank, slabs, freq_index, quad_codes, pole_rates, out_factor, measured, width, lanes, halves
):
    rows, poles = out_factor.shape
    coefficients = pole_terms(freq_index, pole_rates)
    weights = quad_codes.astype(jnp.float32) * 0.25
    weighted = (weights[:, None, None] * coefficients).reshape(-1, poles)
    scaled = (
        out_factor.astype(jnp.float32)[None, None, :, :] * coefficients[:, :, None, :]
    ).astype(jnp.bfloat16)
    pole_weight = jnp.broadcast_to(weighted[:, :, None], (weighted.shape[0], poles, lanes))
    seen = slice_by_ops(rank, slabs, measured, width, 0, halves)
    constants = [scaled.reshape(-1, poles), out_factor.T, pole_weight, weighted[:, None, :]]
    return constants, seen


def half_by_ops(factors, constants, seen, near_send):
    scaled, turned, pole_weight, _ = constants
    width = factors[0].shape[1]
    rows = turned.shape[1]
    terms = pole_weight.shape[0]
    partials, residuals = [], []
    for core, factor in enumerate(factors):
        model = jnp.dot(scaled, factor, preferred_element_type=jnp.float32)
        residual = model - seen[core].reshape(terms * rows, width).astype(jnp.float32)
        residual = residual.astype(jnp.bfloat16)
        residuals.append(residual.reshape(seen.shape[1:]))
        partial = jnp.einsum(
            "ki,tij->tkj",
            turned,
            residual.reshape(terms, rows, width),
            preferred_element_type=jnp.float32,
        )
        partials.append(jnp.sum(pole_weight[:, :, :1] * partial, axis=0))
    send = encode(partials[1])
    if near_send is not None:
        send = jnp.stack([near_send, send])
    return partials[0], send, jnp.stack(residuals), jnp.stack(factors)


def update_by_ops(halves, row_weight, update, scale=None):
    rows, width = halves[0][0].shape[-2:]
    terms = row_weight.shape[0]
    total = sum(
        jnp.einsum(
            "tij,kj->tik",
            residual[core].reshape(terms, rows, width),
            held[core],
            preferred_element_type=jnp.float32,
        )
        for residual, held in halves
        for core in range(2)
    )
    part = jnp.sum(row_weight * total, axis=0)
    total = part if update is None else update + part
    return total if scale is None else total * scale


def after(value, earlier):
    return lax.optimization_barrier((value, *earlier))[0]


def on_device(measured, out_factor, in_factor, pole_rates, freq_index, quad_codes):
    rows, total_in = measured.shape[2:]
    poles, width = in_factor.shape
    ranks = lax.axis_size("port")
    rank = lax.axis_index("port").astype(jnp.int32).reshape(1)
    slabs = ranks // 4
    total_out = rows * ranks
    tiled = width % 128 == 0 and rows % 128 == 0
    prepare = prepare_by_kernel if tiled else prepare_by_ops
    one_half = half_by_kernel if tiled else half_by_ops
    add_update = update_by_kernel if tiled else update_by_ops

    def to_core(block):
        return lax.ppermute(block, "port", [(i, i ^ 1) for i in range(ranks)])

    def to_side(block):
        return lax.ppermute(block, "port", [(i, i ^ 2) for i in range(ranks)])

    ring = ring_order(slabs)
    place = {slab: at for at, slab in enumerate(ring)}

    def along(block, hops):
        pairs = [
            (i, 4 * ring[(place[i // 4] + hops) % slabs] + i % 4) for i in range(ranks)
        ]
        return lax.ppermute(block, "port", pairs)

    near = in_factor
    coming_near = along(near, 1)
    coming_far = to_side(near)
    near_pair = [near, to_core(near)]
    constants, seen = prepare(
        rank,
        slabs,
        freq_index,
        quad_codes,
        pole_rates,
        out_factor,
        measured,
        width,
        min(width, 128),
        2 * slabs,
    )
    nears = [None] * slabs
    keeps = [None] * slabs
    sends = [None] * slabs
    codes = [None] * slabs
    from_sides = [None] * slabs
    halves = []

    def near_half(step, pair, token):
        keep, sends[step], *parts = one_half(pair, constants, after(seen[2 * step], token), None)
        halves.append(parts)
        keeps[step] = [keep]
        return [parts[0]]

    def far_half(step, pair, token):
        keep, sends[step], *parts = one_half(
            pair, constants, after(seen[2 * step + 1], token), sends[step]
        )
        halves.append(parts)
        keeps[step].append(keep)
        return [parts[0]]

    def collect(step, token):
        received = decode(after(to_core(sends[step]), token))
        nears[step] = keeps[step][0] + received[0]
        codes[step] = encode(keeps[step][1] + received[1])
        return [*token, codes[step]]

    def pass_on(step, arriving, token):
        total = nears[step] + decode(after(from_sides[step], token))
        if arriving is not None:
            total = total + decode(after(arriving, token))
        return encode(total)

    arriving = None
    from_next = None
    update = None
    row_weight = constants[3]
    token = near_half(0, near_pair, [row_weight])
    for step in range(slabs):
        if step > 1:
            update = add_update([halves[step - 1]], after(row_weight, token), update)
            token = [*token, update]
        if step + 1 < slabs:
            near = after(coming_near, token)
            token = [*token, near]
            if step + 2 < slabs:
                coming_near = along(near, 1)
        far = after(coming_far, token[:-1] if step == 1 and step + 1 < slabs else token)
        if step + 1 < slabs:
            if step + 2 == slabs:
                coming_far = along(far, 1)
            elif step > 0:
                coming_far = to_side(near)
            near_pair = [near, to_core(near)]
        if step == 1:
            update = add_update([halves[0]], after(row_weight, [*token, far]), update)
            token = [*token, update]
        if step + 1 == slabs and slabs > 2:
            code = pass_on(1, None, token)
            from_next = along(code, -1)
            token = [*token, code]
        far_pair = [far, to_core(far)]
        if step == 0 and slabs > 2:
            coming_far = to_side(after(near, [far]))
        token = far_half(step, far_pair, token)
        if step + 1 < slabs:
            token = near_half(step + 1, near_pair, token)
        else:
            update = add_update([halves[step]], after(row_weight, token), update)
            token = [update]
        token = collect(step, token)
        if step > 0:
            from_sides[step] = to_side(codes[step])
        if step > 2:
            code = pass_on(step - 1, arriving, token)
            arriving = along(code, 1)
            token = [*token, code]

    if slabs > 1:
        middle = slabs + slabs // 2
        update = add_update(halves[slabs:middle], after(row_weight, token), update)
        code = pass_on(slabs - 1, arriving, [update])
        arriving = along(code, 1)
        token = [update, code]
    from_sides[0] = to_side(after(codes[0], token))
    if slabs > 1:
        grad_out = add_update(
            halves[middle:], after(row_weight, token), update, 1.0 / math.sqrt(total_in)
        )
    else:
        grad_out = update * (1.0 / math.sqrt(total_in))
    total = nears[0] + decode(after(from_sides[0], [grad_out]))
    for sums in (from_next, arriving):
        if sums is not None:
            total = total + decode(after(sums, [grad_out]))

    grad_in_t = (total * (1.0 / math.sqrt(total_out))).T
    return (grad_out, grad_in_t)


def solution(mesh):
    in_specs = (
        P("groups", None, "port", None),
        P("port", "groups"),
        P("groups", "port"),
        P("groups"),
        P("groups"),
        P("groups"),
    )
    out_specs = (P("port", "groups"), P("port", "groups"))
    return jax.shard_map(
        on_device, mesh=mesh, in_specs=in_specs, out_specs=out_specs, check_vma=False
    )
```

```python
import functools
import math

import jax
import jax.numpy as jnp
from jax import lax
from jax.experimental import pallas as pl
from jax.experimental.pallas import tpu as pltpu
from jax.sharding import PartitionSpec as P

GRID = 1024


low_freq = 0.1
log_span = math.log(100.0)
least_code = 1e-36


def pole_terms(freq_index, pole_rates):
    omega = low_freq * jnp.exp(log_span * freq_index.astype(jnp.float32) / (GRID - 1))
    denominator = pole_rates[None, :] * pole_rates[None, :] + omega[:, None] * omega[:, None]
    real_side = pole_rates[None, :] / denominator
    imag_side = -omega[:, None] / denominator
    return jnp.stack([real_side, imag_side], axis=1)


def encode(value):
    return ((value * jnp.abs(value)) * (value * value)).astype(jnp.bfloat16)


def decode(code):
    code = code.astype(jnp.float32)
    inverse_root = lax.rsqrt(jnp.maximum(jnp.abs(code), least_code))
    return (code * inverse_root) * (inverse_root * lax.rsqrt(inverse_root))


def ring_order(slabs):
    return [0, *range(1, slabs, 2), *reversed(range(2, slabs, 2))]


def block_at(rank, step, slabs, flip):
    slab = lax.div(rank, 4)
    place = jnp.where(lax.rem(slab, 2) == 1, lax.div(slab + 1, 2), slabs - lax.div(slab, 2))
    place = lax.rem(place + (slabs - step), slabs)
    slab = jnp.where(place <= slabs // 2, 2 * place - 1, 2 * (slabs - place))
    slab = jnp.where(place == 0, 0, slab)
    return 4 * slab + (lax.rem(rank, 4) ^ flip)


def start_copies(rank_ref, measured_ref, first_half, slabs, halves, arrived):
    width = halves[0].shape[-1]
    copies = []
    for at, half in enumerate(halves):
        for core in range(2):
            place = 2 * (first_half + at) + core
            block = block_at(rank_ref[0], place // 4, slabs, place % 4)
            columns = pl.ds(pl.multiple_of(block * width, width), width)
            copy = pltpu.make_async_copy(
                measured_ref.at[:, :, :, columns], half.at[core], arrived.at[2 * at + core]
            )
            copy.start()
            copies.append(copy)
    return copies


def prepare_kernel(
    slabs,
    rank_ref,
    freq_hbm,
    quad_hbm,
    rates_hbm,
    factor_hbm,
    measured_ref,
    scaled_ref,
    turned_ref,
    pole_weight_ref,
    row_weight_ref,
    *refs,
):
    freq_ref, quad_ref, rates_ref, factor_ref, came, arrived = refs[-6:]
    pairs = ((freq_hbm, freq_ref), (quad_hbm, quad_ref), (rates_hbm, rates_ref), (factor_hbm, factor_ref))
    small = [pltpu.make_async_copy(*pair, came.at[at]) for at, pair in enumerate(pairs)]
    for copy in small:
        copy.start()
    copies = start_copies(rank_ref, measured_ref, 0, slabs, refs[:-6], arrived)
    for copy in small:
        copy.wait()
    rates = rates_ref[...]
    factor = factor_ref[...].astype(jnp.float32)
    turned_ref[...] = factor.T.astype(jnp.bfloat16)
    rows = factor.shape[0]
    lanes = pole_weight_ref.shape[2]
    for freq_slot in range(freq_ref.shape[0]):
        index = jnp.full(rates.shape, freq_ref[freq_slot], jnp.int32).astype(jnp.float32)
        weight = jnp.full(rates.shape, quad_ref[freq_slot], jnp.int32).astype(jnp.float32) * 0.25
        omega = low_freq * jnp.exp(log_span * index / (GRID - 1))
        denominator = rates * rates + omega * omega
        for comp_slot, coefficient in enumerate((rates / denominator, -omega / denominator)):
            term = 2 * freq_slot + comp_slot
            scaled_ref[pl.ds(term * rows, rows), :] = (factor * coefficient).astype(jnp.bfloat16)
            weighted = weight * coefficient
            row_weight_ref[term] = weighted
            pole_weight_ref[term] = jnp.broadcast_to(weighted, (lanes, weighted.shape[1])).T
    for copy in copies:
        copy.wait()


def prepare_by_kernel(
    rank, slabs, freq_index, quad_codes, pole_rates, out_factor, measured, width, lanes, halves
):
    rows, poles = out_factor.shape
    terms = 2 * freq_index.shape[0]
    vmem = pl.BlockSpec(memory_space=pltpu.VMEM)
    smem = pl.BlockSpec(memory_space=pltpu.SMEM)
    anywhere = pl.BlockSpec(memory_space=pl.ANY)
    operands = (freq_index, quad_codes, pole_rates[None, :], out_factor, measured)
    made = pl.pallas_call(
        functools.partial(prepare_kernel, slabs),
        in_specs=[smem] + [anywhere] * 5,
        out_specs=[vmem] * (4 + halves),
        out_shape=[
            jax.ShapeDtypeStruct((terms * rows, poles), jnp.bfloat16),
            jax.ShapeDtypeStruct((poles, rows), jnp.bfloat16),
            jax.ShapeDtypeStruct((terms, poles, lanes), jnp.float32),
            jax.ShapeDtypeStruct((terms, 1, poles), jnp.float32),
        ]
        + [jax.ShapeDtypeStruct((2, *measured.shape[:3], width), jnp.bfloat16)] * halves,
        scratch_shapes=[
            pltpu.SMEM(freq_index.shape, jnp.int32),
            pltpu.SMEM(quad_codes.shape, jnp.int32),
            pltpu.VMEM((1, poles), jnp.float32),
            pltpu.VMEM((rows, poles), jnp.bfloat16),
            pltpu.SemaphoreType.DMA((4,)),
            pltpu.SemaphoreType.DMA((2 * halves,)),
        ],
        compiler_params=pltpu.CompilerParams(vmem_limit_bytes=16 * 1024 * 1024),
        cost_estimate=pl.CostEstimate(
            flops=0, bytes_accessed=halves * measured.size // slabs, transcendentals=0
        ),
        name="prepare",
    )(rank, *[pltpu.with_memory_space_constraint(array, pltpu.HBM) for array in operands])
    return made[:4], list(made[4:])


def half_kernel(
    factor_0, factor_1, scaled_ref, turned_ref, pole_weight_ref, seen_ref, *refs
):
    keep_ref, send_ref, residual_ref, held_ref = refs[-4:]
    width = factor_0.shape[1]
    rows = turned_ref.shape[1]
    terms = pole_weight_ref.shape[0]
    models = []
    for core, factor_ref in enumerate((factor_0, factor_1)):
        factor = factor_ref[...]
        held_ref[core] = factor
        models.append(jnp.dot(scaled_ref[...], factor, preferred_element_type=jnp.float32))
    residuals = []
    for core, model in enumerate(models):
        seen = seen_ref[core].reshape(terms * rows, width).astype(jnp.float32)
        residual = (model - seen).astype(jnp.bfloat16)
        residual_ref[core] = residual.reshape(residual_ref.shape[1:])
        residuals.append(residual)
    partials = [None, None]
    for term in range(terms):
        weight = pole_weight_ref[term]
        weight = jnp.concatenate([weight] * (width // weight.shape[1]), axis=1)
        for core, residual in enumerate(residuals):
            part = weight * jnp.dot(
                turned_ref[...],
                residual[term * rows : (term + 1) * rows],
                preferred_element_type=jnp.float32,
            )
            partials[core] = part if term == 0 else partials[core] + part
    keep_ref[...] = partials[0]
    if len(refs) > 4:
        send_ref[0] = refs[0][...]
        send_ref[1] = encode(partials[1])
    else:
        send_ref[...] = encode(partials[1])


def half_by_kernel(factors, constants, seen, near_send):
    scaled, turned, pole_weight, _ = constants
    poles, width = factors[0].shape
    rows = turned.shape[1]
    terms = pole_weight.shape[0]
    half = len(factors) * width
    flops = 2 * 2 * terms * rows * poles * half
    vmem = pl.BlockSpec(memory_space=pltpu.VMEM)
    beside = [] if near_send is None else [near_send]
    return pl.pallas_call(
        half_kernel,
        in_specs=[vmem] * (6 + len(beside)),
        out_specs=[vmem] * 4,
        out_shape=[
            jax.ShapeDtypeStruct((poles, width), jnp.float32),
            jax.ShapeDtypeStruct((2, poles, width) if beside else (poles, width), jnp.bfloat16),
            jax.ShapeDtypeStruct(seen.shape, seen.dtype),
            jax.ShapeDtypeStruct((2, poles, width), jnp.bfloat16),
        ],
        input_output_aliases={5: 2},
        compiler_params=pltpu.CompilerParams(vmem_limit_bytes=16 * 1024 * 1024),
        cost_estimate=pl.CostEstimate(
            flops=10 * flops, bytes_accessed=2 * terms * rows * half, transcendentals=0
        ),
        name="far" if beside else "near",
    )(*factors, scaled, turned, pole_weight, seen, *beside)


def update_kernel(halves, scale, *refs):
    row_weight_ref, *refs, total_ref = refs
    terms = row_weight_ref.shape[0]
    rows, width = refs[0].shape[-2:]
    total = None
    for at in range(halves):
        residual_ref, held_ref = refs[2 * at : 2 * at + 2]
        for core in range(2):
            part = lax.dot_general(
                residual_ref[core].reshape(terms * rows, width),
                held_ref[core],
                (((1,), (1,)), ((), ())),
                preferred_element_type=jnp.float32,
            )
            total = part if total is None else total + part
    update = refs[2 * halves][...] if len(refs) > 2 * halves else 0.0
    for term in range(terms):
        update = update + row_weight_ref[term] * total[term * rows : (term + 1) * rows]
    total_ref[...] = update if scale is None else update * scale


def update_by_kernel(halves, row_weight, update, scale=None):
    poles, width = halves[0][1].shape[1:]
    rows = halves[0][0].shape[-2]
    terms = row_weight.shape[0]
    flops = 4 * len(halves) * terms * rows * poles * width
    vmem = pl.BlockSpec(memory_space=pltpu.VMEM)
    operands = [row_weight, *[array for half in halves for array in half]]
    operands += [] if update is None else [update]
    return pl.pallas_call(
        functools.partial(update_kernel, len(halves), scale),
        in_specs=[vmem] * len(operands),
        out_specs=vmem,
        out_shape=jax.ShapeDtypeStruct((rows, poles), jnp.float32),
        compiler_params=pltpu.CompilerParams(vmem_limit_bytes=16 * 1024 * 1024),
        cost_estimate=pl.CostEstimate(
            flops=20 * flops, bytes_accessed=2 * terms * rows * width, transcendentals=0
        ),
        name="update",
    )(*operands)


def slice_by_ops(rank, slabs, measured, width, first_half, last_half):
    blocks = [
        lax.dynamic_slice_in_dim(
            measured, block_at(rank[0], at // 4, slabs, at % 4) * width, width, 3
        )
        for at in range(2 * first_half, 2 * last_half)
    ]
    return [jnp.stack(blocks[at : at + 2]) for at in range(0, len(blocks), 2)]


def finish_kernel(scale, near_ref, *refs):
    total = near_ref[...]
    for code_ref in refs[:-1]:
        total = total + decode(code_ref[...])
    refs[-1][...] = (total * scale).T


def finish_by_kernel(near, codes, scale):
    poles, width = near.shape
    vmem = pl.BlockSpec(memory_space=pltpu.VMEM)
    return pl.pallas_call(
        functools.partial(finish_kernel, scale),
        in_specs=[vmem] * (1 + len(codes)),
        out_specs=vmem,
        out_shape=jax.ShapeDtypeStruct((width, poles), jnp.float32),
        compiler_params=pltpu.CompilerParams(vmem_limit_bytes=16 * 1024 * 1024),
        cost_estimate=pl.CostEstimate(
            flops=0, bytes_accessed=8 * poles * width, transcendentals=0
        ),
        name="finish",
    )(near, *codes)


def finish_by_ops(near, codes, scale):
    return (sum((decode(code) for code in codes), near) * scale).T


def prepare_by_ops(
    rank, slabs, freq_index, quad_codes, pole_rates, out_factor, measured, width, lanes, halves
):
    rows, poles = out_factor.shape
    coefficients = pole_terms(freq_index, pole_rates)
    weights = quad_codes.astype(jnp.float32) * 0.25
    weighted = (weights[:, None, None] * coefficients).reshape(-1, poles)
    scaled = (
        out_factor.astype(jnp.float32)[None, None, :, :] * coefficients[:, :, None, :]
    ).astype(jnp.bfloat16)
    pole_weight = jnp.broadcast_to(weighted[:, :, None], (weighted.shape[0], poles, lanes))
    seen = slice_by_ops(rank, slabs, measured, width, 0, halves)
    constants = [scaled.reshape(-1, poles), out_factor.T, pole_weight, weighted[:, None, :]]
    return constants, seen


def half_by_ops(factors, constants, seen, near_send):
    scaled, turned, pole_weight, _ = constants
    width = factors[0].shape[1]
    rows = turned.shape[1]
    terms = pole_weight.shape[0]
    partials, residuals = [], []
    for core, factor in enumerate(factors):
        model = jnp.dot(scaled, factor, preferred_element_type=jnp.float32)
        residual = model - seen[core].reshape(terms * rows, width).astype(jnp.float32)
        residual = residual.astype(jnp.bfloat16)
        residuals.append(residual.reshape(seen.shape[1:]))
        partial = jnp.einsum(
            "ki,tij->tkj",
            turned,
            residual.reshape(terms, rows, width),
            preferred_element_type=jnp.float32,
        )
        partials.append(jnp.sum(pole_weight[:, :, :1] * partial, axis=0))
    send = encode(partials[1])
    if near_send is not None:
        send = jnp.stack([near_send, send])
    return partials[0], send, jnp.stack(residuals), jnp.stack(factors)


def update_by_ops(halves, row_weight, update, scale=None):
    rows, width = halves[0][0].shape[-2:]
    terms = row_weight.shape[0]
    total = sum(
        jnp.einsum(
            "tij,kj->tik",
            residual[core].reshape(terms, rows, width),
            held[core],
            preferred_element_type=jnp.float32,
        )
        for residual, held in halves
        for core in range(2)
    )
    part = jnp.sum(row_weight * total, axis=0)
    total = part if update is None else update + part
    return total if scale is None else total * scale


def after(value, earlier):
    return lax.optimization_barrier((value, *earlier))[0]


def on_device(measured, out_factor, in_factor, pole_rates, freq_index, quad_codes):
    rows, total_in = measured.shape[2:]
    poles, width = in_factor.shape
    ranks = lax.axis_size("port")
    rank = lax.axis_index("port").astype(jnp.int32).reshape(1)
    slabs = ranks // 4
    total_out = rows * ranks
    tiled = width % 128 == 0 and rows % 128 == 0
    prepare = prepare_by_kernel if tiled else prepare_by_ops
    one_half = half_by_kernel if tiled else half_by_ops
    add_update = update_by_kernel if tiled else update_by_ops
    finish = finish_by_kernel if tiled else finish_by_ops

    def to_core(block):
        return lax.ppermute(block, "port", [(i, i ^ 1) for i in range(ranks)])

    def to_side(block):
        return lax.ppermute(block, "port", [(i, i ^ 2) for i in range(ranks)])

    ring = ring_order(slabs)
    place = {slab: at for at, slab in enumerate(ring)}

    def along(block, hops):
        pairs = [
            (i, 4 * ring[(place[i // 4] + hops) % slabs] + i % 4) for i in range(ranks)
        ]
        return lax.ppermute(block, "port", pairs)

    near = in_factor
    coming_near = along(near, 1)
    coming_far = to_side(near)
    near_pair = [near, to_core(near)]
    constants, seen = prepare(
        rank,
        slabs,
        freq_index,
        quad_codes,
        pole_rates,
        out_factor,
        measured,
        width,
        min(width, 128),
        2 * slabs,
    )
    nears = [None] * slabs
    keeps = [None] * slabs
    sends = [None] * slabs
    codes = [None] * slabs
    from_sides = [None] * slabs
    halves = []

    def near_half(step, pair, token):
        keep, sends[step], *parts = one_half(pair, constants, after(seen[2 * step], token), None)
        halves.append(parts)
        keeps[step] = [keep]
        return [parts[0]]

    def far_half(step, pair, token):
        keep, sends[step], *parts = one_half(
            pair, constants, after(seen[2 * step + 1], token), sends[step]
        )
        halves.append(parts)
        keeps[step].append(keep)
        return [parts[0]]

    def collect(step, token):
        received = decode(after(to_core(sends[step]), token))
        nears[step] = keeps[step][0] + received[0]
        codes[step] = encode(keeps[step][1] + received[1])
        return [*token, codes[step]]

    def pass_on(step, arriving, token):
        total = nears[step] + decode(after(from_sides[step], token))
        if arriving is not None:
            total = total + decode(after(arriving, token))
        return encode(total)

    arriving = None
    from_next = None
    update = None
    added = 0
    row_weight = constants[3]
    token = near_half(0, near_pair, [row_weight])
    for step in range(slabs):
        if step > 2:
            update = add_update([halves[added]], after(row_weight, token), update)
            added += 1
            token = [*token, update]
        if step + 1 < slabs:
            near = after(coming_near, token)
            token = [*token, near]
            if step + 2 < slabs:
                coming_near = along(near, 1)
        far = after(coming_far, token[:-1] if step == 1 and step + 1 < slabs else token)
        if step + 1 < slabs:
            if step + 2 == slabs:
                coming_far = along(far, 1)
            elif step > 0:
                coming_far = to_side(near)
            near_pair = [near, to_core(near)]
        if step == 1:
            update = add_update([halves[added]], after(row_weight, [*token, far]), update)
            added += 1
            token = [*token, update]
        if step + 1 == slabs and slabs > 2:
            code = pass_on(1, None, token)
            from_next = along(code, -1)
            token = [*token, code]
        far_pair = [far, to_core(far)]
        if step == 0 and slabs > 2:
            coming_far = to_side(after(near, [far]))
        token = far_half(step, far_pair, token)
        if step + 1 < slabs:
            token = near_half(step + 1, near_pair, token)
        else:
            update = add_update([halves[added]], after(row_weight, token), update)
            added += 1
            token = [update]
        token = collect(step, token)
        if step > 0:
            from_sides[step] = to_side(codes[step])
        if step > 2:
            code = pass_on(step - 1, arriving, token)
            arriving = along(code, 1)
            token = [*token, code]

    if slabs > 1:
        middle = (added + 2 * slabs + 1) // 2
        update = add_update(halves[added:middle], after(row_weight, token), update)
        code = pass_on(slabs - 1, arriving, [update])
        arriving = along(code, 1)
        token = [update, code]
    from_sides[0] = to_side(after(codes[0], token))
    if slabs > 1:
        grad_out = add_update(
            halves[middle:], after(row_weight, token), update, 1.0 / math.sqrt(total_in)
        )
    else:
        grad_out = add_update(halves[added:], row_weight, update, 1.0 / math.sqrt(total_in))
    last = [sums for sums in (from_sides[0], from_next, arriving) if sums is not None]
    last = [after(sums, [grad_out]) for sums in last]
    grad_in_t = finish(nears[0], last, 1.0 / math.sqrt(total_out))
    return (grad_out, grad_in_t)


def solution(mesh):
    in_specs = (
        P("groups", None, "port", None),
        P("port", "groups"),
        P("groups", "port"),
        P("groups"),
        P("groups"),
        P("groups"),
    )
    out_specs = (P("port", "groups"), P("port", "groups"))
    return jax.shard_map(
        on_device, mesh=mesh, in_specs=in_specs, out_specs=out_specs, check_vma=False
    )
```

```python
import functools
import math

import jax
import jax.numpy as jnp
from jax import lax
from jax.experimental import pallas as pl
from jax.experimental.pallas import tpu as pltpu
from jax.sharding import PartitionSpec as P

GRID = 1024


low_freq = 0.1
log_span = math.log(100.0)
least_code = 1e-36


def pole_terms(freq_index, pole_rates):
    omega = low_freq * jnp.exp(log_span * freq_index.astype(jnp.float32) / (GRID - 1))
    denominator = pole_rates[None, :] * pole_rates[None, :] + omega[:, None] * omega[:, None]
    real_side = pole_rates[None, :] / denominator
    imag_side = -omega[:, None] / denominator
    return jnp.stack([real_side, imag_side], axis=1)


def encode(value):
    return ((value * jnp.abs(value)) * (value * value)).astype(jnp.bfloat16)


def decode(code):
    code = code.astype(jnp.float32)
    inverse_root = lax.rsqrt(jnp.maximum(jnp.abs(code), least_code))
    return (code * inverse_root) * (inverse_root * lax.rsqrt(inverse_root))


def ring_order(slabs):
    return [0, *range(1, slabs, 2), *reversed(range(2, slabs, 2))]


def block_at(rank, step, slabs, flip):
    slab = lax.div(rank, 4)
    place = jnp.where(lax.rem(slab, 2) == 1, lax.div(slab + 1, 2), slabs - lax.div(slab, 2))
    place = lax.rem(place + (slabs - step), slabs)
    slab = jnp.where(place <= slabs // 2, 2 * place - 1, 2 * (slabs - place))
    slab = jnp.where(place == 0, 0, slab)
    return 4 * slab + (lax.rem(rank, 4) ^ flip)


def start_copies(rank_ref, measured_ref, first_half, slabs, halves, arrived):
    width = halves[0].shape[-1]
    copies = []
    for at, half in enumerate(halves):
        for core in range(2):
            place = 2 * (first_half + at) + core
            block = block_at(rank_ref[0], place // 4, slabs, place % 4)
            columns = pl.ds(pl.multiple_of(block * width, width), width)
            copy = pltpu.make_async_copy(
                measured_ref.at[:, :, :, columns], half.at[core], arrived.at[2 * at + core]
            )
            copy.start()
            copies.append(copy)
    return copies


def prepare_kernel(
    slabs,
    rank_ref,
    freq_hbm,
    quad_hbm,
    rates_hbm,
    factor_hbm,
    measured_ref,
    scaled_ref,
    turned_ref,
    pole_weight_ref,
    row_weight_ref,
    *refs,
):
    freq_ref, quad_ref, rates_ref, factor_ref, came, arrived = refs[-6:]
    pairs = ((freq_hbm, freq_ref), (quad_hbm, quad_ref), (rates_hbm, rates_ref), (factor_hbm, factor_ref))
    small = [pltpu.make_async_copy(*pair, came.at[at]) for at, pair in enumerate(pairs)]
    for copy in small:
        copy.start()
    copies = start_copies(rank_ref, measured_ref, 0, slabs, refs[:-6], arrived)
    for copy in small:
        copy.wait()
    rates = rates_ref[...]
    factor = factor_ref[...].astype(jnp.float32)
    turned_ref[...] = factor.T.astype(jnp.bfloat16)
    rows = factor.shape[0]
    lanes = pole_weight_ref.shape[2]
    for freq_slot in range(freq_ref.shape[0]):
        index = jnp.full(rates.shape, freq_ref[freq_slot], jnp.int32).astype(jnp.float32)
        weight = jnp.full(rates.shape, quad_ref[freq_slot], jnp.int32).astype(jnp.float32) * 0.25
        omega = low_freq * jnp.exp(log_span * index / (GRID - 1))
        denominator = rates * rates + omega * omega
        for comp_slot, coefficient in enumerate((rates / denominator, -omega / denominator)):
            term = 2 * freq_slot + comp_slot
            scaled_ref[pl.ds(term * rows, rows), :] = (factor * coefficient).astype(jnp.bfloat16)
            weighted = weight * coefficient
            row_weight_ref[term] = weighted
            pole_weight_ref[term] = jnp.broadcast_to(weighted, (lanes, weighted.shape[1])).T
    for copy in copies:
        copy.wait()


def prepare_by_kernel(
    rank, slabs, freq_index, quad_codes, pole_rates, out_factor, measured, width, lanes, halves
):
    rows, poles = out_factor.shape
    terms = 2 * freq_index.shape[0]
    vmem = pl.BlockSpec(memory_space=pltpu.VMEM)
    smem = pl.BlockSpec(memory_space=pltpu.SMEM)
    anywhere = pl.BlockSpec(memory_space=pl.ANY)
    operands = (freq_index, quad_codes, pole_rates[None, :], out_factor, measured)
    made = pl.pallas_call(
        functools.partial(prepare_kernel, slabs),
        in_specs=[smem] + [anywhere] * 5,
        out_specs=[vmem] * (4 + halves),
        out_shape=[
            jax.ShapeDtypeStruct((terms * rows, poles), jnp.bfloat16),
            jax.ShapeDtypeStruct((poles, rows), jnp.bfloat16),
            jax.ShapeDtypeStruct((terms, poles, lanes), jnp.float32),
            jax.ShapeDtypeStruct((terms, 1, poles), jnp.float32),
        ]
        + [jax.ShapeDtypeStruct((2, *measured.shape[:3], width), jnp.bfloat16)] * halves,
        scratch_shapes=[
            pltpu.SMEM(freq_index.shape, jnp.int32),
            pltpu.SMEM(quad_codes.shape, jnp.int32),
            pltpu.VMEM((1, poles), jnp.float32),
            pltpu.VMEM((rows, poles), jnp.bfloat16),
            pltpu.SemaphoreType.DMA((4,)),
            pltpu.SemaphoreType.DMA((2 * halves,)),
        ],
        compiler_params=pltpu.CompilerParams(vmem_limit_bytes=16 * 1024 * 1024),
        cost_estimate=pl.CostEstimate(
            flops=0, bytes_accessed=halves * measured.size // slabs, transcendentals=0
        ),
        name="prepare",
    )(rank, *[pltpu.with_memory_space_constraint(array, pltpu.HBM) for array in operands])
    return made[:4], list(made[4:])


def half_kernel(
    factor_0, factor_1, scaled_ref, turned_ref, pole_weight_ref, seen_ref, *refs
):
    keep_ref, send_ref, residual_ref, held_ref = refs[-4:]
    width = factor_0.shape[1]
    rows = turned_ref.shape[1]
    terms = pole_weight_ref.shape[0]
    models = []
    for core, factor_ref in enumerate((factor_0, factor_1)):
        factor = factor_ref[...]
        held_ref[core] = factor
        models.append(jnp.dot(scaled_ref[...], factor, preferred_element_type=jnp.float32))
    residuals = []
    for core, model in enumerate(models):
        seen = seen_ref[core].reshape(terms * rows, width).astype(jnp.float32)
        residual = (model - seen).astype(jnp.bfloat16)
        residual_ref[core] = residual.reshape(residual_ref.shape[1:])
        residuals.append(residual)
    partials = [None, None]
    for term in range(terms):
        weight = pole_weight_ref[term]
        weight = jnp.concatenate([weight] * (width // weight.shape[1]), axis=1)
        for core, residual in enumerate(residuals):
            part = weight * jnp.dot(
                turned_ref[...],
                residual[term * rows : (term + 1) * rows],
                preferred_element_type=jnp.float32,
            )
            partials[core] = part if term == 0 else partials[core] + part
    keep_ref[...] = partials[0]
    if len(refs) > 4:
        send_ref[0] = refs[0][...]
        send_ref[1] = encode(partials[1])
    else:
        send_ref[...] = encode(partials[1])


def half_by_kernel(factors, constants, seen, near_send):
    scaled, turned, pole_weight, _ = constants
    poles, width = factors[0].shape
    rows = turned.shape[1]
    terms = pole_weight.shape[0]
    half = len(factors) * width
    flops = 2 * 2 * terms * rows * poles * half
    vmem = pl.BlockSpec(memory_space=pltpu.VMEM)
    beside = [] if near_send is None else [near_send]
    return pl.pallas_call(
        half_kernel,
        in_specs=[vmem] * (6 + len(beside)),
        out_specs=[vmem] * 4,
        out_shape=[
            jax.ShapeDtypeStruct((poles, width), jnp.float32),
            jax.ShapeDtypeStruct((2, poles, width) if beside else (poles, width), jnp.bfloat16),
            jax.ShapeDtypeStruct(seen.shape, seen.dtype),
            jax.ShapeDtypeStruct((2, poles, width), jnp.bfloat16),
        ],
        input_output_aliases={5: 2},
        compiler_params=pltpu.CompilerParams(vmem_limit_bytes=16 * 1024 * 1024),
        cost_estimate=pl.CostEstimate(
            flops=10 * flops, bytes_accessed=2 * terms * rows * half, transcendentals=0
        ),
        name="far" if beside else "near",
    )(*factors, scaled, turned, pole_weight, seen, *beside)


def update_kernel(halves, scale, *refs):
    row_weight_ref, *refs, total_ref = refs
    terms = row_weight_ref.shape[0]
    rows, width = refs[0].shape[-2:]
    total = None
    for at in range(halves):
        residual_ref, held_ref = refs[2 * at : 2 * at + 2]
        for core in range(2):
            part = lax.dot_general(
                residual_ref[core].reshape(terms * rows, width),
                held_ref[core],
                (((1,), (1,)), ((), ())),
                preferred_element_type=jnp.float32,
            )
            total = part if total is None else total + part
    update = refs[2 * halves][...] if len(refs) > 2 * halves else 0.0
    for term in range(terms):
        update = update + row_weight_ref[term] * total[term * rows : (term + 1) * rows]
    total_ref[...] = update if scale is None else update * scale


def update_by_kernel(halves, row_weight, update, scale=None):
    poles, width = halves[0][1].shape[1:]
    rows = halves[0][0].shape[-2]
    terms = row_weight.shape[0]
    flops = 4 * len(halves) * terms * rows * poles * width
    vmem = pl.BlockSpec(memory_space=pltpu.VMEM)
    operands = [row_weight, *[array for half in halves for array in half]]
    operands += [] if update is None else [update]
    return pl.pallas_call(
        functools.partial(update_kernel, len(halves), scale),
        in_specs=[vmem] * len(operands),
        out_specs=vmem,
        out_shape=jax.ShapeDtypeStruct((rows, poles), jnp.float32),
        compiler_params=pltpu.CompilerParams(vmem_limit_bytes=16 * 1024 * 1024),
        cost_estimate=pl.CostEstimate(
            flops=20 * flops, bytes_accessed=2 * terms * rows * width, transcendentals=0
        ),
        name="update",
    )(*operands)


def slice_by_ops(rank, slabs, measured, width, first_half, last_half):
    blocks = [
        lax.dynamic_slice_in_dim(
            measured, block_at(rank[0], at // 4, slabs, at % 4) * width, width, 3
        )
        for at in range(2 * first_half, 2 * last_half)
    ]
    return [jnp.stack(blocks[at : at + 2]) for at in range(0, len(blocks), 2)]


def finish_kernel(scale, near_ref, *refs):
    total = near_ref[...]
    for code_ref in refs[:-1]:
        total = total + decode(code_ref[...])
    refs[-1][...] = (total * scale).T


def finish_by_kernel(near, codes, scale):
    poles, width = near.shape
    vmem = pl.BlockSpec(memory_space=pltpu.VMEM)
    return pl.pallas_call(
        functools.partial(finish_kernel, scale),
        in_specs=[vmem] * (1 + len(codes)),
        out_specs=vmem,
        out_shape=jax.ShapeDtypeStruct((width, poles), jnp.float32),
        compiler_params=pltpu.CompilerParams(vmem_limit_bytes=16 * 1024 * 1024),
        cost_estimate=pl.CostEstimate(
            flops=0, bytes_accessed=8 * poles * width, transcendentals=0
        ),
        name="finish",
    )(near, *codes)


def finish_by_ops(near, codes, scale):
    return (sum((decode(code) for code in codes), near) * scale).T


def prepare_by_ops(
    rank, slabs, freq_index, quad_codes, pole_rates, out_factor, measured, width, lanes, halves
):
    rows, poles = out_factor.shape
    coefficients = pole_terms(freq_index, pole_rates)
    weights = quad_codes.astype(jnp.float32) * 0.25
    weighted = (weights[:, None, None] * coefficients).reshape(-1, poles)
    scaled = (
        out_factor.astype(jnp.float32)[None, None, :, :] * coefficients[:, :, None, :]
    ).astype(jnp.bfloat16)
    pole_weight = jnp.broadcast_to(weighted[:, :, None], (weighted.shape[0], poles, lanes))
    seen = slice_by_ops(rank, slabs, measured, width, 0, halves)
    constants = [scaled.reshape(-1, poles), out_factor.T, pole_weight, weighted[:, None, :]]
    return constants, seen


def half_by_ops(factors, constants, seen, near_send):
    scaled, turned, pole_weight, _ = constants
    width = factors[0].shape[1]
    rows = turned.shape[1]
    terms = pole_weight.shape[0]
    partials, residuals = [], []
    for core, factor in enumerate(factors):
        model = jnp.dot(scaled, factor, preferred_element_type=jnp.float32)
        residual = model - seen[core].reshape(terms * rows, width).astype(jnp.float32)
        residual = residual.astype(jnp.bfloat16)
        residuals.append(residual.reshape(seen.shape[1:]))
        partial = jnp.einsum(
            "ki,tij->tkj",
            turned,
            residual.reshape(terms, rows, width),
            preferred_element_type=jnp.float32,
        )
        partials.append(jnp.sum(pole_weight[:, :, :1] * partial, axis=0))
    send = encode(partials[1])
    if near_send is not None:
        send = jnp.stack([near_send, send])
    return partials[0], send, jnp.stack(residuals), jnp.stack(factors)


def update_by_ops(halves, row_weight, update, scale=None):
    rows, width = halves[0][0].shape[-2:]
    terms = row_weight.shape[0]
    total = sum(
        jnp.einsum(
            "tij,kj->tik",
            residual[core].reshape(terms, rows, width),
            held[core],
            preferred_element_type=jnp.float32,
        )
        for residual, held in halves
        for core in range(2)
    )
    part = jnp.sum(row_weight * total, axis=0)
    total = part if update is None else update + part
    return total if scale is None else total * scale


def after(value, earlier):
    return lax.optimization_barrier((value, *earlier))[0]


def on_device(measured, out_factor, in_factor, pole_rates, freq_index, quad_codes):
    rows, total_in = measured.shape[2:]
    poles, width = in_factor.shape
    ranks = lax.axis_size("port")
    rank = lax.axis_index("port").astype(jnp.int32).reshape(1)
    slabs = ranks // 4
    total_out = rows * ranks
    tiled = width % 128 == 0 and rows % 128 == 0
    prepare = prepare_by_kernel if tiled else prepare_by_ops
    one_half = half_by_kernel if tiled else half_by_ops
    add_update = update_by_kernel if tiled else update_by_ops
    finish = finish_by_kernel if tiled else finish_by_ops

    def to_core(block):
        return lax.ppermute(block, "port", [(i, i ^ 1) for i in range(ranks)])

    def to_side(block):
        return lax.ppermute(block, "port", [(i, i ^ 2) for i in range(ranks)])

    ring = ring_order(slabs)
    place = {slab: at for at, slab in enumerate(ring)}

    def along(block, hops):
        pairs = [
            (i, 4 * ring[(place[i // 4] + hops) % slabs] + i % 4) for i in range(ranks)
        ]
        return lax.ppermute(block, "port", pairs)

    near = in_factor
    coming_near = along(near, 1)
    coming_far = to_side(near)
    near_pair = [near, to_core(near)]
    constants, seen = prepare(
        rank,
        slabs,
        freq_index,
        quad_codes,
        pole_rates,
        out_factor,
        measured,
        width,
        min(width, 128),
        2 * slabs,
    )
    nears = [None] * slabs
    keeps = [None] * slabs
    sends = [None] * slabs
    codes = [None] * slabs
    from_sides = [None] * slabs
    halves = []

    def near_half(step, pair, token):
        keep, sends[step], *parts = one_half(pair, constants, after(seen[2 * step], token), None)
        halves.append(parts)
        keeps[step] = [keep]
        return [parts[0]]

    def far_half(step, pair, token):
        keep, sends[step], *parts = one_half(
            pair, constants, after(seen[2 * step + 1], token), sends[step]
        )
        halves.append(parts)
        keeps[step].append(keep)
        return [parts[0]]

    def collect(step, token):
        received = decode(after(to_core(sends[step]), token))
        nears[step] = keeps[step][0] + received[0]
        codes[step] = encode(keeps[step][1] + received[1])
        return [*token, codes[step]]

    def pass_on(step, arriving, token):
        total = nears[step] + decode(after(from_sides[step], token))
        if arriving is not None:
            total = total + decode(after(arriving, token))
        return encode(total)

    arriving = None
    from_next = None
    update = None
    added = 0
    row_weight = constants[3]
    token = near_half(0, near_pair, [row_weight])
    for step in range(slabs):
        if step > 2:
            update = add_update([halves[added]], after(row_weight, token), update)
            added += 1
            token = [*token, update]
        if step + 1 < slabs:
            near = after(coming_near, token)
            token = [*token, near]
            if step + 2 < slabs and step != 1:
                coming_near = along(near, 1)
        far = after(coming_far, token[:-1] if 0 < step < slabs - 1 else token)
        if step + 2 < slabs and step == 1:
            coming_near = along(after(near, [far]), 1)
        if step + 1 < slabs:
            if step + 2 == slabs:
                coming_far = along(far, 1)
            elif step > 0:
                coming_far = to_side(near)
            near_pair = [near, to_core(near)]
        if step == 1:
            update = add_update([halves[added]], after(row_weight, [*token, far]), update)
            added += 1
            token = [*token, update]
        if step + 1 == slabs and slabs > 2:
            code = pass_on(1, None, token)
            from_next = along(code, -1)
            token = [*token, code]
        far_pair = [far, to_core(far)]
        if step == 0 and slabs > 2:
            coming_far = to_side(after(near, [far]))
        token = far_half(step, far_pair, token)
        if step + 1 < slabs:
            token = near_half(step + 1, near_pair, token)
        else:
            update = add_update([halves[added]], after(row_weight, token), update)
            added += 1
            token = [update]
        token = collect(step, token)
        if step > 0:
            from_sides[step] = to_side(codes[step])
        if step > 2:
            code = pass_on(step - 1, arriving, token)
            arriving = along(code, 1)
            token = [*token, code]

    if slabs > 1:
        middle = (added + 2 * slabs + 1) // 2
        update = add_update(halves[added:middle], after(row_weight, token), update)
        code = pass_on(slabs - 1, arriving, [update])
        arriving = along(code, 1)
        token = [update, code]
    from_sides[0] = to_side(after(codes[0], token))
    if slabs > 1:
        grad_out = add_update(
            halves[middle:], after(row_weight, token), update, 1.0 / math.sqrt(total_in)
        )
    else:
        grad_out = add_update(halves[added:], row_weight, update, 1.0 / math.sqrt(total_in))
    last = [sums for sums in (from_sides[0], from_next, arriving) if sums is not None]
    last = [after(sums, [grad_out]) for sums in last]
    grad_in_t = finish(nears[0], last, 1.0 / math.sqrt(total_out))
    return (grad_out, grad_in_t)


def solution(mesh):
    in_specs = (
        P("groups", None, "port", None),
        P("port", "groups"),
        P("groups", "port"),
        P("groups"),
        P("groups"),
        P("groups"),
    )
    out_specs = (P("port", "groups"), P("port", "groups"))
    return jax.shard_map(
        on_device, mesh=mesh, in_specs=in_specs, out_specs=out_specs, check_vma=False
    )
```

```python
import functools
import math

import jax
import jax.numpy as jnp
from jax import lax
from jax.experimental import pallas as pl
from jax.experimental.pallas import tpu as pltpu
from jax.sharding import PartitionSpec as P

GRID = 1024


low_freq = 0.1
log_span = math.log(100.0)
least_code = 1e-36


def pole_terms(freq_index, pole_rates):
    omega = low_freq * jnp.exp(log_span * freq_index.astype(jnp.float32) / (GRID - 1))
    denominator = pole_rates[None, :] * pole_rates[None, :] + omega[:, None] * omega[:, None]
    real_side = pole_rates[None, :] / denominator
    imag_side = -omega[:, None] / denominator
    return jnp.stack([real_side, imag_side], axis=1)


def encode(value):
    return ((value * jnp.abs(value)) * (value * value)).astype(jnp.bfloat16)


def decode(code):
    code = code.astype(jnp.float32)
    inverse_root = lax.rsqrt(jnp.maximum(jnp.abs(code), least_code))
    return (code * inverse_root) * (inverse_root * lax.rsqrt(inverse_root))


def ring_order(slabs):
    return [0, *range(1, slabs, 2), *reversed(range(2, slabs, 2))]


def block_at(rank, step, slabs, flip):
    slab = lax.div(rank, 4)
    place = jnp.where(lax.rem(slab, 2) == 1, lax.div(slab + 1, 2), slabs - lax.div(slab, 2))
    place = lax.rem(place + (slabs - step), slabs)
    slab = jnp.where(place <= slabs // 2, 2 * place - 1, 2 * (slabs - place))
    slab = jnp.where(place == 0, 0, slab)
    return 4 * slab + (lax.rem(rank, 4) ^ flip)


def start_copies(rank_ref, measured_ref, first_half, slabs, halves, arrived):
    width = halves[0].shape[-1]
    copies = []
    for at, half in enumerate(halves):
        for core in range(2):
            place = 2 * (first_half + at) + core
            block = block_at(rank_ref[0], place // 4, slabs, place % 4)
            columns = pl.ds(pl.multiple_of(block * width, width), width)
            copy = pltpu.make_async_copy(
                measured_ref.at[:, :, :, columns], half.at[core], arrived.at[2 * at + core]
            )
            copy.start()
            copies.append(copy)
    return copies


def prepare_kernel(
    slabs,
    rank_ref,
    freq_hbm,
    quad_hbm,
    rates_hbm,
    factor_hbm,
    measured_ref,
    scaled_ref,
    turned_ref,
    pole_weight_ref,
    row_weight_ref,
    *refs,
):
    freq_ref, quad_ref, rates_ref, factor_ref, came, arrived = refs[-6:]
    pairs = ((freq_hbm, freq_ref), (quad_hbm, quad_ref), (rates_hbm, rates_ref), (factor_hbm, factor_ref))
    small = [pltpu.make_async_copy(*pair, came.at[at]) for at, pair in enumerate(pairs)]
    for copy in small:
        copy.start()
    copies = start_copies(rank_ref, measured_ref, 0, slabs, refs[:-6], arrived)
    for copy in small:
        copy.wait()
    rates = rates_ref[...]
    factor = factor_ref[...].astype(jnp.float32)
    turned_ref[...] = factor.T.astype(jnp.bfloat16)
    rows = factor.shape[0]
    lanes = pole_weight_ref.shape[2]
    for freq_slot in range(freq_ref.shape[0]):
        index = jnp.full(rates.shape, freq_ref[freq_slot], jnp.int32).astype(jnp.float32)
        weight = jnp.full(rates.shape, quad_ref[freq_slot], jnp.int32).astype(jnp.float32) * 0.25
        omega = low_freq * jnp.exp(log_span * index / (GRID - 1))
        denominator = rates * rates + omega * omega
        for comp_slot, coefficient in enumerate((rates / denominator, -omega / denominator)):
            term = 2 * freq_slot + comp_slot
            scaled_ref[pl.ds(term * rows, rows), :] = (factor * coefficient).astype(jnp.bfloat16)
            weighted = weight * coefficient
            row_weight_ref[term] = weighted
            pole_weight_ref[term] = jnp.broadcast_to(weighted, (lanes, weighted.shape[1])).T
    for copy in copies:
        copy.wait()


def prepare_by_kernel(
    rank, slabs, freq_index, quad_codes, pole_rates, out_factor, measured, width, lanes, halves
):
    rows, poles = out_factor.shape
    terms = 2 * freq_index.shape[0]
    vmem = pl.BlockSpec(memory_space=pltpu.VMEM)
    smem = pl.BlockSpec(memory_space=pltpu.SMEM)
    anywhere = pl.BlockSpec(memory_space=pl.ANY)
    operands = (freq_index, quad_codes, pole_rates[None, :], out_factor, measured)
    made = pl.pallas_call(
        functools.partial(prepare_kernel, slabs),
        in_specs=[smem] + [anywhere] * 5,
        out_specs=[vmem] * (4 + halves),
        out_shape=[
            jax.ShapeDtypeStruct((terms * rows, poles), jnp.bfloat16),
            jax.ShapeDtypeStruct((poles, rows), jnp.bfloat16),
            jax.ShapeDtypeStruct((terms, poles, lanes), jnp.float32),
            jax.ShapeDtypeStruct((terms, 1, poles), jnp.float32),
        ]
        + [jax.ShapeDtypeStruct((2, *measured.shape[:3], width), jnp.bfloat16)] * halves,
        scratch_shapes=[
            pltpu.SMEM(freq_index.shape, jnp.int32),
            pltpu.SMEM(quad_codes.shape, jnp.int32),
            pltpu.VMEM((1, poles), jnp.float32),
            pltpu.VMEM((rows, poles), jnp.bfloat16),
            pltpu.SemaphoreType.DMA((4,)),
            pltpu.SemaphoreType.DMA((2 * halves,)),
        ],
        compiler_params=pltpu.CompilerParams(vmem_limit_bytes=16 * 1024 * 1024),
        cost_estimate=pl.CostEstimate(
            flops=0, bytes_accessed=halves * measured.size // slabs, transcendentals=0
        ),
        name="prepare",
    )(rank, *[pltpu.with_memory_space_constraint(array, pltpu.HBM) for array in operands])
    return made[:4], list(made[4:])


def half_kernel(
    factor_0, factor_1, scaled_ref, turned_ref, pole_weight_ref, seen_ref, *refs
):
    keep_ref, send_ref, residual_ref, held_ref = refs[-4:]
    width = factor_0.shape[1]
    rows = turned_ref.shape[1]
    terms = pole_weight_ref.shape[0]
    models = []
    for core, factor_ref in enumerate((factor_0, factor_1)):
        factor = factor_ref[...]
        held_ref[core] = factor
        models.append(jnp.dot(scaled_ref[...], factor, preferred_element_type=jnp.float32))
    residuals = []
    for core, model in enumerate(models):
        seen = seen_ref[core].reshape(terms * rows, width).astype(jnp.float32)
        residual = (model - seen).astype(jnp.bfloat16)
        residual_ref[core] = residual.reshape(residual_ref.shape[1:])
        residuals.append(residual)
    partials = [None, None]
    for term in range(terms):
        weight = pole_weight_ref[term]
        weight = jnp.concatenate([weight] * (width // weight.shape[1]), axis=1)
        for core, residual in enumerate(residuals):
            part = weight * jnp.dot(
                turned_ref[...],
                residual[term * rows : (term + 1) * rows],
                preferred_element_type=jnp.float32,
            )
            partials[core] = part if term == 0 else partials[core] + part
    keep_ref[...] = partials[0]
    if len(refs) > 4:
        send_ref[0] = refs[0][...]
        send_ref[1] = encode(partials[1])
    else:
        send_ref[...] = encode(partials[1])


def half_by_kernel(factors, constants, seen, near_send):
    scaled, turned, pole_weight, _ = constants
    poles, width = factors[0].shape
    rows = turned.shape[1]
    terms = pole_weight.shape[0]
    half = len(factors) * width
    flops = 2 * 2 * terms * rows * poles * half
    vmem = pl.BlockSpec(memory_space=pltpu.VMEM)
    beside = [] if near_send is None else [near_send]
    return pl.pallas_call(
        half_kernel,
        in_specs=[vmem] * (6 + len(beside)),
        out_specs=[vmem] * 4,
        out_shape=[
            jax.ShapeDtypeStruct((poles, width), jnp.float32),
            jax.ShapeDtypeStruct((2, poles, width) if beside else (poles, width), jnp.bfloat16),
            jax.ShapeDtypeStruct(seen.shape, seen.dtype),
            jax.ShapeDtypeStruct((2, poles, width), jnp.bfloat16),
        ],
        input_output_aliases={5: 2},
        compiler_params=pltpu.CompilerParams(vmem_limit_bytes=16 * 1024 * 1024),
        cost_estimate=pl.CostEstimate(
            flops=10 * flops, bytes_accessed=2 * terms * rows * half, transcendentals=0
        ),
        name="far" if beside else "near",
    )(*factors, scaled, turned, pole_weight, seen, *beside)


def update_kernel(halves, scale, *refs):
    row_weight_ref, *refs, total_ref = refs
    terms = row_weight_ref.shape[0]
    rows, width = refs[0].shape[-2:]
    total = None
    for at in range(halves):
        residual_ref, held_ref = refs[2 * at : 2 * at + 2]
        for core in range(2):
            part = lax.dot_general(
                residual_ref[core].reshape(terms * rows, width),
                held_ref[core],
                (((1,), (1,)), ((), ())),
                preferred_element_type=jnp.float32,
            )
            total = part if total is None else total + part
    update = refs[2 * halves][...] if len(refs) > 2 * halves else 0.0
    for term in range(terms):
        update = update + row_weight_ref[term] * total[term * rows : (term + 1) * rows]
    total_ref[...] = update if scale is None else update * scale


def update_by_kernel(halves, row_weight, update, scale=None):
    poles, width = halves[0][1].shape[1:]
    rows = halves[0][0].shape[-2]
    terms = row_weight.shape[0]
    flops = 4 * len(halves) * terms * rows * poles * width
    vmem = pl.BlockSpec(memory_space=pltpu.VMEM)
    operands = [row_weight, *[array for half in halves for array in half]]
    operands += [] if update is None else [update]
    return pl.pallas_call(
        functools.partial(update_kernel, len(halves), scale),
        in_specs=[vmem] * len(operands),
        out_specs=vmem,
        out_shape=jax.ShapeDtypeStruct((rows, poles), jnp.float32),
        compiler_params=pltpu.CompilerParams(vmem_limit_bytes=16 * 1024 * 1024),
        cost_estimate=pl.CostEstimate(
            flops=20 * flops, bytes_accessed=2 * terms * rows * width, transcendentals=0
        ),
        name="update",
    )(*operands)


def slice_by_ops(rank, slabs, measured, width, first_half, last_half):
    blocks = [
        lax.dynamic_slice_in_dim(
            measured, block_at(rank[0], at // 4, slabs, at % 4) * width, width, 3
        )
        for at in range(2 * first_half, 2 * last_half)
    ]
    return [jnp.stack(blocks[at : at + 2]) for at in range(0, len(blocks), 2)]


def finish_kernel(scale, near_ref, *refs):
    total = near_ref[...]
    for code_ref in refs[:-1]:
        total = total + decode(code_ref[...])
    refs[-1][...] = (total * scale).T


def finish_by_kernel(near, codes, scale):
    poles, width = near.shape
    vmem = pl.BlockSpec(memory_space=pltpu.VMEM)
    return pl.pallas_call(
        functools.partial(finish_kernel, scale),
        in_specs=[vmem] * (1 + len(codes)),
        out_specs=vmem,
        out_shape=jax.ShapeDtypeStruct((width, poles), jnp.float32),
        compiler_params=pltpu.CompilerParams(vmem_limit_bytes=16 * 1024 * 1024),
        cost_estimate=pl.CostEstimate(
            flops=0, bytes_accessed=8 * poles * width, transcendentals=0
        ),
        name="finish",
    )(near, *codes)


def finish_by_ops(near, codes, scale):
    return (sum((decode(code) for code in codes), near) * scale).T


def prepare_by_ops(
    rank, slabs, freq_index, quad_codes, pole_rates, out_factor, measured, width, lanes, halves
):
    rows, poles = out_factor.shape
    coefficients = pole_terms(freq_index, pole_rates)
    weights = quad_codes.astype(jnp.float32) * 0.25
    weighted = (weights[:, None, None] * coefficients).reshape(-1, poles)
    scaled = (
        out_factor.astype(jnp.float32)[None, None, :, :] * coefficients[:, :, None, :]
    ).astype(jnp.bfloat16)
    pole_weight = jnp.broadcast_to(weighted[:, :, None], (weighted.shape[0], poles, lanes))
    seen = slice_by_ops(rank, slabs, measured, width, 0, halves)
    constants = [scaled.reshape(-1, poles), out_factor.T, pole_weight, weighted[:, None, :]]
    return constants, seen


def half_by_ops(factors, constants, seen, near_send):
    scaled, turned, pole_weight, _ = constants
    width = factors[0].shape[1]
    rows = turned.shape[1]
    terms = pole_weight.shape[0]
    partials, residuals = [], []
    for core, factor in enumerate(factors):
        model = jnp.dot(scaled, factor, preferred_element_type=jnp.float32)
        residual = model - seen[core].reshape(terms * rows, width).astype(jnp.float32)
        residual = residual.astype(jnp.bfloat16)
        residuals.append(residual.reshape(seen.shape[1:]))
        partial = jnp.einsum(
            "ki,tij->tkj",
            turned,
            residual.reshape(terms, rows, width),
            preferred_element_type=jnp.float32,
        )
        partials.append(jnp.sum(pole_weight[:, :, :1] * partial, axis=0))
    send = encode(partials[1])
    if near_send is not None:
        send = jnp.stack([near_send, send])
    return partials[0], send, jnp.stack(residuals), jnp.stack(factors)


def update_by_ops(halves, row_weight, update, scale=None):
    rows, width = halves[0][0].shape[-2:]
    terms = row_weight.shape[0]
    total = sum(
        jnp.einsum(
            "tij,kj->tik",
            residual[core].reshape(terms, rows, width),
            held[core],
            preferred_element_type=jnp.float32,
        )
        for residual, held in halves
        for core in range(2)
    )
    part = jnp.sum(row_weight * total, axis=0)
    total = part if update is None else update + part
    return total if scale is None else total * scale


def after(value, earlier):
    return lax.optimization_barrier((value, *earlier))[0]


def on_device(measured, out_factor, in_factor, pole_rates, freq_index, quad_codes):
    rows, total_in = measured.shape[2:]
    poles, width = in_factor.shape
    ranks = lax.axis_size("port")
    rank = lax.axis_index("port").astype(jnp.int32).reshape(1)
    slabs = ranks // 4
    total_out = rows * ranks
    tiled = width % 128 == 0 and rows % 128 == 0
    prepare = prepare_by_kernel if tiled else prepare_by_ops
    one_half = half_by_kernel if tiled else half_by_ops
    add_update = update_by_kernel if tiled else update_by_ops
    finish = finish_by_kernel if tiled else finish_by_ops

    def to_core(block):
        return lax.ppermute(block, "port", [(i, i ^ 1) for i in range(ranks)])

    def to_side(block):
        return lax.ppermute(block, "port", [(i, i ^ 2) for i in range(ranks)])

    ring = ring_order(slabs)
    place = {slab: at for at, slab in enumerate(ring)}

    def along(block, hops):
        pairs = [
            (i, 4 * ring[(place[i // 4] + hops) % slabs] + i % 4) for i in range(ranks)
        ]
        return lax.ppermute(block, "port", pairs)

    near = in_factor
    coming_near = along(near, 1)
    coming_far = to_side(near)
    near_pair = [near, to_core(near)]
    constants, seen = prepare(
        rank,
        slabs,
        freq_index,
        quad_codes,
        pole_rates,
        out_factor,
        measured,
        width,
        min(width, 128),
        2 * slabs,
    )
    nears = [None] * slabs
    keeps = [None] * slabs
    sends = [None] * slabs
    codes = [None] * slabs
    from_sides = [None] * slabs
    halves = []

    def near_half(step, pair, token):
        keep, sends[step], *parts = one_half(pair, constants, after(seen[2 * step], token), None)
        halves.append(parts)
        keeps[step] = [keep]
        return [parts[0]]

    def far_half(step, pair, token):
        keep, sends[step], *parts = one_half(
            pair, constants, after(seen[2 * step + 1], token), sends[step]
        )
        halves.append(parts)
        keeps[step].append(keep)
        return [parts[0]]

    def collect(step, token):
        received = decode(after(to_core(sends[step]), token))
        nears[step] = keeps[step][0] + received[0]
        codes[step] = encode(keeps[step][1] + received[1])
        return [*token, codes[step]]

    def side_sum(step, token):
        return encode(nears[step] + decode(after(from_sides[step], token)))

    came = []
    update = None
    added = 0
    row_weight = constants[3]
    token = near_half(0, near_pair, [row_weight])
    for step in range(slabs):
        if step > 2:
            update = add_update([halves[added]], after(row_weight, token), update)
            added += 1
            token = [*token, update]
        if step + 1 < slabs:
            near = after(coming_near, token)
            token = [*token, near]
            if step + 2 < slabs and step != 1:
                coming_near = along(near, 1)
        far = after(coming_far, token[:-1] if 0 < step < slabs - 1 else token)
        if step + 2 < slabs and step == 1:
            coming_near = along(after(near, [far]), 1)
        if step + 1 < slabs:
            if step + 2 == slabs:
                coming_far = along(far, 1)
            elif step > 0:
                coming_far = to_side(near)
            near_pair = [near, to_core(near)]
        if step == 1:
            update = add_update([halves[added]], after(row_weight, [*token, far]), update)
            added += 1
            token = [*token, update]
        if step + 1 == slabs and slabs > 2:
            code = side_sum(1, token)
            came.append(along(code, -1))
            token = [*token, code]
        far_pair = [far, to_core(far)]
        if step == 0 and slabs > 2:
            coming_far = to_side(after(near, [far]))
        token = far_half(step, far_pair, token)
        if step + 1 < slabs:
            token = near_half(step + 1, near_pair, token)
        else:
            update = add_update([halves[added]], after(row_weight, token), update)
            added += 1
            token = [update]
        token = collect(step, token)
        if step > 0:
            from_sides[step] = to_side(codes[step])
        if step > 2:
            if step == slabs - 1:
                update = add_update([halves[added]], after(row_weight, token), update)
                added += 1
                token = [update]
            code = side_sum(step - 1, token)
            came.append(along(code, 1 - step))
            token = [*token, code]

    if slabs > 1:
        code = side_sum(slabs - 1, token)
        came.append(along(code, 1))
        token = [*token, code]
    from_sides[0] = to_side(after(codes[0], token))
    grad_out = add_update(
        halves[added:], after(row_weight, token), update, 1.0 / math.sqrt(total_in)
    )
    last = [after(sums, [grad_out]) for sums in (from_sides[0], *came)]
    grad_in_t = finish(nears[0], last, 1.0 / math.sqrt(total_out))
    return (grad_out, grad_in_t)


def solution(mesh):
    in_specs = (
        P("groups", None, "port", None),
        P("port", "groups"),
        P("groups", "port"),
        P("groups"),
        P("groups"),
        P("groups"),
    )
    out_specs = (P("port", "groups"), P("port", "groups"))
    return jax.shard_map(
        on_device, mesh=mesh, in_specs=in_specs, out_specs=out_specs, check_vma=False
    )
```

```python
import functools
import math

import jax
import jax.numpy as jnp
from jax import lax
from jax.experimental import pallas as pl
from jax.experimental.pallas import tpu as pltpu
from jax.sharding import PartitionSpec as P

GRID = 1024


low_freq = 0.1
log_span = math.log(100.0)
least_code = 1e-36


def pole_terms(freq_index, pole_rates):
    omega = low_freq * jnp.exp(log_span * freq_index.astype(jnp.float32) / (GRID - 1))
    denominator = pole_rates[None, :] * pole_rates[None, :] + omega[:, None] * omega[:, None]
    real_side = pole_rates[None, :] / denominator
    imag_side = -omega[:, None] / denominator
    return jnp.stack([real_side, imag_side], axis=1)


def encode(value):
    return ((value * jnp.abs(value)) * (value * value)).astype(jnp.bfloat16)


def decode(code):
    code = code.astype(jnp.float32)
    inverse_root = lax.rsqrt(jnp.maximum(jnp.abs(code), least_code))
    return (code * inverse_root) * (inverse_root * lax.rsqrt(inverse_root))


def ring_order(slabs):
    return [0, *range(1, slabs, 2), *reversed(range(2, slabs, 2))]


def block_at(rank, step, slabs, flip):
    slab = lax.div(rank, 4)
    place = jnp.where(lax.rem(slab, 2) == 1, lax.div(slab + 1, 2), slabs - lax.div(slab, 2))
    place = lax.rem(place + (slabs - step), slabs)
    slab = jnp.where(place <= slabs // 2, 2 * place - 1, 2 * (slabs - place))
    slab = jnp.where(place == 0, 0, slab)
    return 4 * slab + (lax.rem(rank, 4) ^ flip)


def start_copies(rank_ref, measured_ref, first_half, slabs, halves, arrived):
    width = halves[0].shape[-1]
    copies = []
    for at, half in enumerate(halves):
        for core in range(2):
            place = 2 * (first_half + at) + core
            block = block_at(rank_ref[0], place // 4, slabs, place % 4)
            columns = pl.ds(pl.multiple_of(block * width, width), width)
            copy = pltpu.make_async_copy(
                measured_ref.at[:, :, :, columns], half.at[core], arrived.at[2 * at + core]
            )
            copy.start()
            copies.append(copy)
    return copies


def prepare_kernel(
    slabs,
    rank_ref,
    freq_hbm,
    quad_hbm,
    rates_hbm,
    factor_hbm,
    measured_ref,
    scaled_ref,
    turned_ref,
    pole_weight_ref,
    row_weight_ref,
    *refs,
):
    freq_ref, quad_ref, rates_ref, factor_ref, came, arrived = refs[-6:]
    pairs = ((freq_hbm, freq_ref), (quad_hbm, quad_ref), (rates_hbm, rates_ref), (factor_hbm, factor_ref))
    small = [pltpu.make_async_copy(*pair, came.at[at]) for at, pair in enumerate(pairs)]
    for copy in small:
        copy.start()
    copies = start_copies(rank_ref, measured_ref, 0, slabs, refs[:-6], arrived)
    for copy in small:
        copy.wait()
    rates = rates_ref[...]
    factor = factor_ref[...].astype(jnp.float32)
    turned_ref[...] = factor.T.astype(jnp.bfloat16)
    rows = factor.shape[0]
    lanes = pole_weight_ref.shape[2]
    for freq_slot in range(freq_ref.shape[0]):
        index = jnp.full(rates.shape, freq_ref[freq_slot], jnp.int32).astype(jnp.float32)
        weight = jnp.full(rates.shape, quad_ref[freq_slot], jnp.int32).astype(jnp.float32) * 0.25
        omega = low_freq * jnp.exp(log_span * index / (GRID - 1))
        denominator = rates * rates + omega * omega
        for comp_slot, coefficient in enumerate((rates / denominator, -omega / denominator)):
            term = 2 * freq_slot + comp_slot
            scaled_ref[pl.ds(term * rows, rows), :] = (factor * coefficient).astype(jnp.bfloat16)
            weighted = weight * coefficient
            row_weight_ref[term] = weighted
            pole_weight_ref[term] = jnp.broadcast_to(weighted, (lanes, weighted.shape[1])).T
    for copy in copies:
        copy.wait()


def prepare_by_kernel(
    rank, slabs, freq_index, quad_codes, pole_rates, out_factor, measured, width, lanes, halves
):
    rows, poles = out_factor.shape
    terms = 2 * freq_index.shape[0]
    vmem = pl.BlockSpec(memory_space=pltpu.VMEM)
    smem = pl.BlockSpec(memory_space=pltpu.SMEM)
    anywhere = pl.BlockSpec(memory_space=pl.ANY)
    operands = (freq_index, quad_codes, pole_rates[None, :], out_factor, measured)
    made = pl.pallas_call(
        functools.partial(prepare_kernel, slabs),
        in_specs=[smem] + [anywhere] * 5,
        out_specs=[vmem] * (4 + halves),
        out_shape=[
            jax.ShapeDtypeStruct((terms * rows, poles), jnp.bfloat16),
            jax.ShapeDtypeStruct((poles, rows), jnp.bfloat16),
            jax.ShapeDtypeStruct((terms, poles, lanes), jnp.float32),
            jax.ShapeDtypeStruct((terms, 1, poles), jnp.float32),
        ]
        + [jax.ShapeDtypeStruct((2, *measured.shape[:3], width), jnp.bfloat16)] * halves,
        scratch_shapes=[
            pltpu.SMEM(freq_index.shape, jnp.int32),
            pltpu.SMEM(quad_codes.shape, jnp.int32),
            pltpu.VMEM((1, poles), jnp.float32),
            pltpu.VMEM((rows, poles), jnp.bfloat16),
            pltpu.SemaphoreType.DMA((4,)),
            pltpu.SemaphoreType.DMA((2 * halves,)),
        ],
        compiler_params=pltpu.CompilerParams(vmem_limit_bytes=16 * 1024 * 1024),
        cost_estimate=pl.CostEstimate(
            flops=0, bytes_accessed=halves * measured.size // slabs, transcendentals=0
        ),
        name="prepare",
    )(rank, *[pltpu.with_memory_space_constraint(array, pltpu.HBM) for array in operands])
    return made[:4], list(made[4:])


def half_kernel(
    factor_0, factor_1, scaled_ref, turned_ref, pole_weight_ref, seen_ref, *refs
):
    keep_ref, send_ref, residual_ref, held_ref = refs[-4:]
    width = factor_0.shape[1]
    rows = turned_ref.shape[1]
    terms = pole_weight_ref.shape[0]
    models = []
    for core, factor_ref in enumerate((factor_0, factor_1)):
        factor = factor_ref[...]
        held_ref[core] = factor
        models.append(jnp.dot(scaled_ref[...], factor, preferred_element_type=jnp.float32))
    residuals = []
    for core, model in enumerate(models):
        seen = seen_ref[core].reshape(terms * rows, width).astype(jnp.float32)
        residual = (model - seen).astype(jnp.bfloat16)
        residual_ref[core] = residual.reshape(residual_ref.shape[1:])
        residuals.append(residual)
    partials = [None, None]
    for term in range(terms):
        weight = pole_weight_ref[term]
        weight = jnp.concatenate([weight] * (width // weight.shape[1]), axis=1)
        for core, residual in enumerate(residuals):
            part = weight * jnp.dot(
                turned_ref[...],
                residual[term * rows : (term + 1) * rows],
                preferred_element_type=jnp.float32,
            )
            partials[core] = part if term == 0 else partials[core] + part
    keep_ref[...] = partials[0]
    if len(refs) > 4:
        send_ref[0] = refs[0][...]
        send_ref[1] = encode(partials[1])
    else:
        send_ref[...] = encode(partials[1])


def half_by_kernel(factors, constants, seen, near_send):
    scaled, turned, pole_weight, _ = constants
    poles, width = factors[0].shape
    rows = turned.shape[1]
    terms = pole_weight.shape[0]
    half = len(factors) * width
    flops = 2 * 2 * terms * rows * poles * half
    vmem = pl.BlockSpec(memory_space=pltpu.VMEM)
    beside = [] if near_send is None else [near_send]
    return pl.pallas_call(
        half_kernel,
        in_specs=[vmem] * (6 + len(beside)),
        out_specs=[vmem] * 4,
        out_shape=[
            jax.ShapeDtypeStruct((poles, width), jnp.float32),
            jax.ShapeDtypeStruct((2, poles, width) if beside else (poles, width), jnp.bfloat16),
            jax.ShapeDtypeStruct(seen.shape, seen.dtype),
            jax.ShapeDtypeStruct((2, poles, width), jnp.bfloat16),
        ],
        input_output_aliases={5: 2},
        compiler_params=pltpu.CompilerParams(vmem_limit_bytes=16 * 1024 * 1024),
        cost_estimate=pl.CostEstimate(
            flops=10 * flops, bytes_accessed=2 * terms * rows * half, transcendentals=0
        ),
        name="far" if beside else "near",
    )(*factors, scaled, turned, pole_weight, seen, *beside)


def update_kernel(halves, scale, *refs):
    row_weight_ref, *refs, total_ref = refs
    terms = row_weight_ref.shape[0]
    rows, width = refs[0].shape[-2:]
    total = None
    for at in range(halves):
        residual_ref, held_ref = refs[2 * at : 2 * at + 2]
        for core in range(2):
            part = lax.dot_general(
                residual_ref[core].reshape(terms * rows, width),
                held_ref[core],
                (((1,), (1,)), ((), ())),
                preferred_element_type=jnp.float32,
            )
            total = part if total is None else total + part
    update = refs[2 * halves][...] if len(refs) > 2 * halves else 0.0
    for term in range(terms):
        update = update + row_weight_ref[term] * total[term * rows : (term + 1) * rows]
    total_ref[...] = update if scale is None else update * scale


def update_by_kernel(halves, row_weight, update, scale=None):
    poles, width = halves[0][1].shape[1:]
    rows = halves[0][0].shape[-2]
    terms = row_weight.shape[0]
    flops = 4 * len(halves) * terms * rows * poles * width
    vmem = pl.BlockSpec(memory_space=pltpu.VMEM)
    operands = [row_weight, *[array for half in halves for array in half]]
    operands += [] if update is None else [update]
    return pl.pallas_call(
        functools.partial(update_kernel, len(halves), scale),
        in_specs=[vmem] * len(operands),
        out_specs=vmem,
        out_shape=jax.ShapeDtypeStruct((rows, poles), jnp.float32),
        compiler_params=pltpu.CompilerParams(vmem_limit_bytes=16 * 1024 * 1024),
        cost_estimate=pl.CostEstimate(
            flops=20 * flops, bytes_accessed=2 * terms * rows * width, transcendentals=0
        ),
        name="update",
    )(*operands)


def slice_by_ops(rank, slabs, measured, width, first_half, last_half):
    blocks = [
        lax.dynamic_slice_in_dim(
            measured, block_at(rank[0], at // 4, slabs, at % 4) * width, width, 3
        )
        for at in range(2 * first_half, 2 * last_half)
    ]
    return [jnp.stack(blocks[at : at + 2]) for at in range(0, len(blocks), 2)]


def finish_kernel(scale, near_ref, *refs):
    total = near_ref[...]
    for code_ref in refs[:-1]:
        total = total + decode(code_ref[...])
    refs[-1][...] = (total * scale).T


def finish_by_kernel(near, codes, scale):
    poles, width = near.shape
    vmem = pl.BlockSpec(memory_space=pltpu.VMEM)
    return pl.pallas_call(
        functools.partial(finish_kernel, scale),
        in_specs=[vmem] * (1 + len(codes)),
        out_specs=vmem,
        out_shape=jax.ShapeDtypeStruct((width, poles), jnp.float32),
        compiler_params=pltpu.CompilerParams(vmem_limit_bytes=16 * 1024 * 1024),
        cost_estimate=pl.CostEstimate(
            flops=0, bytes_accessed=8 * poles * width, transcendentals=0
        ),
        name="finish",
    )(near, *codes)


def finish_by_ops(near, codes, scale):
    return (sum((decode(code) for code in codes), near) * scale).T


def prepare_by_ops(
    rank, slabs, freq_index, quad_codes, pole_rates, out_factor, measured, width, lanes, halves
):
    rows, poles = out_factor.shape
    coefficients = pole_terms(freq_index, pole_rates)
    weights = quad_codes.astype(jnp.float32) * 0.25
    weighted = (weights[:, None, None] * coefficients).reshape(-1, poles)
    scaled = (
        out_factor.astype(jnp.float32)[None, None, :, :] * coefficients[:, :, None, :]
    ).astype(jnp.bfloat16)
    pole_weight = jnp.broadcast_to(weighted[:, :, None], (weighted.shape[0], poles, lanes))
    seen = slice_by_ops(rank, slabs, measured, width, 0, halves)
    constants = [scaled.reshape(-1, poles), out_factor.T, pole_weight, weighted[:, None, :]]
    return constants, seen


def half_by_ops(factors, constants, seen, near_send):
    scaled, turned, pole_weight, _ = constants
    width = factors[0].shape[1]
    rows = turned.shape[1]
    terms = pole_weight.shape[0]
    partials, residuals = [], []
    for core, factor in enumerate(factors):
        model = jnp.dot(scaled, factor, preferred_element_type=jnp.float32)
        residual = model - seen[core].reshape(terms * rows, width).astype(jnp.float32)
        residual = residual.astype(jnp.bfloat16)
        residuals.append(residual.reshape(seen.shape[1:]))
        partial = jnp.einsum(
            "ki,tij->tkj",
            turned,
            residual.reshape(terms, rows, width),
            preferred_element_type=jnp.float32,
        )
        partials.append(jnp.sum(pole_weight[:, :, :1] * partial, axis=0))
    send = encode(partials[1])
    if near_send is not None:
        send = jnp.stack([near_send, send])
    return partials[0], send, jnp.stack(residuals), jnp.stack(factors)


def update_by_ops(halves, row_weight, update, scale=None):
    rows, width = halves[0][0].shape[-2:]
    terms = row_weight.shape[0]
    total = sum(
        jnp.einsum(
            "tij,kj->tik",
            residual[core].reshape(terms, rows, width),
            held[core],
            preferred_element_type=jnp.float32,
        )
        for residual, held in halves
        for core in range(2)
    )
    part = jnp.sum(row_weight * total, axis=0)
    total = part if update is None else update + part
    return total if scale is None else total * scale


def after(value, earlier):
    return lax.optimization_barrier((value, *earlier))[0]


def on_device(measured, out_factor, in_factor, pole_rates, freq_index, quad_codes):
    rows, total_in = measured.shape[2:]
    poles, width = in_factor.shape
    ranks = lax.axis_size("port")
    rank = lax.axis_index("port").astype(jnp.int32).reshape(1)
    slabs = ranks // 4
    total_out = rows * ranks
    tiled = width % 128 == 0 and rows % 128 == 0
    prepare = prepare_by_kernel if tiled else prepare_by_ops
    one_half = half_by_kernel if tiled else half_by_ops
    add_update = update_by_kernel if tiled else update_by_ops
    finish = finish_by_kernel if tiled else finish_by_ops

    def to_core(block):
        return lax.ppermute(block, "port", [(i, i ^ 1) for i in range(ranks)])

    def to_side(block):
        return lax.ppermute(block, "port", [(i, i ^ 2) for i in range(ranks)])

    ring = ring_order(slabs)
    place = {slab: at for at, slab in enumerate(ring)}

    def along(block, hops):
        pairs = [
            (i, 4 * ring[(place[i // 4] + hops) % slabs] + i % 4) for i in range(ranks)
        ]
        return lax.ppermute(block, "port", pairs)

    near = in_factor
    coming_near = along(near, 1)
    coming_far = to_side(near)
    near_pair = [near, to_core(near)]
    constants, seen = prepare(
        rank,
        slabs,
        freq_index,
        quad_codes,
        pole_rates,
        out_factor,
        measured,
        width,
        min(width, 128),
        2 * slabs,
    )
    nears = [None] * slabs
    keeps = [None] * slabs
    sends = [None] * slabs
    codes = [None] * slabs
    from_sides = [None] * slabs
    halves = []

    def near_half(step, pair, token):
        keep, sends[step], *parts = one_half(pair, constants, after(seen[2 * step], token), None)
        halves.append(parts)
        keeps[step] = [keep]
        return [parts[0]]

    def far_half(step, pair, token):
        keep, sends[step], *parts = one_half(
            pair, constants, after(seen[2 * step + 1], token), sends[step]
        )
        halves.append(parts)
        keeps[step].append(keep)
        return [parts[0]]

    def collect(step, token):
        received = decode(after(to_core(sends[step]), token))
        nears[step] = keeps[step][0] + received[0]
        codes[step] = encode(keeps[step][1] + received[1])
        return [*token, codes[step]]

    def pass_on(step, arriving, token):
        total = nears[step] + decode(after(from_sides[step], token))
        if arriving is not None:
            total = total + decode(after(arriving, token))
        return encode(total)

    arriving = None
    from_next = None
    update = None
    added = 0
    row_weight = constants[3]
    token = near_half(0, near_pair, [row_weight])
    for step in range(slabs):
        if step > 2:
            update = add_update([halves[added]], after(row_weight, token), update)
            added += 1
            token = [*token, update]
        if step + 1 < slabs:
            near = after(coming_near, token)
            token = [*token, near]
            if step + 2 < slabs and step != 1:
                coming_near = along(near, 1)
        far = after(coming_far, token[:-1] if 0 < step < slabs - 1 else token)
        if step + 2 < slabs and step == 1:
            coming_near = along(after(near, [far]), 1)
        if step + 1 < slabs:
            if step + 2 == slabs:
                coming_far = along(far, 1)
            elif step > 0:
                coming_far = to_side(near)
            if step > 0:
                near_pair = [near, to_core(near)]
        if step == 1:
            update = add_update([halves[added]], after(row_weight, [*token, far]), update)
            added += 1
            token = [*token, update]
        if step + 1 == slabs and slabs > 2:
            code = pass_on(1, None, token)
            from_next = along(code, -1)
            token = [*token, code]
        far_pair = [far, to_core(far)]
        if step == 0 and slabs > 2:
            coming_far = to_side(after(near, [far]))
        if step == 0 and slabs > 1:
            near_pair = [near, to_core(after(near, far_pair[1:]))]
        token = far_half(step, far_pair, token)
        if step + 1 < slabs:
            token = near_half(step + 1, near_pair, token)
        else:
            update = add_update([halves[added]], after(row_weight, token), update)
            added += 1
            token = [update]
        token = collect(step, token)
        if step > 0:
            from_sides[step] = to_side(codes[step])
        if step > 2:
            code = pass_on(step - 1, arriving, token)
            arriving = along(code, 1)
            token = [*token, code]

    if slabs > 1:
        middle = (added + 2 * slabs + 1) // 2
        update = add_update(halves[added:middle], after(row_weight, token), update)
        code = pass_on(slabs - 1, arriving, [update])
        arriving = along(code, 1)
        token = [update, code]
    from_sides[0] = to_side(after(codes[0], token))
    if slabs > 1:
        grad_out = add_update(
            halves[middle:], after(row_weight, token), update, 1.0 / math.sqrt(total_in)
        )
    else:
        grad_out = add_update(halves[added:], row_weight, update, 1.0 / math.sqrt(total_in))
    last = [sums for sums in (from_sides[0], from_next, arriving) if sums is not None]
    last = [after(sums, [grad_out]) for sums in last]
    grad_in_t = finish(nears[0], last, 1.0 / math.sqrt(total_out))
    return (grad_out, grad_in_t)


def solution(mesh):
    in_specs = (
        P("groups", None, "port", None),
        P("port", "groups"),
        P("groups", "port"),
        P("groups"),
        P("groups"),
        P("groups"),
    )
    out_specs = (P("port", "groups"), P("port", "groups"))
    return jax.shard_map(
        on_device, mesh=mesh, in_specs=in_specs, out_specs=out_specs, check_vma=False
    )
```

```python
import functools
import math

import jax
import jax.numpy as jnp
from jax import lax
from jax.experimental import pallas as pl
from jax.experimental.pallas import tpu as pltpu
from jax.sharding import PartitionSpec as P

GRID = 1024


low_freq = 0.1
log_span = math.log(100.0)
least_code = 1e-36


def pole_terms(freq_index, pole_rates):
    omega = low_freq * jnp.exp(log_span * freq_index.astype(jnp.float32) / (GRID - 1))
    denominator = pole_rates[None, :] * pole_rates[None, :] + omega[:, None] * omega[:, None]
    real_side = pole_rates[None, :] / denominator
    imag_side = -omega[:, None] / denominator
    return jnp.stack([real_side, imag_side], axis=1)


def encode(value):
    return ((value * jnp.abs(value)) * (value * value)).astype(jnp.bfloat16)


def decode(code):
    code = code.astype(jnp.float32)
    inverse_root = lax.rsqrt(jnp.maximum(jnp.abs(code), least_code))
    return (code * inverse_root) * (inverse_root * lax.rsqrt(inverse_root))


def ring_order(slabs):
    return [0, *range(1, slabs, 2), *reversed(range(2, slabs, 2))]


def block_at(rank, step, slabs, flip):
    slab = lax.div(rank, 4)
    place = jnp.where(lax.rem(slab, 2) == 1, lax.div(slab + 1, 2), slabs - lax.div(slab, 2))
    place = lax.rem(place + (slabs - step), slabs)
    slab = jnp.where(place <= slabs // 2, 2 * place - 1, 2 * (slabs - place))
    slab = jnp.where(place == 0, 0, slab)
    return 4 * slab + (lax.rem(rank, 4) ^ flip)


def start_copies(rank_ref, measured_ref, first_half, slabs, halves, arrived):
    width = halves[0].shape[-1]
    copies = []
    for at, half in enumerate(halves):
        for core in range(2):
            place = 2 * (first_half + at) + core
            block = block_at(rank_ref[0], place // 4, slabs, place % 4)
            columns = pl.ds(pl.multiple_of(block * width, width), width)
            copy = pltpu.make_async_copy(
                measured_ref.at[:, :, :, columns], half.at[core], arrived.at[2 * at + core]
            )
            copy.start()
            copies.append(copy)
    return copies


def prepare_kernel(
    slabs,
    rank_ref,
    freq_hbm,
    quad_hbm,
    rates_hbm,
    factor_hbm,
    measured_ref,
    scaled_ref,
    turned_ref,
    pole_weight_ref,
    row_weight_ref,
    *refs,
):
    freq_ref, quad_ref, rates_ref, factor_ref, came, arrived = refs[-6:]
    pairs = ((freq_hbm, freq_ref), (quad_hbm, quad_ref), (rates_hbm, rates_ref), (factor_hbm, factor_ref))
    small = [pltpu.make_async_copy(*pair, came.at[at]) for at, pair in enumerate(pairs)]
    for copy in small:
        copy.start()
    copies = start_copies(rank_ref, measured_ref, 0, slabs, refs[:-6], arrived)
    for copy in small:
        copy.wait()
    rates = rates_ref[...]
    factor = factor_ref[...].astype(jnp.float32)
    turned_ref[...] = factor.T.astype(jnp.bfloat16)
    rows = factor.shape[0]
    lanes = pole_weight_ref.shape[2]
    for freq_slot in range(freq_ref.shape[0]):
        index = jnp.full(rates.shape, freq_ref[freq_slot], jnp.int32).astype(jnp.float32)
        weight = jnp.full(rates.shape, quad_ref[freq_slot], jnp.int32).astype(jnp.float32) * 0.25
        omega = low_freq * jnp.exp(log_span * index / (GRID - 1))
        denominator = rates * rates + omega * omega
        for comp_slot, coefficient in enumerate((rates / denominator, -omega / denominator)):
            term = 2 * freq_slot + comp_slot
            scaled_ref[pl.ds(term * rows, rows), :] = (factor * coefficient).astype(jnp.bfloat16)
            weighted = weight * coefficient
            row_weight_ref[term] = weighted
            pole_weight_ref[term] = jnp.broadcast_to(weighted, (lanes, weighted.shape[1])).T
    for copy in copies:
        copy.wait()


def prepare_by_kernel(
    rank, slabs, freq_index, quad_codes, pole_rates, out_factor, measured, width, lanes, halves
):
    rows, poles = out_factor.shape
    terms = 2 * freq_index.shape[0]
    vmem = pl.BlockSpec(memory_space=pltpu.VMEM)
    smem = pl.BlockSpec(memory_space=pltpu.SMEM)
    anywhere = pl.BlockSpec(memory_space=pl.ANY)
    operands = (freq_index, quad_codes, pole_rates[None, :], out_factor, measured)
    made = pl.pallas_call(
        functools.partial(prepare_kernel, slabs),
        in_specs=[smem] + [anywhere] * 5,
        out_specs=[vmem] * (4 + halves),
        out_shape=[
            jax.ShapeDtypeStruct((terms * rows, poles), jnp.bfloat16),
            jax.ShapeDtypeStruct((poles, rows), jnp.bfloat16),
            jax.ShapeDtypeStruct((terms, poles, lanes), jnp.float32),
            jax.ShapeDtypeStruct((terms, 1, poles), jnp.float32),
        ]
        + [jax.ShapeDtypeStruct((2, *measured.shape[:3], width), jnp.bfloat16)] * halves,
        scratch_shapes=[
            pltpu.SMEM(freq_index.shape, jnp.int32),
            pltpu.SMEM(quad_codes.shape, jnp.int32),
            pltpu.VMEM((1, poles), jnp.float32),
            pltpu.VMEM((rows, poles), jnp.bfloat16),
            pltpu.SemaphoreType.DMA((4,)),
            pltpu.SemaphoreType.DMA((2 * halves,)),
        ],
        compiler_params=pltpu.CompilerParams(vmem_limit_bytes=16 * 1024 * 1024),
        cost_estimate=pl.CostEstimate(
            flops=0, bytes_accessed=halves * measured.size // slabs, transcendentals=0
        ),
        name="prepare",
    )(rank, *[pltpu.with_memory_space_constraint(array, pltpu.HBM) for array in operands])
    return made[:4], list(made[4:])


def half_kernel(
    factor_0, factor_1, scaled_ref, turned_ref, pole_weight_ref, seen_ref, *refs
):
    keep_ref, send_ref, residual_ref, held_ref = refs[-4:]
    width = factor_0.shape[1]
    rows = turned_ref.shape[1]
    terms = pole_weight_ref.shape[0]
    models = []
    for core, factor_ref in enumerate((factor_0, factor_1)):
        factor = factor_ref[...]
        held_ref[core] = factor
        models.append(jnp.dot(scaled_ref[...], factor, preferred_element_type=jnp.float32))
    residuals = []
    for core, model in enumerate(models):
        seen = seen_ref[core].reshape(terms * rows, width).astype(jnp.float32)
        residual = (model - seen).astype(jnp.bfloat16)
        residual_ref[core] = residual.reshape(residual_ref.shape[1:])
        residuals.append(residual)
    partials = [None, None]
    for term in range(terms):
        weight = pole_weight_ref[term]
        weight = jnp.concatenate([weight] * (width // weight.shape[1]), axis=1)
        for core, residual in enumerate(residuals):
            part = weight * jnp.dot(
                turned_ref[...],
                residual[term * rows : (term + 1) * rows],
                preferred_element_type=jnp.float32,
            )
            partials[core] = part if term == 0 else partials[core] + part
    keep_ref[...] = partials[0]
    if len(refs) > 4:
        send_ref[0] = refs[0][...]
        send_ref[1] = encode(partials[1])
    else:
        send_ref[...] = encode(partials[1])


def half_by_kernel(factors, constants, seen, near_send):
    scaled, turned, pole_weight, _ = constants
    poles, width = factors[0].shape
    rows = turned.shape[1]
    terms = pole_weight.shape[0]
    half = len(factors) * width
    flops = 2 * 2 * terms * rows * poles * half
    vmem = pl.BlockSpec(memory_space=pltpu.VMEM)
    beside = [] if near_send is None else [near_send]
    return pl.pallas_call(
        half_kernel,
        in_specs=[vmem] * (6 + len(beside)),
        out_specs=[vmem] * 4,
        out_shape=[
            jax.ShapeDtypeStruct((poles, width), jnp.float32),
            jax.ShapeDtypeStruct((2, poles, width) if beside else (poles, width), jnp.bfloat16),
            jax.ShapeDtypeStruct(seen.shape, seen.dtype),
            jax.ShapeDtypeStruct((2, poles, width), jnp.bfloat16),
        ],
        input_output_aliases={5: 2},
        compiler_params=pltpu.CompilerParams(vmem_limit_bytes=16 * 1024 * 1024),
        cost_estimate=pl.CostEstimate(
            flops=10 * flops, bytes_accessed=2 * terms * rows * half, transcendentals=0
        ),
        name="far" if beside else "near",
    )(*factors, scaled, turned, pole_weight, seen, *beside)


def update_kernel(halves, scale, *refs):
    row_weight_ref, *refs, total_ref = refs
    terms = row_weight_ref.shape[0]
    rows, width = refs[0].shape[-2:]
    total = None
    for at in range(halves):
        residual_ref, held_ref = refs[2 * at : 2 * at + 2]
        for core in range(2):
            part = lax.dot_general(
                residual_ref[core].reshape(terms * rows, width),
                held_ref[core],
                (((1,), (1,)), ((), ())),
                preferred_element_type=jnp.float32,
            )
            total = part if total is None else total + part
    update = refs[2 * halves][...] if len(refs) > 2 * halves else 0.0
    for term in range(terms):
        update = update + row_weight_ref[term] * total[term * rows : (term + 1) * rows]
    total_ref[...] = update if scale is None else update * scale


def update_by_kernel(halves, row_weight, update, scale=None):
    poles, width = halves[0][1].shape[1:]
    rows = halves[0][0].shape[-2]
    terms = row_weight.shape[0]
    flops = 4 * len(halves) * terms * rows * poles * width
    vmem = pl.BlockSpec(memory_space=pltpu.VMEM)
    operands = [row_weight, *[array for half in halves for array in half]]
    operands += [] if update is None else [update]
    return pl.pallas_call(
        functools.partial(update_kernel, len(halves), scale),
        in_specs=[vmem] * len(operands),
        out_specs=vmem,
        out_shape=jax.ShapeDtypeStruct((rows, poles), jnp.float32),
        compiler_params=pltpu.CompilerParams(vmem_limit_bytes=16 * 1024 * 1024),
        cost_estimate=pl.CostEstimate(
            flops=20 * flops, bytes_accessed=2 * terms * rows * width, transcendentals=0
        ),
        name="update",
    )(*operands)


def slice_by_ops(rank, slabs, measured, width, first_half, last_half):
    blocks = [
        lax.dynamic_slice_in_dim(
            measured, block_at(rank[0], at // 4, slabs, at % 4) * width, width, 3
        )
        for at in range(2 * first_half, 2 * last_half)
    ]
    return [jnp.stack(blocks[at : at + 2]) for at in range(0, len(blocks), 2)]


def finish_kernel(scale, upper_ref, lower_ref, code_ref, out_ref):
    poles = upper_ref.shape[0]
    out_ref[:, :poles] = (upper_ref[...] * scale).T
    out_ref[:, poles:] = ((lower_ref[...] + decode(code_ref[...])) * scale).T


def finish_by_kernel(own, code, scale):
    width = own[0].shape[1]
    poles = own[0].shape[0] + own[1].shape[0]
    vmem = pl.BlockSpec(memory_space=pltpu.VMEM)
    return pl.pallas_call(
        functools.partial(finish_kernel, scale),
        in_specs=[vmem] * 3,
        out_specs=vmem,
        out_shape=jax.ShapeDtypeStruct((width, poles), jnp.float32),
        compiler_params=pltpu.CompilerParams(vmem_limit_bytes=16 * 1024 * 1024),
        cost_estimate=pl.CostEstimate(
            flops=0, bytes_accessed=8 * poles * width, transcendentals=0
        ),
        name="finish",
    )(*own, code)


def finish_by_ops(own, code, scale):
    return (jnp.concatenate([own[0], own[1] + decode(code)]) * scale).T


def prepare_by_ops(
    rank, slabs, freq_index, quad_codes, pole_rates, out_factor, measured, width, lanes, halves
):
    rows, poles = out_factor.shape
    coefficients = pole_terms(freq_index, pole_rates)
    weights = quad_codes.astype(jnp.float32) * 0.25
    weighted = (weights[:, None, None] * coefficients).reshape(-1, poles)
    scaled = (
        out_factor.astype(jnp.float32)[None, None, :, :] * coefficients[:, :, None, :]
    ).astype(jnp.bfloat16)
    pole_weight = jnp.broadcast_to(weighted[:, :, None], (weighted.shape[0], poles, lanes))
    seen = slice_by_ops(rank, slabs, measured, width, 0, halves)
    constants = [scaled.reshape(-1, poles), out_factor.T, pole_weight, weighted[:, None, :]]
    return constants, seen


def half_by_ops(factors, constants, seen, near_send):
    scaled, turned, pole_weight, _ = constants
    width = factors[0].shape[1]
    rows = turned.shape[1]
    terms = pole_weight.shape[0]
    partials, residuals = [], []
    for core, factor in enumerate(factors):
        model = jnp.dot(scaled, factor, preferred_element_type=jnp.float32)
        residual = model - seen[core].reshape(terms * rows, width).astype(jnp.float32)
        residual = residual.astype(jnp.bfloat16)
        residuals.append(residual.reshape(seen.shape[1:]))
        partial = jnp.einsum(
            "ki,tij->tkj",
            turned,
            residual.reshape(terms, rows, width),
            preferred_element_type=jnp.float32,
        )
        partials.append(jnp.sum(pole_weight[:, :, :1] * partial, axis=0))
    send = encode(partials[1])
    if near_send is not None:
        send = jnp.stack([near_send, send])
    return partials[0], send, jnp.stack(residuals), jnp.stack(factors)


def update_by_ops(halves, row_weight, update, scale=None):
    rows, width = halves[0][0].shape[-2:]
    terms = row_weight.shape[0]
    total = sum(
        jnp.einsum(
            "tij,kj->tik",
            residual[core].reshape(terms, rows, width),
            held[core],
            preferred_element_type=jnp.float32,
        )
        for residual, held in halves
        for core in range(2)
    )
    part = jnp.sum(row_weight * total, axis=0)
    total = part if update is None else update + part
    return total if scale is None else total * scale


def after(value, earlier):
    return lax.optimization_barrier((value, *earlier))[0]


def on_device(measured, out_factor, in_factor, pole_rates, freq_index, quad_codes):
    rows, total_in = measured.shape[2:]
    poles, width = in_factor.shape
    ranks = lax.axis_size("port")
    rank = lax.axis_index("port").astype(jnp.int32).reshape(1)
    slabs = ranks // 4
    total_out = rows * ranks
    tiled = width % 128 == 0 and rows % 128 == 0
    prepare = prepare_by_kernel if tiled else prepare_by_ops
    one_half = half_by_kernel if tiled else half_by_ops
    add_update = update_by_kernel if tiled else update_by_ops
    finish = finish_by_kernel if tiled else finish_by_ops

    def to_core(block):
        return lax.ppermute(block, "port", [(i, i ^ 1) for i in range(ranks)])

    def to_side(block):
        return lax.ppermute(block, "port", [(i, i ^ 2) for i in range(ranks)])

    ring = ring_order(slabs)
    place = {slab: at for at, slab in enumerate(ring)}

    def along(block, hops):
        pairs = [
            (i, 4 * ring[(place[i // 4] + hops) % slabs] + i % 4) for i in range(ranks)
        ]
        return lax.ppermute(block, "port", pairs)

    near = in_factor
    coming_near = along(near, 1)
    coming_far = to_side(near)
    near_pair = [near, to_core(near)]
    constants, seen = prepare(
        rank,
        slabs,
        freq_index,
        quad_codes,
        pole_rates,
        out_factor,
        measured,
        width,
        min(width, 128),
        2 * slabs,
    )
    nears = [None] * slabs
    keeps = [None] * slabs
    sends = [None] * slabs
    codes = [None] * slabs
    from_sides = [None] * slabs
    halves = []

    def near_half(step, pair, token):
        keep, sends[step], *parts = one_half(pair, constants, after(seen[2 * step], token), None)
        halves.append(parts)
        keeps[step] = [keep]
        return [parts[0]]

    def far_half(step, pair, token):
        keep, sends[step], *parts = one_half(
            pair, constants, after(seen[2 * step + 1], token), sends[step]
        )
        halves.append(parts)
        keeps[step].append(keep)
        return [parts[0]]

    def collect(step, token):
        received = decode(after(to_core(sends[step]), token))
        nears[step] = keeps[step][0] + received[0]
        codes[step] = encode(keeps[step][1] + received[1])
        return [*token, codes[step]]

    parts = (slice(0, poles // 2), slice(poles // 2, poles))

    def pass_on(step, part, arriving, token):
        total = nears[step][parts[part]] + decode(after(from_sides[step], token)[parts[part]])
        if arriving is not None and len(arriving) == 1:
            total = total + decode(after(arriving[0], token)[parts[part]])
        elif arriving is not None:
            total = total + decode(after(arriving[part], token))
        return encode(total)

    arriving = None
    update = None
    added = 0
    row_weight = constants[3]
    token = near_half(0, near_pair, [row_weight])
    for step in range(slabs):
        if step > 2:
            update = add_update([halves[added]], after(row_weight, token), update)
            added += 1
            token = [*token, update]
        if step + 1 < slabs:
            near = after(coming_near, token)
            token = [*token, near]
            if step > 0:
                near_pair = [near, to_core(near)]
            if step + 2 < slabs and step != 1:
                coming_near = along(near, 1)
        if step == 1 and step + 1 < slabs:
            far = after(coming_far, [*token[:-1], near_pair[1]])
        else:
            far = after(coming_far, token[:-1] if 0 < step < slabs - 1 else token)
        if step + 2 < slabs and step == 1:
            coming_near = along(after(near, [far]), 1)
        if step + 1 < slabs:
            if step + 2 == slabs:
                coming_far = along(far, 1)
            elif step > 0:
                coming_far = to_side(near)
        if step == 1:
            update = add_update([halves[added]], after(row_weight, [*token, far]), update)
            added += 1
            token = [*token, update]
        if step + 1 == slabs and slabs > 2:
            code = encode(nears[1] + decode(after(from_sides[1], token)))
            arriving = [along(code, 1)]
            token = [*token, code]
        far_pair = [far, to_core(far)]
        if step == 0 and slabs > 2:
            coming_far = to_side(after(near, [far]))
        if step == 0 and slabs > 1:
            near_pair = [near, to_core(after(near, far_pair[1:]))]
        token = far_half(step, far_pair, token)
        if step + 1 < slabs:
            token = near_half(step + 1, near_pair, token)
        else:
            update = add_update([halves[added]], after(row_weight, token), update)
            added += 1
            token = [update]
        token = collect(step, token)
        if step > 0:
            from_sides[step] = to_side(codes[step])
        if step > 2:
            if step == slabs - 1:
                update = add_update(
                    halves[added : added + 3], after(row_weight, token), update
                )
                added += 3
                token = [update]
            sums = [pass_on(step - 1, part, arriving, token) for part in (0, 1)]
            arriving = [along(code, 1) for code in sums]
            token = [*token, *sums]

    if slabs > 1:
        sums = [pass_on(slabs - 1, 0, arriving, token)]
        update = add_update([halves[added]], after(row_weight, sums), update)
        added += 1
        sums.append(pass_on(slabs - 1, 1, arriving, [update]))
        arriving = [along(code, 1) for code in sums]
        token = sums
    from_sides[0] = to_side(after(codes[0], token[:1]))
    own = [nears[0][part] for part in parts]
    if slabs > 1:
        from_side = decode(after(from_sides[0], token))
        own = [mine + from_side[part] for mine, part in zip(own, parts)]
        own[0] = own[0] + decode(after(arriving[0], token))
        token = own
    grad_out = add_update(
        halves[added:], after(row_weight, token), update, 1.0 / math.sqrt(total_in)
    )
    last = after(arriving[1] if slabs > 1 else from_sides[0], [grad_out])
    grad_in_t = finish(own, last, 1.0 / math.sqrt(total_out))
    return (grad_out, grad_in_t)


def solution(mesh):
    in_specs = (
        P("groups", None, "port", None),
        P("port", "groups"),
        P("groups", "port"),
        P("groups"),
        P("groups"),
        P("groups"),
    )
    out_specs = (P("port", "groups"), P("port", "groups"))
    return jax.shard_map(
        on_device, mesh=mesh, in_specs=in_specs, out_specs=out_specs, check_vma=False
    )
```

```python
import functools
import math

import jax
import jax.numpy as jnp
from jax import lax
from jax.experimental import pallas as pl
from jax.experimental.pallas import tpu as pltpu
from jax.sharding import PartitionSpec as P

GRID = 1024


low_freq = 0.1
log_span = math.log(100.0)
least_code = 1e-36


def pole_terms(freq_index, pole_rates):
    omega = low_freq * jnp.exp(log_span * freq_index.astype(jnp.float32) / (GRID - 1))
    denominator = pole_rates[None, :] * pole_rates[None, :] + omega[:, None] * omega[:, None]
    real_side = pole_rates[None, :] / denominator
    imag_side = -omega[:, None] / denominator
    return jnp.stack([real_side, imag_side], axis=1)


def encode(value):
    return ((value * jnp.abs(value)) * (value * value)).astype(jnp.bfloat16)


def decode(code):
    code = code.astype(jnp.float32)
    inverse_root = lax.rsqrt(jnp.maximum(jnp.abs(code), least_code))
    return (code * inverse_root) * (inverse_root * lax.rsqrt(inverse_root))


def ring_order(slabs):
    return [0, *range(1, slabs, 2), *reversed(range(2, slabs, 2))]


def block_at(rank, step, slabs, flip):
    slab = lax.div(rank, 4)
    place = jnp.where(lax.rem(slab, 2) == 1, lax.div(slab + 1, 2), slabs - lax.div(slab, 2))
    place = lax.rem(place + (slabs - step), slabs)
    slab = jnp.where(place <= slabs // 2, 2 * place - 1, 2 * (slabs - place))
    slab = jnp.where(place == 0, 0, slab)
    return 4 * slab + (lax.rem(rank, 4) ^ flip)


def start_copies(rank_ref, measured_ref, first_half, slabs, halves, arrived):
    width = halves[0].shape[-1]
    copies = []
    for at, half in enumerate(halves):
        for core in range(2):
            place = 2 * (first_half + at) + core
            block = block_at(rank_ref[0], place // 4, slabs, place % 4)
            columns = pl.ds(pl.multiple_of(block * width, width), width)
            copy = pltpu.make_async_copy(
                measured_ref.at[:, :, :, columns], half.at[core], arrived.at[2 * at + core]
            )
            copy.start()
            copies.append(copy)
    return copies


def prepare_kernel(
    slabs,
    rank_ref,
    freq_hbm,
    quad_hbm,
    rates_hbm,
    factor_hbm,
    measured_ref,
    scaled_ref,
    turned_ref,
    pole_weight_ref,
    row_weight_ref,
    *refs,
):
    freq_ref, quad_ref, rates_ref, factor_ref, came, arrived = refs[-6:]
    pairs = ((freq_hbm, freq_ref), (quad_hbm, quad_ref), (rates_hbm, rates_ref), (factor_hbm, factor_ref))
    small = [pltpu.make_async_copy(*pair, came.at[at]) for at, pair in enumerate(pairs)]
    for copy in small:
        copy.start()
    copies = start_copies(rank_ref, measured_ref, 0, slabs, refs[:-6], arrived)
    for copy in small:
        copy.wait()
    rates = rates_ref[...]
    factor = factor_ref[...].astype(jnp.float32)
    turned_ref[...] = factor.T.astype(jnp.bfloat16)
    rows = factor.shape[0]
    lanes = pole_weight_ref.shape[2]
    for freq_slot in range(freq_ref.shape[0]):
        index = jnp.full(rates.shape, freq_ref[freq_slot], jnp.int32).astype(jnp.float32)
        weight = jnp.full(rates.shape, quad_ref[freq_slot], jnp.int32).astype(jnp.float32) * 0.25
        omega = low_freq * jnp.exp(log_span * index / (GRID - 1))
        denominator = rates * rates + omega * omega
        for comp_slot, coefficient in enumerate((rates / denominator, -omega / denominator)):
            term = 2 * freq_slot + comp_slot
            scaled_ref[pl.ds(term * rows, rows), :] = (factor * coefficient).astype(jnp.bfloat16)
            weighted = weight * coefficient
            row_weight_ref[term] = weighted
            pole_weight_ref[term] = jnp.broadcast_to(weighted, (lanes, weighted.shape[1])).T
    for copy in copies:
        copy.wait()


def prepare_by_kernel(
    rank, slabs, freq_index, quad_codes, pole_rates, out_factor, measured, width, lanes, halves
):
    rows, poles = out_factor.shape
    terms = 2 * freq_index.shape[0]
    vmem = pl.BlockSpec(memory_space=pltpu.VMEM)
    smem = pl.BlockSpec(memory_space=pltpu.SMEM)
    anywhere = pl.BlockSpec(memory_space=pl.ANY)
    operands = (freq_index, quad_codes, pole_rates[None, :], out_factor, measured)
    made = pl.pallas_call(
        functools.partial(prepare_kernel, slabs),
        in_specs=[smem] + [anywhere] * 5,
        out_specs=[vmem] * (4 + halves),
        out_shape=[
            jax.ShapeDtypeStruct((terms * rows, poles), jnp.bfloat16),
            jax.ShapeDtypeStruct((poles, rows), jnp.bfloat16),
            jax.ShapeDtypeStruct((terms, poles, lanes), jnp.float32),
            jax.ShapeDtypeStruct((terms, 1, poles), jnp.float32),
        ]
        + [jax.ShapeDtypeStruct((2, *measured.shape[:3], width), jnp.bfloat16)] * halves,
        scratch_shapes=[
            pltpu.SMEM(freq_index.shape, jnp.int32),
            pltpu.SMEM(quad_codes.shape, jnp.int32),
            pltpu.VMEM((1, poles), jnp.float32),
            pltpu.VMEM((rows, poles), jnp.bfloat16),
            pltpu.SemaphoreType.DMA((4,)),
            pltpu.SemaphoreType.DMA((2 * halves,)),
        ],
        compiler_params=pltpu.CompilerParams(vmem_limit_bytes=16 * 1024 * 1024),
        cost_estimate=pl.CostEstimate(
            flops=0, bytes_accessed=halves * measured.size // slabs, transcendentals=0
        ),
        name="prepare",
    )(rank, *[pltpu.with_memory_space_constraint(array, pltpu.HBM) for array in operands])
    return made[:4], list(made[4:])


def half_kernel(
    factor_0, factor_1, scaled_ref, turned_ref, pole_weight_ref, seen_ref, *refs
):
    keep_ref, send_ref, residual_ref, held_ref = refs[-4:]
    width = factor_0.shape[1]
    rows = turned_ref.shape[1]
    terms = pole_weight_ref.shape[0]
    models = []
    for core, factor_ref in enumerate((factor_0, factor_1)):
        factor = factor_ref[...]
        held_ref[core] = factor
        models.append(jnp.dot(scaled_ref[...], factor, preferred_element_type=jnp.float32))
    residuals = []
    for core, model in enumerate(models):
        seen = seen_ref[core].reshape(terms * rows, width).astype(jnp.float32)
        residual = (model - seen).astype(jnp.bfloat16)
        residual_ref[core] = residual.reshape(residual_ref.shape[1:])
        residuals.append(residual)
    partials = [None, None]
    for term in range(terms):
        weight = pole_weight_ref[term]
        weight = jnp.concatenate([weight] * (width // weight.shape[1]), axis=1)
        for core, residual in enumerate(residuals):
            part = weight * jnp.dot(
                turned_ref[...],
                residual[term * rows : (term + 1) * rows],
                preferred_element_type=jnp.float32,
            )
            partials[core] = part if term == 0 else partials[core] + part
    keep_ref[...] = partials[0]
    if len(refs) > 4:
        send_ref[0] = refs[0][...]
        send_ref[1] = encode(partials[1])
    else:
        send_ref[...] = encode(partials[1])


def half_by_kernel(factors, constants, seen, near_send):
    scaled, turned, pole_weight, _ = constants
    poles, width = factors[0].shape
    rows = turned.shape[1]
    terms = pole_weight.shape[0]
    half = len(factors) * width
    flops = 2 * 2 * terms * rows * poles * half
    vmem = pl.BlockSpec(memory_space=pltpu.VMEM)
    beside = [] if near_send is None else [near_send]
    return pl.pallas_call(
        half_kernel,
        in_specs=[vmem] * (6 + len(beside)),
        out_specs=[vmem] * 4,
        out_shape=[
            jax.ShapeDtypeStruct((poles, width), jnp.float32),
            jax.ShapeDtypeStruct((2, poles, width) if beside else (poles, width), jnp.bfloat16),
            jax.ShapeDtypeStruct(seen.shape, seen.dtype),
            jax.ShapeDtypeStruct((2, poles, width), jnp.bfloat16),
        ],
        input_output_aliases={5: 2},
        compiler_params=pltpu.CompilerParams(vmem_limit_bytes=16 * 1024 * 1024),
        cost_estimate=pl.CostEstimate(
            flops=10 * flops, bytes_accessed=2 * terms * rows * half, transcendentals=0
        ),
        name="far" if beside else "near",
    )(*factors, scaled, turned, pole_weight, seen, *beside)


def update_kernel(halves, scale, *refs):
    row_weight_ref, *refs, total_ref = refs
    terms = row_weight_ref.shape[0]
    rows, width = refs[0].shape[-2:]
    total = None
    for at in range(halves):
        residual_ref, held_ref = refs[2 * at : 2 * at + 2]
        for core in range(2):
            part = lax.dot_general(
                residual_ref[core].reshape(terms * rows, width),
                held_ref[core],
                (((1,), (1,)), ((), ())),
                preferred_element_type=jnp.float32,
            )
            total = part if total is None else total + part
    update = refs[2 * halves][...] if len(refs) > 2 * halves else 0.0
    for term in range(terms):
        update = update + row_weight_ref[term] * total[term * rows : (term + 1) * rows]
    total_ref[...] = update if scale is None else update * scale


def update_by_kernel(halves, row_weight, update, scale=None):
    poles, width = halves[0][1].shape[1:]
    rows = halves[0][0].shape[-2]
    terms = row_weight.shape[0]
    flops = 4 * len(halves) * terms * rows * poles * width
    vmem = pl.BlockSpec(memory_space=pltpu.VMEM)
    operands = [row_weight, *[array for half in halves for array in half]]
    operands += [] if update is None else [update]
    return pl.pallas_call(
        functools.partial(update_kernel, len(halves), scale),
        in_specs=[vmem] * len(operands),
        out_specs=vmem,
        out_shape=jax.ShapeDtypeStruct((rows, poles), jnp.float32),
        compiler_params=pltpu.CompilerParams(vmem_limit_bytes=16 * 1024 * 1024),
        cost_estimate=pl.CostEstimate(
            flops=20 * flops, bytes_accessed=2 * terms * rows * width, transcendentals=0
        ),
        name="update",
    )(*operands)


def slice_by_ops(rank, slabs, measured, width, first_half, last_half):
    blocks = [
        lax.dynamic_slice_in_dim(
            measured, block_at(rank[0], at // 4, slabs, at % 4) * width, width, 3
        )
        for at in range(2 * first_half, 2 * last_half)
    ]
    return [jnp.stack(blocks[at : at + 2]) for at in range(0, len(blocks), 2)]


def finish_kernel(scale, upper_ref, lower_ref, code_ref, out_ref):
    poles = upper_ref.shape[0]
    out_ref[:, :poles] = (upper_ref[...] * scale).T
    out_ref[:, poles:] = ((lower_ref[...] + decode(code_ref[...])) * scale).T


def finish_by_kernel(own, code, scale):
    width = own[0].shape[1]
    poles = own[0].shape[0] + own[1].shape[0]
    vmem = pl.BlockSpec(memory_space=pltpu.VMEM)
    return pl.pallas_call(
        functools.partial(finish_kernel, scale),
        in_specs=[vmem] * 3,
        out_specs=vmem,
        out_shape=jax.ShapeDtypeStruct((width, poles), jnp.float32),
        compiler_params=pltpu.CompilerParams(vmem_limit_bytes=16 * 1024 * 1024),
        cost_estimate=pl.CostEstimate(
            flops=0, bytes_accessed=8 * poles * width, transcendentals=0
        ),
        name="finish",
    )(*own, code)


def finish_by_ops(own, code, scale):
    return (jnp.concatenate([own[0], own[1] + decode(code)]) * scale).T


def prepare_by_ops(
    rank, slabs, freq_index, quad_codes, pole_rates, out_factor, measured, width, lanes, halves
):
    rows, poles = out_factor.shape
    coefficients = pole_terms(freq_index, pole_rates)
    weights = quad_codes.astype(jnp.float32) * 0.25
    weighted = (weights[:, None, None] * coefficients).reshape(-1, poles)
    scaled = (
        out_factor.astype(jnp.float32)[None, None, :, :] * coefficients[:, :, None, :]
    ).astype(jnp.bfloat16)
    pole_weight = jnp.broadcast_to(weighted[:, :, None], (weighted.shape[0], poles, lanes))
    seen = slice_by_ops(rank, slabs, measured, width, 0, halves)
    constants = [scaled.reshape(-1, poles), out_factor.T, pole_weight, weighted[:, None, :]]
    return constants, seen


def half_by_ops(factors, constants, seen, near_send):
    scaled, turned, pole_weight, _ = constants
    width = factors[0].shape[1]
    rows = turned.shape[1]
    terms = pole_weight.shape[0]
    partials, residuals = [], []
    for core, factor in enumerate(factors):
        model = jnp.dot(scaled, factor, preferred_element_type=jnp.float32)
        residual = model - seen[core].reshape(terms * rows, width).astype(jnp.float32)
        residual = residual.astype(jnp.bfloat16)
        residuals.append(residual.reshape(seen.shape[1:]))
        partial = jnp.einsum(
            "ki,tij->tkj",
            turned,
            residual.reshape(terms, rows, width),
            preferred_element_type=jnp.float32,
        )
        partials.append(jnp.sum(pole_weight[:, :, :1] * partial, axis=0))
    send = encode(partials[1])
    if near_send is not None:
        send = jnp.stack([near_send, send])
    return partials[0], send, jnp.stack(residuals), jnp.stack(factors)


def update_by_ops(halves, row_weight, update, scale=None):
    rows, width = halves[0][0].shape[-2:]
    terms = row_weight.shape[0]
    total = sum(
        jnp.einsum(
            "tij,kj->tik",
            residual[core].reshape(terms, rows, width),
            held[core],
            preferred_element_type=jnp.float32,
        )
        for residual, held in halves
        for core in range(2)
    )
    part = jnp.sum(row_weight * total, axis=0)
    total = part if update is None else update + part
    return total if scale is None else total * scale


def after(value, earlier):
    return lax.optimization_barrier((value, *earlier))[0]


def on_device(measured, out_factor, in_factor, pole_rates, freq_index, quad_codes):
    rows, total_in = measured.shape[2:]
    poles, width = in_factor.shape
    ranks = lax.axis_size("port")
    rank = lax.axis_index("port").astype(jnp.int32).reshape(1)
    slabs = ranks // 4
    total_out = rows * ranks
    tiled = width % 128 == 0 and rows % 128 == 0
    prepare = prepare_by_kernel if tiled else prepare_by_ops
    one_half = half_by_kernel if tiled else half_by_ops
    add_update = update_by_kernel if tiled else update_by_ops
    finish = finish_by_kernel if tiled else finish_by_ops

    def to_core(block):
        return lax.ppermute(block, "port", [(i, i ^ 1) for i in range(ranks)])

    def to_side(block):
        return lax.ppermute(block, "port", [(i, i ^ 2) for i in range(ranks)])

    ring = ring_order(slabs)
    place = {slab: at for at, slab in enumerate(ring)}

    def along(block, hops):
        pairs = [
            (i, 4 * ring[(place[i // 4] + hops) % slabs] + i % 4) for i in range(ranks)
        ]
        return lax.ppermute(block, "port", pairs)

    near = in_factor
    coming_near = along(near, 1)
    coming_far = to_side(near)
    near_pair = [near, to_core(near)]
    constants, seen = prepare(
        rank,
        slabs,
        freq_index,
        quad_codes,
        pole_rates,
        out_factor,
        measured,
        width,
        min(width, 128),
        2 * slabs,
    )
    nears = [None] * slabs
    keeps = [None] * slabs
    sends = [None] * slabs
    codes = [None] * slabs
    from_sides = [None] * slabs
    halves = []

    def near_half(step, pair, token):
        keep, sends[step], *parts = one_half(pair, constants, after(seen[2 * step], token), None)
        halves.append(parts)
        keeps[step] = [keep]
        return [parts[0]]

    def far_half(step, pair, token):
        keep, sends[step], *parts = one_half(
            pair, constants, after(seen[2 * step + 1], token), sends[step]
        )
        halves.append(parts)
        keeps[step].append(keep)
        return [parts[0]]

    def collect(step, token):
        received = decode(after(to_core(sends[step]), token))
        nears[step] = keeps[step][0] + received[0]
        codes[step] = encode(keeps[step][1] + received[1])
        return [*token, codes[step]]

    parts = (slice(0, poles // 2), slice(poles // 2, poles))

    def pass_on(step, part, arriving, token):
        total = nears[step][parts[part]] + decode(after(from_sides[step], token)[parts[part]])
        if arriving is not None and len(arriving) == 1:
            total = total + decode(after(arriving[0], token)[parts[part]])
        elif arriving is not None:
            total = total + decode(after(arriving[part], token))
        return encode(total)

    arriving = None
    update = None
    added = 0
    row_weight = constants[3]
    token = near_half(0, near_pair, [row_weight])
    for step in range(slabs):
        if step == 1 or step > 2:
            count = 2 if 2 < step == slabs - 1 else 1
            update = add_update(halves[added : added + count], after(row_weight, token), update)
            added += count
            token = [*token, update]
        if step + 1 < slabs:
            near = after(coming_near, token)
            token = [*token, near]
            if step > 0:
                near_pair = [near, to_core(near)]
            if step + 2 < slabs and step != 1:
                coming_near = along(near, 1)
        if step == 1 and step + 1 < slabs:
            far = after(coming_far, [*token[:-1], near_pair[1]])
        else:
            far = after(coming_far, token[:-1] if 0 < step < slabs - 1 else token)
        if step + 2 < slabs and step == 1:
            coming_near = along(after(near, [far]), 1)
        if step + 1 < slabs:
            if step + 2 == slabs:
                coming_far = along(far, 1)
            elif step > 0:
                coming_far = to_side(near)
        if step == 1:
            update = add_update([halves[added]], after(row_weight, [*token, far]), update)
            added += 1
            token = [*token, update]
        if step + 1 == slabs and slabs > 2:
            code = encode(nears[1] + decode(after(from_sides[1], token)))
            arriving = [along(code, 1)]
            token = [*token, code]
        far_pair = [far, to_core(far)]
        if step == 0 and slabs > 2:
            coming_far = to_side(after(near, [far]))
        if step == 0 and slabs > 1:
            near_pair = [near, to_core(after(near, far_pair[1:]))]
        token = far_half(step, far_pair, token)
        if step + 1 < slabs:
            token = near_half(step + 1, near_pair, token)
        else:
            count = 2 if 2 < step else 1
            update = add_update(halves[added : added + count], after(row_weight, token), update)
            added += count
            token = [update]
        token = collect(step, token)
        if step > 0:
            from_sides[step] = to_side(codes[step])
        if step > 2:
            if step == slabs - 1:
                update = add_update([halves[added]], after(row_weight, token), update)
                added += 1
                token = [update]
            sums = [pass_on(step - 1, part, arriving, token) for part in (0, 1)]
            arriving = [along(code, 1) for code in sums]
            token = [*token, *sums]

    if slabs > 1:
        sums = [pass_on(slabs - 1, 0, arriving, token)]
        last_weight = after(row_weight, sums)
    else:
        last_weight = row_weight
    grad_out = add_update(halves[added:], last_weight, update, 1.0 / math.sqrt(total_in))
    own = [nears[0][part] for part in parts]
    if slabs > 1:
        from_sides[0] = to_side(after(codes[0], sums))
        sums.append(pass_on(slabs - 1, 1, arriving, [grad_out]))
        arriving = [along(code, 1) for code in sums]
        from_side = decode(after(from_sides[0], sums[1:]))
        own = [mine + from_side[part] for mine, part in zip(own, parts)]
        own[0] = own[0] + decode(after(arriving[0], sums[1:]))
    else:
        from_sides[0] = to_side(codes[0])
    last = arriving[1] if slabs > 1 else from_sides[0]
    grad_in_t = finish(own, last, 1.0 / math.sqrt(total_out))
    return (grad_out, grad_in_t)


def solution(mesh):
    in_specs = (
        P("groups", None, "port", None),
        P("port", "groups"),
        P("groups", "port"),
        P("groups"),
        P("groups"),
        P("groups"),
    )
    out_specs = (P("port", "groups"), P("port", "groups"))
    return jax.shard_map(
        on_device, mesh=mesh, in_specs=in_specs, out_specs=out_specs, check_vma=False
    )
```

```python
import functools
import math

import jax
import jax.numpy as jnp
from jax import lax
from jax.experimental import pallas as pl
from jax.experimental.pallas import tpu as pltpu
from jax.sharding import PartitionSpec as P

GRID = 1024


low_freq = 0.1
log_span = math.log(100.0)
least_code = 1e-36


def pole_terms(freq_index, pole_rates):
    omega = low_freq * jnp.exp(log_span * freq_index.astype(jnp.float32) / (GRID - 1))
    denominator = pole_rates[None, :] * pole_rates[None, :] + omega[:, None] * omega[:, None]
    real_side = pole_rates[None, :] / denominator
    imag_side = -omega[:, None] / denominator
    return jnp.stack([real_side, imag_side], axis=1)


def encode(value):
    return ((value * jnp.abs(value)) * (value * value)).astype(jnp.bfloat16)


def decode(code):
    code = code.astype(jnp.float32)
    inverse_root = lax.rsqrt(jnp.maximum(jnp.abs(code), least_code))
    return (code * inverse_root) * (inverse_root * lax.rsqrt(inverse_root))


def ring_order(slabs):
    return [0, *range(1, slabs, 2), *reversed(range(2, slabs, 2))]


def block_at(rank, step, slabs, flip):
    slab = lax.div(rank, 4)
    place = jnp.where(lax.rem(slab, 2) == 1, lax.div(slab + 1, 2), slabs - lax.div(slab, 2))
    place = lax.rem(place + (slabs - step), slabs)
    slab = jnp.where(place <= slabs // 2, 2 * place - 1, 2 * (slabs - place))
    slab = jnp.where(place == 0, 0, slab)
    return 4 * slab + (lax.rem(rank, 4) ^ flip)


def start_copies(rank_ref, measured_ref, first_half, slabs, halves, arrived):
    width = halves[0].shape[-1]
    copies = []
    for at, half in enumerate(halves):
        for core in range(2):
            place = 2 * (first_half + at) + core
            block = block_at(rank_ref[0], place // 4, slabs, place % 4)
            columns = pl.ds(pl.multiple_of(block * width, width), width)
            copy = pltpu.make_async_copy(
                measured_ref.at[:, :, :, columns], half.at[core], arrived.at[2 * at + core]
            )
            copy.start()
            copies.append(copy)
    return copies


def prepare_kernel(
    slabs,
    rank_ref,
    freq_hbm,
    quad_hbm,
    rates_hbm,
    factor_hbm,
    measured_ref,
    scaled_ref,
    turned_ref,
    pole_weight_ref,
    row_weight_ref,
    *refs,
):
    freq_ref, quad_ref, rates_ref, factor_ref, came, arrived = refs[-6:]
    pairs = ((freq_hbm, freq_ref), (quad_hbm, quad_ref), (rates_hbm, rates_ref), (factor_hbm, factor_ref))
    small = [pltpu.make_async_copy(*pair, came.at[at]) for at, pair in enumerate(pairs)]
    for copy in small:
        copy.start()
    copies = start_copies(rank_ref, measured_ref, 0, slabs, refs[:-6], arrived)
    for copy in small:
        copy.wait()
    rates = rates_ref[...]
    factor = factor_ref[...].astype(jnp.float32)
    turned_ref[...] = factor.T.astype(jnp.bfloat16)
    rows = factor.shape[0]
    lanes = pole_weight_ref.shape[2]
    for freq_slot in range(freq_ref.shape[0]):
        index = jnp.full(rates.shape, freq_ref[freq_slot], jnp.int32).astype(jnp.float32)
        weight = jnp.full(rates.shape, quad_ref[freq_slot], jnp.int32).astype(jnp.float32) * 0.25
        omega = low_freq * jnp.exp(log_span * index / (GRID - 1))
        denominator = rates * rates + omega * omega
        for comp_slot, coefficient in enumerate((rates / denominator, -omega / denominator)):
            term = 2 * freq_slot + comp_slot
            scaled_ref[pl.ds(term * rows, rows), :] = (factor * coefficient).astype(jnp.bfloat16)
            weighted = weight * coefficient
            row_weight_ref[term] = weighted
            pole_weight_ref[term] = jnp.broadcast_to(weighted, (lanes, weighted.shape[1])).T
    for copy in copies:
        copy.wait()


def prepare_by_kernel(
    rank, slabs, freq_index, quad_codes, pole_rates, out_factor, measured, width, lanes, halves
):
    rows, poles = out_factor.shape
    terms = 2 * freq_index.shape[0]
    vmem = pl.BlockSpec(memory_space=pltpu.VMEM)
    smem = pl.BlockSpec(memory_space=pltpu.SMEM)
    anywhere = pl.BlockSpec(memory_space=pl.ANY)
    operands = (freq_index, quad_codes, pole_rates[None, :], out_factor, measured)
    made = pl.pallas_call(
        functools.partial(prepare_kernel, slabs),
        in_specs=[smem] + [anywhere] * 5,
        out_specs=[vmem] * (4 + halves),
        out_shape=[
            jax.ShapeDtypeStruct((terms * rows, poles), jnp.bfloat16),
            jax.ShapeDtypeStruct((poles, rows), jnp.bfloat16),
            jax.ShapeDtypeStruct((terms, poles, lanes), jnp.float32),
            jax.ShapeDtypeStruct((terms, 1, poles), jnp.float32),
        ]
        + [jax.ShapeDtypeStruct((2, *measured.shape[:3], width), jnp.bfloat16)] * halves,
        scratch_shapes=[
            pltpu.SMEM(freq_index.shape, jnp.int32),
            pltpu.SMEM(quad_codes.shape, jnp.int32),
            pltpu.VMEM((1, poles), jnp.float32),
            pltpu.VMEM((rows, poles), jnp.bfloat16),
            pltpu.SemaphoreType.DMA((4,)),
            pltpu.SemaphoreType.DMA((2 * halves,)),
        ],
        compiler_params=pltpu.CompilerParams(vmem_limit_bytes=16 * 1024 * 1024),
        cost_estimate=pl.CostEstimate(
            flops=0, bytes_accessed=halves * measured.size // slabs, transcendentals=0
        ),
        name="prepare",
    )(rank, *[pltpu.with_memory_space_constraint(array, pltpu.HBM) for array in operands])
    return made[:4], list(made[4:])


def half_kernel(
    factor_0, factor_1, scaled_ref, turned_ref, pole_weight_ref, seen_ref, *refs
):
    keep_ref, send_ref, residual_ref, held_ref = refs[-4:]
    width = factor_0.shape[1]
    rows = turned_ref.shape[1]
    terms = pole_weight_ref.shape[0]
    models = []
    for core, factor_ref in enumerate((factor_0, factor_1)):
        factor = factor_ref[...]
        held_ref[core] = factor
        models.append(jnp.dot(scaled_ref[...], factor, preferred_element_type=jnp.float32))
    residuals = []
    for core, model in enumerate(models):
        seen = seen_ref[core].reshape(terms * rows, width).astype(jnp.float32)
        residual = (model - seen).astype(jnp.bfloat16)
        residual_ref[core] = residual.reshape(residual_ref.shape[1:])
        residuals.append(residual)
    partials = [None, None]
    for term in range(terms):
        weight = pole_weight_ref[term]
        weight = jnp.concatenate([weight] * (width // weight.shape[1]), axis=1)
        for core, residual in enumerate(residuals):
            part = weight * jnp.dot(
                turned_ref[...],
                residual[term * rows : (term + 1) * rows],
                preferred_element_type=jnp.float32,
            )
            partials[core] = part if term == 0 else partials[core] + part
    keep_ref[...] = partials[0]
    if len(refs) > 4:
        send_ref[0] = refs[0][...]
        send_ref[1] = encode(partials[1])
    else:
        send_ref[...] = encode(partials[1])


def half_by_kernel(factors, constants, seen, near_send):
    scaled, turned, pole_weight, _ = constants
    poles, width = factors[0].shape
    rows = turned.shape[1]
    terms = pole_weight.shape[0]
    half = len(factors) * width
    flops = 2 * 2 * terms * rows * poles * half
    vmem = pl.BlockSpec(memory_space=pltpu.VMEM)
    beside = [] if near_send is None else [near_send]
    return pl.pallas_call(
        half_kernel,
        in_specs=[vmem] * (6 + len(beside)),
        out_specs=[vmem] * 4,
        out_shape=[
            jax.ShapeDtypeStruct((poles, width), jnp.float32),
            jax.ShapeDtypeStruct((2, poles, width) if beside else (poles, width), jnp.bfloat16),
            jax.ShapeDtypeStruct(seen.shape, seen.dtype),
            jax.ShapeDtypeStruct((2, poles, width), jnp.bfloat16),
        ],
        input_output_aliases={5: 2},
        compiler_params=pltpu.CompilerParams(vmem_limit_bytes=16 * 1024 * 1024),
        cost_estimate=pl.CostEstimate(
            flops=10 * flops, bytes_accessed=2 * terms * rows * half, transcendentals=0
        ),
        name="far" if beside else "near",
    )(*factors, scaled, turned, pole_weight, seen, *beside)


def update_kernel(halves, scale, *refs):
    row_weight_ref, *refs, total_ref = refs
    terms = row_weight_ref.shape[0]
    rows, width = refs[0].shape[-2:]
    total = None
    for at in range(halves):
        residual_ref, held_ref = refs[2 * at : 2 * at + 2]
        for core in range(2):
            part = lax.dot_general(
                residual_ref[core].reshape(terms * rows, width),
                held_ref[core],
                (((1,), (1,)), ((), ())),
                preferred_element_type=jnp.float32,
            )
            total = part if total is None else total + part
    update = refs[2 * halves][...] if len(refs) > 2 * halves else 0.0
    for term in range(terms):
        update = update + row_weight_ref[term] * total[term * rows : (term + 1) * rows]
    total_ref[...] = update if scale is None else update * scale


def update_by_kernel(halves, row_weight, update, scale=None):
    poles, width = halves[0][1].shape[1:]
    rows = halves[0][0].shape[-2]
    terms = row_weight.shape[0]
    flops = 4 * len(halves) * terms * rows * poles * width
    vmem = pl.BlockSpec(memory_space=pltpu.VMEM)
    operands = [row_weight, *[array for half in halves for array in half]]
    operands += [] if update is None else [update]
    return pl.pallas_call(
        functools.partial(update_kernel, len(halves), scale),
        in_specs=[vmem] * len(operands),
        out_specs=vmem,
        out_shape=jax.ShapeDtypeStruct((rows, poles), jnp.float32),
        compiler_params=pltpu.CompilerParams(vmem_limit_bytes=16 * 1024 * 1024),
        cost_estimate=pl.CostEstimate(
            flops=20 * flops, bytes_accessed=2 * terms * rows * width, transcendentals=0
        ),
        name="update",
    )(*operands)


def slice_by_ops(rank, slabs, measured, width, first_half, last_half):
    blocks = [
        lax.dynamic_slice_in_dim(
            measured, block_at(rank[0], at // 4, slabs, at % 4) * width, width, 3
        )
        for at in range(2 * first_half, 2 * last_half)
    ]
    return [jnp.stack(blocks[at : at + 2]) for at in range(0, len(blocks), 2)]


def finish_kernel(scale, near_ref, *refs):
    total = near_ref[...]
    for code_ref in refs[:-1]:
        total = total + decode(code_ref[...])
    refs[-1][...] = (total * scale).T


def finish_by_kernel(near, codes, scale):
    poles, width = near.shape
    vmem = pl.BlockSpec(memory_space=pltpu.VMEM)
    return pl.pallas_call(
        functools.partial(finish_kernel, scale),
        in_specs=[vmem] * (1 + len(codes)),
        out_specs=vmem,
        out_shape=jax.ShapeDtypeStruct((width, poles), jnp.float32),
        compiler_params=pltpu.CompilerParams(vmem_limit_bytes=16 * 1024 * 1024),
        cost_estimate=pl.CostEstimate(
            flops=0, bytes_accessed=8 * poles * width, transcendentals=0
        ),
        name="finish",
    )(near, *codes)


def finish_by_ops(near, codes, scale):
    return (sum((decode(code) for code in codes), near) * scale).T


def prepare_by_ops(
    rank, slabs, freq_index, quad_codes, pole_rates, out_factor, measured, width, lanes, halves
):
    rows, poles = out_factor.shape
    coefficients = pole_terms(freq_index, pole_rates)
    weights = quad_codes.astype(jnp.float32) * 0.25
    weighted = (weights[:, None, None] * coefficients).reshape(-1, poles)
    scaled = (
        out_factor.astype(jnp.float32)[None, None, :, :] * coefficients[:, :, None, :]
    ).astype(jnp.bfloat16)
    pole_weight = jnp.broadcast_to(weighted[:, :, None], (weighted.shape[0], poles, lanes))
    seen = slice_by_ops(rank, slabs, measured, width, 0, halves)
    constants = [scaled.reshape(-1, poles), out_factor.T, pole_weight, weighted[:, None, :]]
    return constants, seen


def half_by_ops(factors, constants, seen, near_send):
    scaled, turned, pole_weight, _ = constants
    width = factors[0].shape[1]
    rows = turned.shape[1]
    terms = pole_weight.shape[0]
    partials, residuals = [], []
    for core, factor in enumerate(factors):
        model = jnp.dot(scaled, factor, preferred_element_type=jnp.float32)
        residual = model - seen[core].reshape(terms * rows, width).astype(jnp.float32)
        residual = residual.astype(jnp.bfloat16)
        residuals.append(residual.reshape(seen.shape[1:]))
        partial = jnp.einsum(
            "ki,tij->tkj",
            turned,
            residual.reshape(terms, rows, width),
            preferred_element_type=jnp.float32,
        )
        partials.append(jnp.sum(pole_weight[:, :, :1] * partial, axis=0))
    send = encode(partials[1])
    if near_send is not None:
        send = jnp.stack([near_send, send])
    return partials[0], send, jnp.stack(residuals), jnp.stack(factors)


def update_by_ops(halves, row_weight, update, scale=None):
    rows, width = halves[0][0].shape[-2:]
    terms = row_weight.shape[0]
    total = sum(
        jnp.einsum(
            "tij,kj->tik",
            residual[core].reshape(terms, rows, width),
            held[core],
            preferred_element_type=jnp.float32,
        )
        for residual, held in halves
        for core in range(2)
    )
    part = jnp.sum(row_weight * total, axis=0)
    total = part if update is None else update + part
    return total if scale is None else total * scale


def after(value, earlier):
    return lax.optimization_barrier((value, *earlier))[0]


def on_device(measured, out_factor, in_factor, pole_rates, freq_index, quad_codes):
    rows, total_in = measured.shape[2:]
    poles, width = in_factor.shape
    ranks = lax.axis_size("port")
    rank = lax.axis_index("port").astype(jnp.int32).reshape(1)
    slabs = ranks // 4
    total_out = rows * ranks
    tiled = width % 128 == 0 and rows % 128 == 0
    prepare = prepare_by_kernel if tiled else prepare_by_ops
    one_half = half_by_kernel if tiled else half_by_ops
    add_update = update_by_kernel if tiled else update_by_ops
    finish = finish_by_kernel if tiled else finish_by_ops

    def to_core(block):
        return lax.ppermute(block, "port", [(i, i ^ 1) for i in range(ranks)])

    def to_side(block):
        return lax.ppermute(block, "port", [(i, i ^ 2) for i in range(ranks)])

    ring = ring_order(slabs)
    place = {slab: at for at, slab in enumerate(ring)}

    def along(block, hops):
        pairs = [
            (i, 4 * ring[(place[i // 4] + hops) % slabs] + i % 4) for i in range(ranks)
        ]
        return lax.ppermute(block, "port", pairs)

    near = in_factor
    coming_near = along(near, 1)
    coming_far = to_side(near)
    near_pair = [near, to_core(near)]
    constants, seen = prepare(
        rank,
        slabs,
        freq_index,
        quad_codes,
        pole_rates,
        out_factor,
        measured,
        width,
        min(width, 128),
        2 * slabs,
    )
    nears = [None] * slabs
    keeps = [None] * slabs
    sends = [None] * slabs
    codes = [None] * slabs
    from_sides = [None] * slabs
    halves = []

    def near_half(step, pair, token):
        keep, sends[step], *parts = one_half(pair, constants, after(seen[2 * step], token), None)
        halves.append(parts)
        keeps[step] = [keep]
        return [parts[0]]

    def far_half(step, pair, token):
        keep, sends[step], *parts = one_half(
            pair, constants, after(seen[2 * step + 1], token), sends[step]
        )
        halves.append(parts)
        keeps[step].append(keep)
        return [parts[0]]

    def collect(step, token):
        received = decode(after(to_core(sends[step]), token))
        nears[step] = keeps[step][0] + received[0]
        codes[step] = encode(keeps[step][1] + received[1])
        return [*token, codes[step]]

    def pass_on(step, arriving, token):
        total = nears[step] + decode(after(from_sides[step], token))
        if arriving is not None:
            total = total + decode(after(arriving, token))
        return encode(total)

    arriving = None
    from_next = None
    update = None
    added = 0
    row_weight = constants[3]
    token = near_half(0, near_pair, [row_weight])
    for step in range(slabs):
        if step + 1 < slabs:
            near = after(coming_near, token)
            token = [*token, near]
            near_pair = [near, to_core(near)]
            if step + 2 < slabs and step != 1:
                coming_near = along(near, 1)
        if step == 1 and step + 1 < slabs:
            far = after(coming_far, [*token[:-1], near_pair[1]])
        else:
            far = after(coming_far, token[:-1] if 0 < step < slabs - 1 else token)
        if step + 2 < slabs and step == 1:
            coming_near = along(after(near, [far]), 1)
        if step + 1 < slabs:
            if step + 2 == slabs:
                coming_far = along(far, 1)
            elif step > 0:
                coming_far = to_side(near)
        if step == 1:
            update = add_update([halves[added]], after(row_weight, [*token, far]), update)
            added += 1
            token = [*token, update]
        if step + 1 == slabs and slabs > 2:
            code = pass_on(1, None, token)
            from_next = along(code, -1)
            token = [*token, code]
        far_pair = [far, to_core(far)]
        if step == 0 and slabs > 2:
            coming_far = to_side(after(near, [far]))
        token = far_half(step, far_pair, token)
        if step == 2:
            from_sides[1] = to_side(after(codes[1], token))
        if step < min(2, slabs - 1):
            token = near_half(step + 1, near_pair, token)
        elif step > 1:
            update = add_update([halves[added]], after(row_weight, token), update)
            added += 1
            token = [update]
        token = collect(step, token)
        if step > 1 and step < slabs - 1 or 0 < step == slabs - 1 < 3:
            from_sides[step] = to_side(codes[step])
        if 1 < step < slabs - 1:
            token = near_half(step + 1, near_pair, token)
        if step > 2:
            code = pass_on(step - 1, arriving, token)
            arriving = along(code, 1)
            token = [*token, code]
            if step == slabs - 1:
                from_sides[step] = to_side(after(codes[step], [code]))

    if slabs > 1:
        middle = (added + 2 * slabs + 1) // 2
        update = add_update(halves[added:middle], after(row_weight, token), update)
        code = pass_on(slabs - 1, arriving, [update])
        arriving = along(code, 1)
        token = [update, code]
    from_sides[0] = to_side(after(codes[0], token))
    if slabs > 1:
        grad_out = add_update(
            halves[middle:], after(row_weight, token), update, 1.0 / math.sqrt(total_in)
        )
    else:
        grad_out = add_update(halves[added:], row_weight, update, 1.0 / math.sqrt(total_in))
    last = [sums for sums in (from_sides[0], from_next, arriving) if sums is not None]
    last = [after(sums, [grad_out]) for sums in last]
    grad_in_t = finish(nears[0], last, 1.0 / math.sqrt(total_out))
    return (grad_out, grad_in_t)


def solution(mesh):
    in_specs = (
        P("groups", None, "port", None),
        P("port", "groups"),
        P("groups", "port"),
        P("groups"),
        P("groups"),
        P("groups"),
    )
    out_specs = (P("port", "groups"), P("port", "groups"))
    return jax.shard_map(
        on_device, mesh=mesh, in_specs=in_specs, out_specs=out_specs, check_vma=False
    )
```
